32 devices in a mesh: rows: 16 (over z, y, x), ch: 2 (over core).
Axes of the slice: x: 2, y: 2, z: 4, core: 2. Of those that a mesh axis runs over, the one named last changes fastest.
Arguments:
- inputs: bfloat16 [65536, 800], P(('rows', 'ch')), may hold values from -9 to 9
- cotangent: bfloat16 [65536, 800], P(('rows', 'ch')), may hold values from -9 to 9
- doc_lengths: int32 [16, 4], P('rows'), may hold values from 1 to 3072, 4096 in all within a row
- trailing_pad_tokens: int32 [16], P('rows'), may hold values from 1 to 512
- first_norm_gain: bfloat16 [800], replicated, may hold values from 0.25 to 1.75
- first_norm_bias: bfloat16 [800], replicated, may hold values from -1.796875 to 1.796875
- first_down: bfloat16 [800, 400], P(None, 'ch'), may hold values from -0.21875 to 0.21875
- first_inner_gain: bfloat16 [2, 400], P(None, 'ch'), may hold values from 0.25 to 1.75
- first_inner_bias: bfloat16 [2, 400], P(None, 'ch'), may hold values from -1.796875 to 1.796875
- first_conv: bfloat16 [5, 400, 400], P(None, None, 'ch'), may hold values from -0.125 to 0.125
- first_up: bfloat16 [400, 800], P('ch'), may hold values from -0.3125 to 0.3125
- second_norm_gain: bfloat16 [800], replicated, may hold values from 0.25 to 1.75
- second_norm_bias: bfloat16 [800], replicated, may hold values from -1.796875 to 1.796875
- second_down: bfloat16 [800, 400], P(None, 'ch'), may hold values from -0.21875 to 0.21875
- second_inner_gain: bfloat16 [2, 400], P(None, 'ch'), may hold values from 0.25 to 1.75
- second_inner_bias: bfloat16 [2, 400], P(None, 'ch'), may hold values from -1.796875 to 1.796875
- second_conv: bfloat16 [3, 400, 400], P(None, None, 'ch'), may hold values from -0.1875 to 0.1875
- second_up: bfloat16 [400, 800], P('ch'), may hold values from -0.3125 to 0.3125
Outputs:
- first_output: bfloat16 [65536, 800], P(('rows', 'ch'))
- second_output: bfloat16 [65536, 800], P(('rows', 'ch'))
- input_grad: float32 [65536, 800], P(('rows', 'ch'))
- first_norm_gain_grad: float32 [800], replicated
- first_norm_bias_grad: float32 [800], replicated
- first_down_grad: float32 [800, 400], P(None, 'ch')
- first_inner_gain_grad: float32 [2, 400], P(None, 'ch')
- first_inner_bias_grad: float32 [2, 400], P(None, 'ch')
- first_conv_grad: float32 [5, 400, 400], P(None, None, 'ch')
- first_up_grad: float32 [400, 800], P('ch')
- second_norm_gain_grad: float32 [800], replicated
- second_norm_bias_grad: float32 [800], replicated
- second_down_grad: float32 [800, 400], P(None, 'ch')
- second_inner_gain_grad: float32 [2, 400], P(None, 'ch')
- second_inner_bias_grad: float32 [2, 400], P(None, 'ch')
- second_conv_grad: float32 [3, 400, 400], P(None, None, 'ch')
- second_up_grad: float32 [400, 800], P('ch')
- stream_rms: float32 [5], replicated
The draws below stay inside these ranges and needn't reach their ends.
Inputs may be any that keep to these rules, and one draw needn't show every extreme that they name: `doc_lengths`: each row holds 4 lengths that sum to 4096; the largest of each row is exactly 3072.
All inputs are finite; a program needn't handle non-finite values.
Results may differ from the reference program's by a relative error of at most 0.012.
Values may be sent and summed in bfloat16 or wider, within the bound.
No kernel may reach another device: no remote copies, remote signals or barrier semaphores. Data moves between devices by JAX's collectives and lax.ppermute only.
A program may use at most 256 MiB of HBM per device.

```python
import math
import jax
import jax.numpy as jnp
import numpy as np
from jax import lax

D = 800
INNER = 400
ENCODER_TAPS = 5
DECODER_TAPS = 3
DILATION_RATE = 8
DOCS = 4
TOK_DEV = 2048
GROUP = 4096
LONGEST = 3072
TOKENS = 65536
N_ROWS = 16


def scaled_rows(key, base_scale):
    places = jnp.arange(TOKENS, dtype=jnp.float32)[:, None] / TOKENS
    scaling = base_scale * jnp.exp(jnp.log(3.0) * places)
    values = jnp.clip(jax.random.normal(key, (TOKENS, D), jnp.float32), -5.0, 5.0)
    return (values * scaling).astype(jnp.bfloat16)


def draw_inputs(key, part):
    key = jax.random.fold_in(key, 11)
    return scaled_rows(key, 0.6)


def draw_cotangent(key, part):
    key = jax.random.fold_in(key, 12)
    return scaled_rows(key, 0.5)


def place_ends(values, rng, smallest, largest):
    spot = [jax.random.randint(jax.random.fold_in(rng, axis), (), 0, length) for axis, length in enumerate(values.shape)]
    main_axis = values.shape.index(max(values.shape))
    beside = spot[:main_axis] + [(spot[main_axis] + 1) % values.shape[main_axis]] + spot[main_axis + 1:]
    return values.at[tuple(spot)].set(smallest).at[tuple(beside)].set(largest)


def block_levels(rng, shape, shards, least, top_value):
    factor_of, own = 1.0, jax.random.fold_in(rng, 6)
    for dim, shards_of in shards:
        draws = jnp.exp(jax.random.uniform(jax.random.fold_in(own, dim), (shards_of,), jnp.float32, least / len(shards), top_value / len(shards)))
        factor_of = factor_of * jnp.repeat(draws, shape[dim] // shards_of).reshape([-1 if axis == dim else 1 for axis in range(len(shape))])
    return factor_of


def length_profile(count, total, reach, lean):
    weights = [(1 << 20) // math.isqrt(grade ** lean) + 1 for grade in range(2, count + 1)]
    spare, counts = total - reach - (count - 1), [1] * (count - 1)
    while spare > 0:
        candidates = [i for i in range(count - 1) if counts[i] < reach]
        mass, left = sum([weights[i] for i in candidates]), spare
        for i in candidates:
            addition = min(reach - counts[i], max(1, left * weights[i] // mass), spare)
            counts[i] = counts[i] + addition
            spare = spare - addition
    return np.array([reach] + counts)


def uneven(own_key, number_of, total, bound, lean):
    if number_of == 2:
        one = jax.random.randint(own_key, (), max(1, total - bound), min(bound, total - 1) + 1)
        return jnp.stack([one, total - one])
    tallies = jnp.asarray(length_profile(number_of, total, bound, lean), jnp.int32)
    twos = (number_of - 1) // 2
    giver, taker = tallies[1:1 + 2 * twos:2], tallies[2:2 + 2 * twos:2]
    slack = jnp.minimum(giver - 1, bound - taker)
    moved = jax.random.randint(jax.random.fold_in(own_key, 1), (twos,), 0, 1 << 20) % (slack + 1)
    tallies = tallies.at[1:1 + 2 * twos:2].set(giver - moved).at[2:2 + 2 * twos:2].set(taker + moved)
    return tallies[jax.random.permutation(jax.random.fold_in(own_key, 2), number_of)]


def bell_draw(rng, extent, deviation, limit, cuts=(), kind=jnp.bfloat16):
    entries = deviation * jax.random.normal(rng, extent, jnp.float32)
    if cuts:
        entries = entries * block_levels(rng, extent, cuts, -0.22, 0.18)
    return jnp.clip(entries, -limit, limit).astype(kind)


def setup_inputs(seed: int = 0) -> dict:
    seeds = jax.random.split(jax.random.key(seed), 19)
    return {
        "inputs": draw_inputs(jax.random.fold_in(seeds[18], 71), 0),
        "cotangent": draw_cotangent(jax.random.fold_in(seeds[18], 71), 0),
        "doc_lengths": jax.vmap(lambda own: uneven(own, DOCS, GROUP, LONGEST, 2))(jax.random.split(seeds[2], N_ROWS)).reshape((N_ROWS, DOCS)).astype(jnp.int32),
        "trailing_pad_tokens": place_ends(jax.random.randint(seeds[3], (N_ROWS,), 1, TOK_DEV // 4 + 1), jax.random.fold_in(seeds[3], 1), 1, (TOK_DEV // 4 + 1) - 1).astype(jnp.int32),
        "first_norm_gain": jnp.clip(1.0 + 0.15 * jax.random.normal(seeds[4], (D,), jnp.float32), 0.25, 1.75).astype(jnp.bfloat16),
        "first_norm_bias": bell_draw(seeds[5], (D,), 0.3, 1.796875),
        "first_down": bell_draw(seeds[6], (D, INNER), D ** -0.5, 0.21875, ((1, 2),)),
        "first_inner_gain": jnp.clip(1.0 + 0.15 * jax.random.normal(seeds[7], (2, INNER), jnp.float32), 0.25, 1.75).astype(jnp.bfloat16),
        "first_inner_bias": bell_draw(seeds[8], (2, INNER), 0.3, 1.796875, ((1, 2),)),
        "first_conv": bell_draw(seeds[9], (ENCODER_TAPS, INNER, INNER), (ENCODER_TAPS * INNER) ** -0.5, 0.125, ((2, 2),)),
        "first_up": bell_draw(seeds[10], (INNER, D), INNER ** -0.5, 0.3125, ((0, 2),)),
        "second_norm_gain": jnp.clip(1.0 + 0.15 * jax.random.normal(seeds[11], (D,), jnp.float32), 0.25, 1.75).astype(jnp.bfloat16),
        "second_norm_bias": bell_draw(seeds[12], (D,), 0.3, 1.796875),
        "second_down": bell_draw(seeds[13], (D, INNER), D ** -0.5, 0.21875, ((1, 2),)),
        "second_inner_gain": jnp.clip(1.0 + 0.15 * jax.random.normal(seeds[14], (2, INNER), jnp.float32), 0.25, 1.75).astype(jnp.bfloat16),
        "second_inner_bias": bell_draw(seeds[15], (2, INNER), 0.3, 1.796875, ((1, 2),)),
        "second_conv": bell_draw(seeds[16], (DECODER_TAPS, INNER, INNER), (DECODER_TAPS * INNER) ** -0.5, 0.1875, ((2, 2),)),
        "second_up": bell_draw(seeds[17], (INNER, D), INNER ** -0.5, 0.3125, ((0, 2),)),
    }


EPS = 1e-05

@jax.custom_vjp
def low(v):
    return lax.optimization_barrier(v.astype(jnp.bfloat16)).astype(jnp.float32)

@jax.custom_vjp
def low_back(v):
    return v

def low_keep(v):
    return (low(v), None)

def low_pass(kept, grad):
    return (grad,)

def back_keep(v):
    return (v, None)

def back_low(kept, grad):
    return (low(grad),)
low.defvjp(low_keep, low_pass)
low_back.defvjp(back_keep, back_low)

def matmul(left_side, right_side):
    return jnp.dot(left_side, right_side, precision=lax.Precision.HIGHEST, preferred_element_type=jnp.float32)

def layer_norm(values, gain_row, bias_row):
    centre = lax.optimization_barrier(jnp.mean(values, axis=-1, keepdims=True))
    shifted = values - centre
    spread = lax.optimization_barrier(jnp.mean(shifted * shifted, axis=-1, keepdims=True))
    return shifted * lax.rsqrt(spread + EPS) * gain_row + bias_row

def tap_offsets(filter_weight, causal):
    if causal:
        return [(tap_number - filter_weight + 1) * DILATION_RATE for tap_number in range(filter_weight)]
    return [(tap_number - (filter_weight - 1) // 2) * DILATION_RATE for tap_number in range(filter_weight)]

def segment_ids(lengths_row, pad_count):
    places = jnp.arange(GROUP, dtype=jnp.int32)
    doc_ends = jnp.cumsum(lengths_row).astype(jnp.int32)
    counted = lax.optimization_barrier(jnp.sum((places[:, None] >= doc_ends[None, :]).astype(jnp.int32), axis=1))
    return jnp.where(places >= GROUP - pad_count, DOCS, counted).astype(jnp.int32)

def tap_masks(segment, offsets):
    places = jnp.arange(GROUP, dtype=jnp.int32)
    result = []
    for offset in offsets:
        source = places + offset
        inside = (source >= 0) & (source < GROUP)
        source_seg = jnp.take(segment, jnp.clip(source, 0, GROUP - 1).astype(jnp.int32))
        result.append((inside & (source_seg == segment) & (source_seg < DOCS)).astype(jnp.float32))
    return result

def residual_block(stream, valid_rows, masks, offsets, params):
    norm_gain, norm_bias, down_proj, inner_gain, inner_bias, conv_taps, up_proj = params
    receptive_span = max((abs(offset) for offset in offsets))
    normed = low(jax.nn.gelu(layer_norm(stream, norm_gain, norm_bias)))
    hidden = low_back(matmul(normed, down_proj))
    inner_act = low(jax.nn.gelu(layer_norm(hidden, inner_gain[0], inner_bias[0])))
    padded = jnp.pad(inner_act, ((receptive_span, receptive_span), (0, 0)))
    stacked = jnp.concatenate([masks[tap_number][:, None] * padded[receptive_span + offsets[tap_number]:receptive_span + offsets[tap_number] + GROUP] for tap_number in range(len(offsets))], axis=1)
    mixed = low_back(matmul(stacked, conv_taps.reshape(len(offsets) * INNER, INNER)))
    outer_act = low(jax.nn.gelu(layer_norm(mixed, inner_gain[1], inner_bias[1])))
    branch = valid_rows[:, None] * low_back(matmul(outer_act, up_proj))
    return (stream + branch, branch)

def forward_pass(stream_all, lengths_all, pads_all, first_params, second_params):
    offsets_enc = tap_offsets(ENCODER_TAPS, False)
    offsets_dec = tap_offsets(DECODER_TAPS, True)

    def one_group(totals, group_item):
        stream, lengths_row, pad_count = group_item
        segment = segment_ids(lengths_row, pad_count)
        valid_rows = (segment < DOCS).astype(jnp.float32)
        middle, branch_one = residual_block(stream, valid_rows, tap_masks(segment, offsets_enc), offsets_enc, first_params)
        final_rows, branch_two = residual_block(middle, valid_rows, tap_masks(segment, offsets_dec), offsets_dec, second_params)
        weights_rows = valid_rows[:, None]
        group_sums = jnp.stack([jnp.sum(weights_rows * stream * stream), jnp.sum(branch_one * branch_one), jnp.sum(weights_rows * middle * middle), jnp.sum(branch_two * branch_two), jnp.sum(weights_rows * final_rows * final_rows), jnp.sum(valid_rows)])
        return (totals + group_sums, (middle, final_rows))
    totals, outputs = lax.scan(jax.checkpoint(one_group), jnp.zeros((6,), jnp.float32), (stream_all, lengths_all, pads_all))
    return (outputs[1], (outputs[0], totals))

def reference(inputs, cotangent, doc_lengths, trailing_pad_tokens, first_norm_gain, first_norm_bias, first_down, first_inner_gain, first_inner_bias, first_conv, first_up, second_norm_gain, second_norm_bias, second_down, second_inner_gain, second_inner_bias, second_conv, second_up):
    first_params = tuple((weight.astype(jnp.float32) for weight in (first_norm_gain, first_norm_bias, first_down, first_inner_gain, first_inner_bias, first_conv, first_up)))
    second_params = tuple((weight.astype(jnp.float32) for weight in (second_norm_gain, second_norm_bias, second_down, second_inner_gain, second_inner_bias, second_conv, second_up)))
    stream_all = inputs.astype(jnp.float32).reshape(N_ROWS, GROUP, D)

    def wrapped(stream_in, params_one, params_two):
        return forward_pass(stream_in, doc_lengths, trailing_pad_tokens, params_one, params_two)
    final_rows, pullback, aux_values = jax.vjp(wrapped, stream_all, first_params, second_params, has_aux=True)
    middle, totals = aux_values
    grad_stream, grads_one, grads_two = pullback(cotangent.astype(jnp.float32).reshape(N_ROWS, GROUP, D))
    stream_rms = jnp.sqrt(totals[:5] / (totals[5] * D))
    return (middle.reshape(TOKENS, D).astype(jnp.bfloat16), final_rows.reshape(TOKENS, D).astype(jnp.bfloat16), grad_stream.reshape(TOKENS, D), grads_one[0], grads_one[1], grads_one[2], grads_one[3], grads_one[4], grads_one[5], grads_one[6], grads_two[0], grads_two[1], grads_two[2], grads_two[3], grads_two[4], grads_two[5], grads_two[6], stream_rms)
```

```python
import functools
import math

import jax
import jax.numpy as jnp
from jax import lax
from jax.experimental import pallas as pl
from jax.experimental.pallas import tpu as pltpu
from jax.sharding import PartitionSpec as P

DILATION_RATE = 8
EPS = 1e-05
CHAIN = 256
CHAINS = 2
TILE = CHAIN * CHAINS
LANES = 128
CHUNK = 32
K0 = math.sqrt(2.0 / math.pi)
BEND = (K0 * 0.044715) ** (1.0 / 3.0)
BASE = K0 / BEND
F32 = jnp.float32
BF16 = jnp.bfloat16


def gelu(m):
    square = m * m
    bent = jnp.tanh(m * (BASE + square))
    share = (0.5 / BEND) + (0.5 / BEND) * bent
    act = m * share
    return act, share + (act * (1.0 - bent)) * (BASE + 3.0 * square)


def scaled_by(gains, first, rows, hat):
    return hat * wide(gains[first, rows, :]) + wide(gains[first + 1, rows, :])


def wide(column):
    return jnp.concatenate([column, column], axis=1)


def fold(v):
    return v[:, :LANES] + v[:, LANES:]


def down_rows(v):
    return jnp.sum(v.reshape(-1, 8, v.shape[1]), axis=0)


def total_rows(v):
    return jnp.sum(v, axis=0, keepdims=True)


def chunks(count):
    return [slice(start, min(start + CHUNK, count)) for start in range(0, count, CHUNK)]


def half_chunks(count):
    half = count // 2
    return [slice(base + c.start, base + c.stop) for base in (0, half) for c in chunks(half)]


def up_to(value, step):
    return (value + step - 1) // step * step


def chain_lanes(chain):
    return slice(chain * CHAIN, (chain + 1) * CHAIN)


def together(*lists):
    marked = []
    for steps in lists:
        marked += [((k + 0.5) / len(steps), step) for k, step in enumerate(steps)]
    for _, step in sorted(marked, key=lambda pair: pair[0]):
        step()


def in_chains(*stages):
    built = [[stage(chain, chain_lanes(chain)) for stage in stages] for chain in range(CHAINS)]
    first, second = built
    together(first[0])
    for k in range(1, len(stages)):
        together(first[k], second[k - 1])
    together(second[-1])


def per_chunk(count, work):
    return [functools.partial(work, rows) for rows in chunks(count)]


class Places:
    def __init__(self, lengths, padding, own, step):
        self.own = own
        self.core = lax.axis_index("ch")
        self.step = step
        self.ends = []
        end = 0
        for k in range(lengths.shape[1]):
            end = end + lengths[0, k]
            self.ends.append(end)
        self.pad_start = 2 * own - padding[0]

    def of(self, chain):
        base = self.core * self.own + self.step * TILE + chain * CHAIN
        return base + lax.broadcasted_iota(jnp.int32, (1, CHAIN), 1)

    def segment(self, at):
        count = jnp.zeros((1, CHAIN), jnp.int32)
        for end in self.ends:
            count = count + jnp.where(at >= end, 1, 0)
        count = jnp.where(at >= self.pad_start, len(self.ends), count)
        return jnp.where(at < 0, -1, count)

    def valid(self, chain):
        return self.of(chain) < self.pad_start

    def tokens(self):
        return jnp.clip(self.pad_start - self.core * self.own, 0, self.own).astype(F32)


def tap_masks(places, chain, offsets):
    at = places.of(chain)
    mine = places.segment(at)
    result = []
    for offset in offsets:
        other = places.segment(at + offset * DILATION_RATE)
        keep = jnp.where((other == mine) & (mine < len(places.ends)), 1.0, 0.0)
        result.append(jnp.broadcast_to(keep, (16, CHAIN)).astype(BF16))
    return result


def shifted(parts, rows, chain, offset, mask):
    left, middle, right = parts
    lanes = chain_lanes(chain)
    if offset == 0:
        piece = middle[rows, lanes]
    elif offset < 0:
        before = left[rows, :] if chain == 0 else middle[rows, lanes.start - LANES : lanes.start]
        ext = jnp.concatenate([before, middle[rows, lanes]], axis=1)
        piece = pltpu.roll(ext, -offset * DILATION_RATE, 1)[:, LANES:]
    else:
        after = right[rows, :] if chain == CHAINS - 1 else middle[rows, lanes.stop : lanes.stop + LANES]
        ext = jnp.concatenate([middle[rows, lanes], after], axis=1)
        piece = pltpu.roll(ext, ext.shape[1] - offset * DILATION_RATE, 1)[:, :CHAIN]
    count = piece.shape[0]
    if count % 16:
        return piece * jnp.concatenate([mask] * (count // 16 + 1), axis=0)[:count]
    return (piece.reshape(count // 16, 16, CHAIN) * mask[None]).reshape(count, CHAIN)


def stack_forward(stack, parts, places, offsets):
    count = parts[1].shape[0]

    def stage(chain, lanes):
        masks = tap_masks(places, chain, offsets)

        def step(number, rows):
            piece = shifted(parts, rows, chain, offsets[number], masks[number])
            stack[number * count + rows.start : number * count + rows.stop, lanes] = piece

        return [functools.partial(step, number, rows) for number in range(len(offsets)) for rows in chunks(count)]

    return stage


def stack_backward(stack, parts, places, offsets):
    count = parts[1].shape[0]
    half = count // 2
    part = stack.shape[0] // 2

    def stage(chain, lanes):
        masks = tap_masks(places, chain, offsets)

        def step(number, rows):
            piece = shifted(parts, rows, chain, offsets[number], masks[number])
            for which in range(2):
                first = max(rows.start, which * half)
                last = min(rows.stop, (which + 1) * half)
                if first < last:
                    at = which * part + number * half + first - which * half
                    stack[at : at + last - first, lanes] = piece[first - rows.start : last - rows.start, :]

        return [functools.partial(step, number, rows) for number in range(len(offsets)) for rows in chunks(count)]

    return stage


class Totals:
    def __init__(self):
        self.sums = {}

    def add(self, name, value):
        value = down_rows(value)
        self.sums[name] = self.sums[name] + value if name in self.sums else value

    def get(self, name):
        return total_rows(self.sums[name])


def inner_norm(values, lanes, gains, first, act_out, hat_out, scale_out, slope_out=None):
    count = values.shape[0]
    totals, stats = Totals(), {}

    def measure(rows):
        value = values[rows, lanes]
        totals.add("one", value)
        totals.add("two", value * value)

    def settle():
        stats["centre"] = totals.get("one") / count
        stats["scale"] = lax.rsqrt(totals.get("two") / count - stats["centre"] * stats["centre"] + EPS)
        scale_out[:, lanes] = stats["scale"]

    def apply(rows):
        hat = (values[rows, lanes] - stats["centre"]) * stats["scale"]
        hat_out[rows, lanes] = hat.astype(hat_out.dtype)
        act, slope = gelu(scaled_by(gains, first, rows, hat))
        act_out[rows, lanes] = act.astype(BF16)
        if slope_out is not None:
            slope_out[rows, lanes] = slope.astype(BF16)

    return [*per_chunk(count, measure), settle, *per_chunk(count, apply)]


def outer_norm(begin, load, reload, count, lanes, gains, act_out, hat_out, scale_out, squares):
    totals, stats = Totals(), {}

    def prepare():
        stats["about"] = begin()

    def measure(rows):
        shifted = load(rows) - stats["about"]
        totals.add("one", shifted)
        totals.add("two", shifted * shifted)

    def settle():
        off = totals.get("one") / count
        spread = totals.get("two") / count - off * off
        stats["centre"] = stats["about"] + off
        stats["scale"] = lax.rsqrt(spread + EPS)
        scale_out[:, lanes] = stats["scale"]
        squares(count * (spread + stats["centre"] * stats["centre"]))

    def apply(rows):
        hat = (reload(rows) - stats["centre"]) * stats["scale"]
        hat_out[rows, lanes] = hat.astype(BF16)
        act_out[rows, lanes] = gelu(scaled_by(gains, 0, rows, hat))[0].astype(BF16)

    return [prepare, *per_chunk(count, measure), settle, *per_chunk(count, apply)]


def norm_back(grad, lanes, hat_of, scale_of, gains, first, sums, store, slope_of=None, act_out=None):
    count = grad.shape[0]
    totals, stats = Totals(), {}

    def measure(rows):
        hat = hat_of(rows)
        if slope_of is None:
            act, slope = gelu(scaled_by(gains, first, rows, hat))
            if act_out is not None:
                act_out[rows, lanes] = act.astype(BF16)
        else:
            slope = slope_of(rows)
        gain = wide(gains[first, rows, :])
        before = grad[rows, lanes] * slope
        along = before * hat
        sums[0, rows, :] += fold(along)
        sums[1, rows, :] += fold(before)
        scaled = before * gain
        grad[rows, lanes] = scaled
        totals.add("one", scaled)
        totals.add("two", along * gain)

    def settle():
        scale = scale_of()
        stats["scale"] = scale
        stats["base"] = scale * (totals.get("one") / count)
        stats["tilt"] = scale * (totals.get("two") / count)

    def apply(rows):
        value = grad[rows, lanes] * stats["scale"] - stats["base"]
        store(rows, value - hat_of(rows) * stats["tilt"])

    return [*per_chunk(count, measure), settle, *per_chunk(count, apply)]


def kept_back(grad, lanes, hats, scales, gains, sums, store, **more):
    return norm_back(grad, lanes, lambda rows: hats[rows, lanes].astype(F32), lambda: scales[:, lanes], gains, 0,
                     sums, store, **more)


def dot(left, right):
    return jnp.dot(left, right, preferred_element_type=F32)


def dot_nt(left, right):
    return lax.dot_general(left, right, (((1,), (1,)), ((), ())), preferred_element_type=F32)


def multiply(target, left, right):
    rows, depth = left.shape

    def stage(chain, lanes):
        def deep(start):
            stop = min(start + 2 * CHAIN, depth)
            part = dot(left[:, start:stop], right[start:stop, lanes])
            target[:, lanes] = part if start == 0 else target[:, lanes] + part

        def high(start):
            stop = min(start + 400, rows)
            target[start:stop, lanes] = dot(left[start:stop, :], right[:, lanes])

        if depth > 2 * CHAIN:
            return [functools.partial(deep, start) for start in range(0, depth, 2 * CHAIN)]
        return [functools.partial(high, start) for start in range(0, rows, 400)]

    return stage


def add_product(target, left, right, lanes=slice(None)):
    count = 400 if left.shape[0] % 400 == 0 else 512

    def step(start):
        stop = min(start + count, left.shape[0])
        target[start:stop, :] += dot_nt(left[start:stop, lanes], right[:, lanes])

    return [functools.partial(step, start) for start in range(0, left.shape[0], count)]


def in_order(core, mine, other, axis):
    return jnp.where(
        core == 0, jnp.concatenate([mine, other], axis=axis), jnp.concatenate([other, mine], axis=axis)
    )


def spread_outer(gain, bias, gains):
    for place, vector in enumerate((gain, bias)):
        column = vector[...].astype(F32).reshape(1, -1).T
        gains[place, :, :] = jnp.broadcast_to(BEND * column, gains.shape[1:])


def spread_inner(core, small, small_other, numbers, gains):
    columns = in_order(core, small[...].astype(F32).T, small_other[...].astype(F32).T, 0)
    for place, number in enumerate(numbers):
        gains[place, :, :] = jnp.broadcast_to(BEND * columns[:, number : number + 1], gains.shape[1:])


def joined(core, mine, other, target):
    target[...] = in_order(core, mine[...], other[...], 0)


def joined_t(core, mine, other, target):
    target[...] = in_order(core, mine[...], other[...], 0).T


def conv_forward_weight(core, mine, other, target):
    taps, count, _ = mine.shape
    for tap in range(taps):
        target[:, tap * count : (tap + 1) * count] = in_order(core, mine[tap].T, other[tap].T, 0)


def conv_backward_weight(core, mine, other, target):
    taps, _, half = mine.shape
    part = target.shape[1] // 2
    target[...] = jnp.zeros(target.shape, target.dtype)
    for tap in range(taps):
        one, two = mine[tap], other[tap]
        target[:, tap * half : (tap + 1) * half] = jnp.where(core == 0, one, two)
        target[:, part + tap * half : part + (tap + 1) * half] = jnp.where(core == 0, two, one)


def pack_conv(acc, core, mine, other, base):
    both, count = acc.shape
    slabs = both // 2 // LANES
    for slab in range(slabs):
        one = acc[slab * LANES : (slab + 1) * LANES, :].astype(BF16).T
        two = acc[both // 2 + slab * LANES : both // 2 + (slab + 1) * LANES, :].astype(BF16).T
        at = base + slab * count
        mine[at : at + count, :] = jnp.where(core == 0, one, two)
        other[at : at + count, :] = jnp.where(core == 0, two, one)


def pack_wide(acc, core, mine, other, base):
    width, count = acc.shape
    half = count // 2
    for slab in range(up_to(width, LANES) // LANES):
        some = min(LANES, width - slab * LANES)
        value = acc[slab * LANES : slab * LANES + some, :]
        if some < LANES:
            value = jnp.concatenate([value, jnp.zeros((LANES - some, count), F32)], axis=0)
        value = value.astype(BF16).T
        one, two = value[:half, :], value[half:, :]
        at = base + slab * half
        mine[at : at + half, :] = jnp.where(core == 0, one, two)
        other[at : at + half, :] = jnp.where(core == 0, two, one)


def wide_rows(half, width):
    return up_to(width, LANES) // LANES * half


def row_form(sums, target):
    for k in range(sums.shape[0]):
        target[k, :, :] = lax.dot_general(
            jnp.full((8, LANES), BEND, F32), sums[k, :, :], (((1,), (1,)), ((), ())),
            precision=lax.Precision.HIGHEST, preferred_element_type=F32,
        )


def clear(step, *refs):
    @pl.when(step == 0)
    def _():
        for ref in refs:
            ref[...] = jnp.zeros(ref.shape, ref.dtype)


def row_list(line):
    width = line.shape[1]
    line = jnp.concatenate([line, jnp.zeros((1, up_to(width, LANES) - width), F32)], axis=1)
    return [line[:, at : at + LANES] for at in range(0, line.shape[1], LANES)]


def rows_together(rows, multiple):
    pad = up_to(len(rows), multiple) - len(rows)
    return jnp.concatenate(rows + [jnp.zeros((pad, LANES), F32)] * bool(pad), axis=0)


def small_rows(core, inner):
    mine, other = [], []
    for ref in inner:
        for k in range(2):
            line = ref[k, 0:1, :]
            half = line.shape[1] // 2
            for one, two in zip(row_list(line[:, :half]), row_list(line[:, half:])):
                mine.append(jnp.where(core == 0, one, two))
                other.append(jnp.where(core == 0, two, one))
    return rows_together(mine, 16), rows_together(other, 16)


def small_count(half):
    return up_to(8 * (up_to(half, LANES) // LANES), 16)


def moment_row(moments, count):
    lane = lax.broadcasted_iota(jnp.int32, (1, LANES), 1)
    line = jnp.where(lane == len(moments), count, jnp.zeros((1, LANES), F32))
    for k, row in enumerate(moments):
        line = line + jnp.where(lane == k, jnp.sum(row, axis=1, keepdims=True), 0.0)
    return line


def keep_edge(core, step, tiles, source, target):
    @pl.when(step == jnp.where(core == 0, tiles - 1, 0))
    def _():
        target[...] = jnp.where(core == 0, source[:, TILE - LANES :], source[:, :LANES])


def kernel_one(tiles, lengths, padding, x, norm_gain, norm_bias, small, small_other, down, down_other, a_out,
               xhat_out, xscale_out, b_out, hat_out, scale_out, edge_out, moments, g_outer, g_inner, down_t, hidden):
    step = pl.program_id(0)
    places = Places(lengths, padding, tiles * TILE, step)
    core = places.core

    @pl.when(step == 0)
    def _():
        spread_outer(norm_gain, norm_bias, g_outer)
        spread_inner(core, small, small_other, (0, 2), g_inner)
        joined(core, down, down_other, down_t)

    clear(step, moments)

    def norm(chain, lanes):
        def load(rows):
            return x[rows, lanes].astype(F32)

        def squares(value):
            moments[0:1, :] += jnp.where(places.valid(chain), value, 0.0)

        return outer_norm(lambda: load(slice(0, 16))[0:1], load, load, x.shape[0], lanes, g_outer, a_out,
                          xhat_out, xscale_out, squares)

    def inner(chain, lanes):
        return inner_norm(hidden, lanes, g_inner, 0, b_out, hat_out, scale_out)

    in_chains(norm, multiply(hidden, down_t, a_out), inner)
    keep_edge(core, step, tiles, b_out, edge_out)


def choose_edges(step, tiles, halo, left, right, edge_left, edge_right):
    if left is not None:
        edge_left[...] = jnp.where(step == 0, halo[...], left[...])
    if right is not None:
        edge_right[...] = jnp.where(step == tiles - 1, halo[...], right[...])


def kernel_two(tiles, lengths, padding, b_left, b_mid, b_right, x, b_halo, norm_gain, norm_bias, small,
               small_other, conv, conv_other, up, up_other, down, down_other, y_out, chat_out, cscale_out, a_out,
               yhat_out, yscale_out, b_out, hat_out, scale_out, edge_out, moments, stack, g_outer, g_inner, conv_f, up_t, down_t, mixed, stream,
               edge_left, edge_right, act):
    step = pl.program_id(0)
    places = Places(lengths, padding, tiles * TILE, step)
    core = places.core

    @pl.when(step == 0)
    def _():
        spread_outer(norm_gain, norm_bias, g_outer)
        spread_inner(core, small, small_other, (1, 3, 4, 6), g_inner)
        conv_forward_weight(core, conv, conv_other, conv_f)
        joined_t(core, up, up_other, up_t)
        joined(core, down, down_other, down_t)

    clear(step, moments)
    choose_edges(step, tiles, b_halo, b_left, b_right, edge_left, edge_right)
    width = x.shape[0]
    gather = stack_forward(stack, (edge_left, b_mid, edge_right), places, (-2, -1, 0, 1, 2))

    def second(chain, lanes):
        return inner_norm(mixed, lanes, g_inner, 0, act, chat_out, cscale_out)

    def outer(chain, lanes):
        valid = places.valid(chain)
        totals = Totals()

        def branch_of(rows):
            return jnp.where(valid, stream[rows, lanes], 0.0)

        def begin():
            return branch_of(slice(0, 8))[0:1] + x[0:16, lanes].astype(F32)[0:1]

        def load(rows):
            branch = branch_of(rows)
            value = x[rows, lanes].astype(F32) + branch
            stream[rows, lanes] = value
            y_out[rows, lanes] = value.astype(BF16)
            totals.add("branch", branch * branch)
            return value

        def squares(value):
            moments[0:1, :] += totals.get("branch")
            moments[1:2, :] += jnp.where(valid, value, 0.0)

        return outer_norm(begin, load, lambda rows: stream[rows, lanes], width, lanes, g_outer, a_out,
                          yhat_out, yscale_out, squares)

    def first(chain, lanes):
        return inner_norm(mixed, lanes, g_inner, 2, b_out, hat_out, scale_out)

    in_chains(gather, multiply(mixed, conv_f, stack), second, multiply(stream, up_t, act), outer,
              multiply(mixed, down_t, a_out), first)
    keep_edge(core, step, tiles, b_out, edge_out)


def kernel_three(tiles, lengths, padding, b_left, b_mid, t, b_halo, small, small_other, conv, conv_other, up,
                 up_other, act, dc_out, edge_out, mine, other, sums_out, stack, g_inner, conv_f, up_all, sums, mixed,
                 turned, hats, slopes, scales, du, edge_left, up_grad):
    step = pl.program_id(0)
    places = Places(lengths, padding, tiles * TILE, step)
    core = places.core

    @pl.when(step == 0)
    def _():
        spread_inner(core, small, small_other, (5, 7), g_inner)
        conv_forward_weight(core, conv, conv_other, conv_f)
        joined(core, up, up_other, up_all)

    clear(step, sums, up_grad)
    choose_edges(step, tiles, b_halo, b_left, None, edge_left, None)
    gather = stack_forward(stack, (edge_left, b_mid, None), places, (-2, -1, 0))

    def turn(chain, lanes):
        keep = jnp.where(places.valid(chain), 1.0, 0.0)
        keep = jnp.broadcast_to(keep, (16, CHAIN)).astype(BF16)

        def step(rows):
            piece = t[rows, lanes].reshape(-1, 16, CHAIN) * keep[None]
            du[rows, lanes] = piece.reshape(-1, CHAIN)

        return per_chunk(t.shape[0], step)

    def second(chain, lanes):
        return inner_norm(mixed, lanes, g_inner, 0, act, hats, scales, slopes)

    def back(chain, lanes):
        def store(rows, v):
            dc_out[rows, lanes] = v.astype(BF16)

        return kept_back(turned, lanes, hats, scales, g_inner, sums, store,
                          slope_of=lambda rows: slopes[rows, lanes].astype(F32))

    one, two = ((chain, chain_lanes(chain)) for chain in range(CHAINS))
    convolve, lower = multiply(mixed, conv_f, stack), multiply(turned, up_all, du)
    together(gather(*one) + turn(*one))
    together(convolve(*one) + lower(*one), gather(*two) + turn(*two))
    together(convolve(*two) + lower(*two), second(*one) + back(*one))
    together(second(*two))
    together(add_product(up_grad, du, act), back(*two))
    keep_edge(core, step, tiles, dc_out, edge_out)

    @pl.when(step == tiles - 1)
    def _():
        row_form(sums, sums_out)
        pack_wide(up_grad, core, mine, other, 0)


def kernel_last(tiles, lengths, padding, e_mid, y, up, up_other, y_out, moments, up_t, stream):
    step = pl.program_id(0)
    places = Places(lengths, padding, tiles * TILE, step)

    @pl.when(step == 0)
    def _():
        joined_t(places.core, up, up_other, up_t)

    clear(step, moments)

    def finish(chain, lanes):
        valid = places.valid(chain)
        totals = Totals()

        def step(rows):
            branch = jnp.where(valid, stream[rows, lanes], 0.0)
            value = y[rows, lanes].astype(F32) + branch
            y_out[rows, lanes] = value.astype(BF16)
            totals.add("branch", branch * branch)
            totals.add("value", value * value)

        def settle():
            moments[0:1, :] += totals.get("branch")
            moments[1:2, :] += jnp.where(valid, totals.get("value"), 0.0)

        return [*per_chunk(y.shape[0], step), settle]

    in_chains(multiply(stream, up_t, e_mid), finish)


def back_conv(gather, conv_b, stack, hats, scales, g_inner, sums, mixed, dh, b_mid, a_mid, conv_grad, down_grad):
    def first(chain, lanes):
        def store(rows, v):
            dh[rows, lanes] = v.astype(BF16)

        return kept_back(mixed, lanes, hats, scales, g_inner, sums, store)

    one, two = ((chain, chain_lanes(chain)) for chain in range(CHAINS))
    convolve = multiply(mixed, conv_b, stack)
    together(gather(*one))
    together(convolve(*one), gather(*two))
    together(convolve(*two), first(*one))
    together(add_product(conv_grad, stack, b_mid), first(*two))
    together(add_product(down_grad, a_mid, dh))


def kernel_four(tiles, lengths, padding, dc_mid, dc_right, b_mid, hats, scales, a_mid, yhats, yscales, t, chats,
                cscales, dc_halo, norm_gain, norm_bias, small, small_other, conv, conv_other, down, down_other, up,
                up_other, mine_up, other_up, g_out, dc_out, edge_out, mine, other, outer_out, inner_out, prev_out,
                stack, g_outer, g_inner, g_prev, conv_b, down_all, up_all, sums_outer, sums_inner, sums_prev,
                conv_grad, down_grad, up_grad, mixed, lower_mixed, wide_grad, dh, du, act, edge_right):
    step = pl.program_id(0)
    places = Places(lengths, padding, tiles * TILE, step)
    core = places.core

    @pl.when(step == 0)
    def _():
        spread_outer(norm_gain, norm_bias, g_outer)
        spread_inner(core, small, small_other, (4, 6), g_inner)
        spread_inner(core, small, small_other, (1, 3), g_prev)
        conv_backward_weight(core, conv, conv_other, conv_b)
        joined_t(core, down, down_other, down_all)
        joined(core, up, up_other, up_all)

    clear(step, stack, conv_grad, down_grad, up_grad, sums_outer, sums_inner, sums_prev)
    choose_edges(step, tiles, dc_halo, None, dc_right, None, edge_right)
    gather = stack_backward(stack, (None, dc_mid, edge_right), places, (2, 1, 0))

    def first(chain, lanes):
        def store(rows, v):
            dh[rows, lanes] = v.astype(BF16)

        return kept_back(mixed, lanes, hats, scales, g_inner, sums_inner, store)

    def outer(chain, lanes):
        keep = jnp.where(places.valid(chain), 1.0, 0.0)
        keep = jnp.broadcast_to(keep, (16, CHAIN)).astype(BF16)

        def store(rows, v):
            grad = (v + t[rows, lanes].astype(F32)).astype(BF16)
            g_out[rows, lanes] = grad
            du[rows, lanes] = (grad.reshape(-1, 16, CHAIN) * keep[None]).reshape(-1, CHAIN)

        return kept_back(wide_grad, lanes, yhats, yscales, g_outer, sums_outer, store)

    def second(chain, lanes):
        def store(rows, v):
            dc_out[rows, lanes] = v.astype(BF16)

        return kept_back(lower_mixed, lanes, chats, cscales, g_prev, sums_prev, store, act_out=act)

    one, two = ((chain, chain_lanes(chain)) for chain in range(CHAINS))
    convolve, lift = multiply(mixed, conv_b, stack), multiply(wide_grad, down_all, dh)
    lower = multiply(lower_mixed, up_all, du)
    products = add_product(conv_grad, stack, b_mid)
    some = len(products) // 2
    together(gather(*one))
    together(convolve(*one), gather(*two))
    together(convolve(*two), first(*one))
    together(lift(*one), first(*two))
    together(lift(*two) + products[:some], outer(*one))
    together(lower(*one) + products[some:], outer(*two))
    together(lower(*two) + add_product(down_grad, a_mid, dh), second(*one))
    together(add_product(up_grad, du, act, one[1]), second(*two))
    together(add_product(up_grad, du, act, two[1]))
    keep_edge(core, step, tiles, dc_out, edge_out)

    @pl.when(step == tiles - 1)
    def _():
        row_form(sums_outer, outer_out)
        row_form(sums_inner, inner_out)
        row_form(sums_prev, prev_out)
        at = pack(core, mine, other, conv_grad, (down_grad, up_grad))
        rows = mine_up.shape[0]
        mine[at : at + rows, :] = mine_up[...]
        other[at : at + rows, :] = other_up[...]
        pad_payload(mine, other, at + rows)


def pack(core, mine, other, conv_grad, wides):
    both, count = conv_grad.shape
    pack_conv(conv_grad, core, mine, other, 0)
    at = count * (both // 2 // LANES)
    for ref in wides:
        pack_wide(ref, core, mine, other, at)
        at += wide_rows(count // 2, ref.shape[0])
    return at


def pad_payload(mine, other, at):
    if at < mine.shape[0]:
        for target in (mine, other):
            target[at:, :] = jnp.zeros((mine.shape[0] - at, LANES), BF16)


def kernel_six(tiles, lengths, padding, dc_left, dc_mid, dc_right, b_mid, hats, scales, a_mid, dc_halo, small, small_other, conv, conv_other, inner_two, prev_one, prev_two, dh_out,
               mine, other, stack, g_inner, conv_b, sums, conv_grad, down_grad, mixed, edge_left,
               edge_right, inner_one):
    step = pl.program_id(0)
    places = Places(lengths, padding, tiles * TILE, step)
    core = places.core

    @pl.when(step == 0)
    def _():
        spread_inner(core, small, small_other, (0, 2), g_inner)
        conv_backward_weight(core, conv, conv_other, conv_b)

    clear(step, stack, conv_grad, down_grad, sums)
    choose_edges(step, tiles, dc_halo, dc_left, dc_right, edge_left, edge_right)
    gather = stack_backward(stack, (edge_left, dc_mid, edge_right), places, (2, 1, 0, -1, -2))
    back_conv(gather, conv_b, stack, hats, scales, g_inner, sums, mixed, dh_out, b_mid, a_mid, conv_grad, down_grad)

    @pl.when(step == tiles - 1)
    def _():
        row_form(sums, inner_one)
        extra = small_rows(core, (inner_one, prev_one, inner_two, prev_two))
        at = pack(core, mine, other, conv_grad, (down_grad,))
        for target, value in zip((mine, other), extra):
            target[at : at + value.shape[0], :] = value.astype(BF16)
        pad_payload(mine, other, at + extra[0].shape[0])


def outer_first_tile(dh, xhats, xscales, g, down_all, g_outer, sums, dx_out, wide_grad):
    def outer(chain, lanes):
        def store(rows, v):
            dx_out[rows, lanes] = v + g[rows, lanes].astype(F32)

        return kept_back(wide_grad, lanes, xhats, xscales, g_outer, sums, store)

    in_chains(multiply(wide_grad, down_all, dh), outer)


def kernel_seven(tiles, lengths, padding, dh, xhats, xscales, g, norm_gain, norm_bias, down, down_other, dx_out,
                 sums, g_outer, down_all, wide_grad):
    step = pl.program_id(0)
    core = lax.axis_index("ch")

    @pl.when(step == 0)
    def _():
        spread_outer(norm_gain, norm_bias, g_outer)
        joined_t(core, down, down_other, down_all)

    clear(step, sums)
    outer_first_tile(dh, xhats, xscales, g, down_all, g_outer, sums, dx_out, wide_grad)


def kernel_eight(tiles, lengths, padding, dh, xhats, xscales, g, dx_begun, norm_gain, norm_bias, down, down_other,
                 sums_begun, moments_one, moments_two, moments_three, outer_two, dx_out, rows_out, g_outer,
                 down_all, sums, wide_grad, outer_one):
    step = pl.program_id(0)
    places = Places(lengths, padding, tiles * TILE, step)
    core = places.core

    @pl.when(step == 0)
    def _():
        spread_outer(norm_gain, norm_bias, g_outer)
        joined_t(core, down, down_other, down_all)
        sums[...] = sums_begun[...]

    outer_first_tile(dh, xhats, xscales, g, down_all, g_outer, sums, dx_out, wide_grad)

    @pl.when(step == pl.num_programs(0) - 1)
    def _():
        row_form(sums, outer_one)
        rows = [moments_one[0:1, :], moments_two[0:1, :], moments_two[1:2, :], moments_three[0:1, :],
                moments_three[1:2, :]]
        lines = [row for ref in (outer_one, outer_two) for k in range(2) for row in row_list(ref[k, 0:1, :])]
        rows_out[...] = rows_together(lines + [moment_row(rows, places.tokens())], 8)


def split_three(v):
    one = v.astype(BF16)
    rest = v - one.astype(F32)
    two = rest.astype(BF16)
    return one, two, (rest - two.astype(F32)).astype(BF16)


def sum_of_three(parts):
    one, two, three = (part.astype(F32) for part in parts)
    return one + (two + three)


def write_lines(out, at, lines):
    for part in split_three(lines):
        out[at : at + part.shape[0], :] = part
        at += part.shape[0]


def read_lines(ref, count):
    start = ref.shape[0] - 3 * count
    return sum_of_three([ref[start + k * count : start + (k + 1) * count, :] for k in range(3)])


def all_lines(refs, count):
    values = [read_lines(ref, count) for ref in refs]
    while len(values) > 1:
        values = [values[k] + values[k + 1] for k in range(0, len(values), 2)]
    return values[0]


def finish_kernel(own, *refs):
    *arrived, lines, lines_other, out = refs
    total = own[...]
    for ref in arrived:
        total = total + ref[...].astype(F32)
    rows = total.shape[0]
    out[:rows, :] = total.astype(BF16)
    write_lines(out, rows, lines[...] + lines_other[...])


def place_kernel(number, count, scal, *refs):
    *parts, out = refs
    rows = parts[0].shape[0] - 3 * count
    for turn, ref in enumerate(parts):
        out[pl.ds(pl.multiple_of((scal[number] ^ turn) * rows, 16), rows), :] = ref[:rows, :]
    if count:
        write_lines(out, len(parts) * rows, all_lines(parts, count))


def unpack(rows_of, conv_out, wide_outs, inner_outs):
    taps, count, half = conv_out.shape
    slabs = up_to(taps * half, LANES) // LANES
    for start in range(0, count, 80):
        rows = min(80, count - start)
        line = jnp.concatenate([rows_of(k * count + start, rows) for k in range(slabs)], axis=1)
        for tap in range(taps):
            conv_out[tap, start : start + rows, :] = line[:, tap * half : (tap + 1) * half]
    base = slabs * count
    for out in wide_outs:
        width = out.shape[1]
        for slab in range(up_to(width, LANES) // LANES):
            lanes = slice(slab * LANES, min(width, (slab + 1) * LANES))
            value = rows_of(base + slab * half, half)
            out[:, lanes] = value[:, : lanes.stop - lanes.start]
        base += wide_rows(half, width)
    if not inner_outs:
        return
    table = rows_of(base, small_count(half))
    at = 0
    count = up_to(half, LANES) // LANES
    for number in range(8):
        line = jnp.concatenate([table[at + k : at + k + 1, :] for k in range(count)], axis=1)
        norm, what = number // 2, number % 2
        inner_outs[2 * (norm // 2) + what][norm % 2 : norm % 2 + 1, :] = line[:, :half]
        at += count


def unpack_kernel(number, wides, count, scal, one, two, conv_out, *rest):
    flat = rest[-1]
    rows = one.shape[0] - 3 * count
    for turn, ref in enumerate((one, two)):
        flat[pl.ds(pl.multiple_of((scal[number] ^ turn) * rows, 16), rows), :] = ref[:rows, :]
    outs = rest[:-1]
    if count:
        *outs, moments_out = outs
        outs, vectors = outs[:-4], outs[-4:]
        lines = all_lines((one, two), count)
        width = vectors[0].shape[0]
        at = 0
        for vector in vectors:
            for start in range(0, width, LANES):
                some = min(LANES, width - start)
                vector[start : start + some] = lines[at : at + 1, :some].reshape(some)
                at += 1
        totals = lines[at : at + 1, :]
        amount = moments_out.shape[0]
        means = totals[:, :amount] / (totals[:, amount : amount + 1] * width)
        moments_out[...] = jnp.sqrt(means).reshape(amount)
    unpack(lambda at, some: flat[at : at + some, :].astype(F32), conv_out, outs[:wides], outs[wides:])


def swap(values):
    return lax.ppermute(values, "ch", [(0, 1), (1, 0)])


def local(inputs, cotangent, doc_lengths, trailing_pad_tokens, first_norm_gain, first_norm_bias, first_down,
          first_inner_gain, first_inner_bias, first_conv, first_up, second_norm_gain, second_norm_bias,
          second_down, second_inner_gain, second_inner_bias, second_conv, second_up):
    own, width = inputs.shape
    half = first_down.shape[1]
    inner = 2 * half
    tiles = own // TILE
    x = inputs.T
    t = cotangent.T

    small = jnp.concatenate([first_inner_gain, first_inner_bias, second_inner_gain, second_inner_bias], axis=0)
    smalls = (small, swap(small))
    vector_rows = up_to(width, LANES) // LANES
    first_vectors = (first_norm_gain, first_norm_bias)
    second_vectors = (second_norm_gain, second_norm_bias)

    def with_other(v):
        return v, swap(v)

    down_1 = with_other(first_down.T)
    conv_1 = with_other(first_conv)
    up_1 = with_other(first_up)
    down_2 = with_other(second_down.T)
    conv_2 = with_other(second_conv)
    up_2 = with_other(second_up)

    last_lane = own // LANES - 1
    ratio = TILE // LANES

    def tile_of(count, first=0):
        return pl.BlockSpec((count, TILE), lambda i, *s: (0, i + first))

    def left_of(count):
        return pl.BlockSpec((count, LANES), lambda i, *s: (0, jnp.maximum(ratio * i - 1, 0)))

    def right_of(count):
        return pl.BlockSpec((count, LANES), lambda i, *s: (0, jnp.minimum(ratio * i + ratio, last_lane)))

    def whole(*shape):
        zeros = (0,) * len(shape)
        return pl.BlockSpec(shape, lambda i, *s: zeros)

    def whole_of(v):
        return whole(*v.shape)

    anywhere = pl.BlockSpec(memory_space=pl.ANY)

    def shape(*dims, dtype=F32):
        return jax.ShapeDtypeStruct(dims, dtype)

    limits = {
        "norm_down": 16,
        "conv_up_norm_down": 32,
        "conv_turn": 22,
        "back_second": 44,
        "back_conv_first": 30,
        "up_second": 12,
        "back_outer_early": 16,
        "back_outer_late": 18,
        "places": 6,
        "finish": 6,
        "unpack_second": 14,
        "unpack_first": 14,
    }

    def params(name):
        return pltpu.CompilerParams(vmem_limit_bytes=limits[name] * 1024 * 1024)


    def call(kernel, name, in_specs, outs, scratch, *args, first=0, steps=tiles, aliases={}):
        specs = list(in_specs) + [whole_of(v) for v in args[len(in_specs):]]
        out_specs = [tile_of(o[0], first) if isinstance(o, tuple) else whole_of(o) for o in outs]
        out_shape = [shape(o[0], own, dtype=o[1]) if isinstance(o, tuple) else o for o in outs]
        return pl.pallas_call(
            functools.partial(kernel, tiles),
            grid_spec=pltpu.PrefetchScalarGridSpec(
                num_scalar_prefetch=2,
                grid=(steps,),
                in_specs=specs,
                out_specs=out_specs,
                scratch_shapes=scratch,
            ),
            out_shape=out_shape,
            input_output_aliases=aliases,
            compiler_params=params(name),
            cost_estimate=pl.CostEstimate(flops=15 * 1_150_000_000, bytes_accessed=0, transcendentals=0),
            name=name,
        )(doc_lengths, trailing_pad_tokens, *args)

    def vm(*dims, dtype=F32):
        return pltpu.VMEM(dims, dtype)

    def tile(count, dtype=F32):
        return pltpu.VMEM((count, TILE), dtype)

    outer_gains = vm(2, width, LANES)
    inner_gains = vm(2, inner, LANES)
    edge = vm(inner, LANES, dtype=BF16)
    edge_shape = shape(inner, LANES, dtype=BF16)
    moment_shape = shape(8, CHAIN)
    taps_1, taps_2 = first_conv.shape[0], second_conv.shape[0]
    part_1, part_2 = up_to(taps_1 * half, LANES), up_to(taps_2 * half, LANES)
    normed = [(inner, BF16), (1, F32)]
    kept = [(width, BF16), (width, BF16), (1, F32)]

    a1, xhat, xscale, b1, hat1, scale1, b1_edge, moments_one = call(
        kernel_one, "norm_down", [tile_of(width)],
        [*kept, (inner, BF16), *normed, edge_shape, moment_shape],
        [outer_gains, inner_gains, vm(inner, width, dtype=BF16), tile(inner)],
        x, *first_vectors, *smalls, *down_1,
    )

    y1, chat1, cscale1, a2, yhat, yscale, b2, hat2, scale2, b2_edge, moments_two = call(
        kernel_two, "conv_up_norm_down",         [left_of(inner), tile_of(inner), right_of(inner), tile_of(width)],
        [(width, BF16), *normed, *kept, (inner, BF16), *normed, edge_shape, moment_shape],
        [tile(taps_1 * inner, BF16), outer_gains, vm(4, inner, LANES), vm(inner, taps_1 * inner, dtype=BF16),
         vm(width, inner, dtype=BF16), vm(inner, width, dtype=BF16), tile(inner), tile(width), edge, edge,
         tile(inner, BF16)],
        b1, b1, b1, x, swap(b1_edge), *second_vectors, *smalls, *conv_1, *up_1, *down_2,
    )

    pair = wide_rows(half, width)
    gradient_up = [shape(pair, LANES, dtype=BF16)] * 2
    e2, dc2, dc2_edge, mine_up, other_up, sums_c2 = call(
        kernel_three, "conv_turn", [left_of(inner), tile_of(inner), tile_of(width)],
        [(inner, BF16), (inner, BF16), edge_shape, *gradient_up, shape(2, 8, inner)],
        [tile(taps_2 * inner, BF16), inner_gains, vm(inner, taps_2 * inner, dtype=BF16),
         vm(inner, width, dtype=BF16), vm(2, inner, LANES), tile(inner), tile(inner), tile(inner),
         tile(inner, BF16), tile(1), tile(width, BF16), edge, vm(width, inner)],
        b2, b2, t, swap(b2_edge), *smalls, *conv_2, *up_2,
    )

    row_count = lax.axis_size("rows")
    inner_in = [tile_of(inner), tile_of(1)]
    wide_in = [tile_of(width), tile_of(1)]
    rows_two = up_to(inner * (part_2 // LANES) + 3 * pair, 16 * row_count)
    rows_one = up_to(inner * (part_1 // LANES) + pair + small_count(half), 16 * row_count)
    g1, dc1, dc1_edge, mine_two, other_two, sums_o2, sums_h2, sums_c1 = call(
        kernel_four, "back_second",
        [tile_of(inner), right_of(inner), tile_of(inner), *inner_in, tile_of(width), *wide_in, tile_of(width),
         *inner_in],
        [(width, BF16), (inner, BF16), edge_shape, shape(rows_two, LANES, dtype=BF16),
         shape(rows_two, LANES, dtype=BF16), shape(2, 8, width), shape(2, 8, inner), shape(2, 8, inner)],
        [tile(2 * part_2, BF16), outer_gains, inner_gains, inner_gains, vm(inner, 2 * part_2, dtype=BF16),
         vm(width, inner, dtype=BF16), vm(inner, width, dtype=BF16), vm(2, width, LANES), vm(2, inner, LANES),
         vm(2, inner, LANES), vm(2 * part_2, inner), vm(width, inner), vm(width, inner), tile(inner),
         tile(inner), tile(width), tile(inner, BF16), tile(width, BF16), tile(inner, BF16), edge],
        dc2, dc2, b2, hat2, scale2, a2, yhat, yscale, t, chat1, cscale1, swap(dc2_edge), *second_vectors, *smalls,
        *conv_2, *down_2, *up_1, mine_up, other_up,
    )

    row_index = lax.axis_index("rows")
    core = lax.axis_index("ch")
    above = 0
    while 4 ** (above + 1) < row_count:
        above += 1
    assert 4 ** (above + 1) == row_count
    low, high = (row_index >> core) & 1, (row_index >> (1 - core)) & 1
    digits = jnp.stack(
        [2 * high + low, high, low] + [(row_index >> (2 * k + 2)) & 3 for k in range(above)]
    ).astype(jnp.int32)
    ALL, HIGH, LOW, ABOVE = 0, 1, 2, 3

    def radix(level):
        return 2 if level in (HIGH, LOW) else 4

    def flip(level, turn, c):
        if level >= ABOVE:
            return turn << (2 * (level - ABOVE) + 2)
        low_bit, high_bit = 1 << c, 1 << (1 - c)
        if level == LOW:
            return low_bit
        if level == HIGH:
            return high_bit
        return low_bit * (turn & 1) + high_bit * (turn >> 1)

    def send(v, level, turn):
        pairs = [(2 * r + c, 2 * (r ^ flip(level, turn, c)) + c) for r in range(row_count) for c in range(2)]
        return lax.ppermute(v, ("rows", "ch"), pairs)

    def small_call(kernel, name, out_shape, *args, scratch=()):
        return pl.pallas_call(
            kernel,
            grid_spec=pltpu.PrefetchScalarGridSpec(
                num_scalar_prefetch=1, grid=(1,), in_specs=[whole_of(v) for v in args],
                out_specs=jax.tree.map(whole_of, out_shape), scratch_shapes=list(scratch),
            ),
            out_shape=out_shape,
            compiler_params=params(name),
            name=name,
        )(digits, *args)

    z_levels = [ABOVE + k for k in range(above)]

    class Sum:
        def __init__(self, mine, other, levels):
            self.own, self.arrived = mine, [other]
            self.down, self.up = list(levels), [HIGH, LOW, *z_levels]

        def part(self):
            level = self.down[0]
            turns = radix(level)
            parts = [v.reshape(turns, -1, LANES) for v in (self.own, *self.arrived)]

            def share(turn):
                picked = [lax.dynamic_index_in_dim(v, digits[level] ^ turn, 0, False) for v in parts]
                return sum(v.astype(F32) for v in picked)

            self.own, *self.sends = [share(turn) for turn in range(turns)]
            self.sends = [v.astype(BF16) for v in self.sends]

        def go(self):
            level = self.down.pop(0)
            self.arrived = [send(v, level, turn + 1) for turn, v in enumerate(self.sends)]

        def finish(self, lines=None):
            self.lines = 0
            if lines is None:
                self.own = (self.own + sum(v.astype(F32) for v in self.arrived)).astype(BF16)
                return
            self.lines = lines.shape[0]
            self.own = pl.pallas_call(
                finish_kernel, out_shape=shape(self.own.shape[0] + 3 * self.lines, LANES, dtype=BF16),
                compiler_params=params("finish"), name="finish",
            )(self.own, *self.arrived, lines, swap(lines))

        def spread(self):
            self.level = self.up.pop()
            self.parts = [self.own] + [send(self.own, self.level, turn) for turn in range(1, radix(self.level))]

        def place(self):
            extra, turns = 3 * self.lines, len(self.parts)
            rows = turns * (self.own.shape[0] - extra) + extra
            self.own = small_call(
                functools.partial(place_kernel, self.level, self.lines), "places", shape(rows, LANES, dtype=BF16),
                *self.parts,
            )

    barrier = lax.optimization_barrier
    sum_two = Sum(mine_two, swap(other_two), [ALL, *z_levels])
    sum_two.part()
    dc1, *sum_two.sends = barrier((dc1, *sum_two.sends))
    sum_two.go()

    dh1, mine_one, other_one = call(
        kernel_six, "back_conv_first",
        [left_of(inner), tile_of(inner), right_of(inner), tile_of(inner), *inner_in, tile_of(width)],
        [(inner, BF16), shape(rows_one, LANES, dtype=BF16), shape(rows_one, LANES, dtype=BF16)],
        [tile(2 * part_1, BF16), inner_gains, vm(inner, 2 * part_1, dtype=BF16), vm(2, inner, LANES),
         vm(2 * part_1, inner), vm(width, inner), tile(inner), edge, edge, vm(2, 8, inner)],
        dc1, dc1, dc1, b1, hat1, scale1, a1, swap(dc1_edge), *smalls, *conv_1, sums_h2, sums_c1, sums_c2,
    )
    sum_two.part()
    dh1, mine_one, other_one, *sum_two.sends = barrier((dh1, mine_one, other_one, *sum_two.sends))
    sum_two.go()
    sum_one = Sum(mine_one, swap(other_one), [HIGH, LOW, *z_levels])
    sum_one.part()
    dh1, e2, *sum_one.sends = barrier((dh1, e2, *sum_one.sends))
    sum_one.go()

    y2, moments_three = call(
        kernel_last, "up_second", [tile_of(inner), tile_of(width)],
        [(width, BF16), moment_shape], [vm(width, inner, dtype=BF16), tile(width)],
        e2, y1, *up_2,
    )
    moments_three, *sum_two.arrived = barrier((moments_three, *sum_two.arrived))
    while sum_two.down:
        sum_two.part()
        sum_two.go()
    sum_two.finish()
    sum_one.part()
    dh1, moments_three, sum_two.own, *sum_one.sends = barrier((dh1, moments_three, sum_two.own, *sum_one.sends))
    sum_one.go()
    sum_two.spread()

    early = tiles // 2
    dx, sums_begun = call(
        kernel_seven, "back_outer_early", [tile_of(inner), *wide_in, tile_of(width)],
        [(width, F32), shape(2, width, LANES)],
        [outer_gains, vm(width, inner, dtype=BF16), tile(width)],
        dh1, xhat, xscale, g1, *first_vectors, *down_1, steps=early,
    )
    sum_two.place()
    sum_one.part()
    dh1, sums_begun, sum_two.own, *sum_one.sends = barrier((dh1, sums_begun, sum_two.own, *sum_one.sends))
    sum_one.go()
    sum_two.spread()

    line_count = up_to(4 * vector_rows + 1, 8)
    later = [tile_of(rows, early) for rows in (inner, width, 1, width)]
    dx, lines = call(
        kernel_eight, "back_outer_late", [*later, anywhere],
        [(width, F32), shape(line_count, LANES)],
        [outer_gains, vm(width, inner, dtype=BF16), vm(2, width, LANES), tile(width), vm(2, 8, width)],
        dh1, xhat, xscale, g1, dx, *first_vectors, *down_1, sums_begun, moments_one, moments_two,
        moments_three, sums_o2, first=early, steps=tiles - early, aliases={6: 0},
    )
    while sum_one.down:
        sum_one.part()
        if sum_two.up:
            sum_two.place()
        lines, sum_two.own, *sum_one.sends = barrier((lines, sum_two.own, *sum_one.sends))
        sum_one.go()
        if sum_two.up:
            sum_two.spread()
    while sum_two.up:
        sum_two.place()
        lines, sum_two.own = barrier((lines, sum_two.own))
        sum_two.spread()
    sum_one.finish(lines)
    while sum_one.up:
        sum_one.spread()
        if sum_one.up:
            sum_one.place()

    wide_shape = shape(half, width)
    conv_grad2, down_grad2, up_grad1, up_grad2 = small_call(
        functools.partial(unpack_kernel, HIGH, 3, 0), "unpack_second",
        [shape(*second_conv.shape), wide_shape, wide_shape, wide_shape],
        *sum_two.parts, scratch=[vm(rows_two, LANES, dtype=BF16)],
    )
    conv_grad1, down_grad1, *rest = small_call(
        functools.partial(unpack_kernel, HIGH, 1, line_count), "unpack_first",
        [shape(*first_conv.shape), wide_shape] + [shape(2, half)] * 4 + [shape(width)] * 4 + [shape(5)],
        *sum_one.parts, scratch=[vm(rows_one, LANES, dtype=BF16)],
    )
    return (
        y1.T, y2.T, dx.T,
        rest[4], rest[5], down_grad1.T, rest[0], rest[1], conv_grad1, up_grad1,
        rest[6], rest[7], down_grad2.T, rest[2], rest[3], conv_grad2, up_grad2,
        rest[8],
    )


def solution(mesh):
    tokens = P(("rows", "ch"), None)
    block = (P(), P(), P(None, "ch"), P(None, "ch"), P(None, "ch"), P(None, None, "ch"), P("ch", None))
    return jax.shard_map(
        local,
        mesh=mesh,
        in_specs=(tokens, tokens, P("rows", None), P("rows"), *block, *block),
        out_specs=(tokens, tokens, tokens, *block, *block, P()),
        check_vma=False,
    )
```

```python
import functools
import math

import jax
import jax.numpy as jnp
from jax import lax
from jax.experimental import pallas as pl
from jax.experimental.pallas import tpu as pltpu
from jax.sharding import PartitionSpec as P

DILATION_RATE = 8
EPS = 1e-05
CHAIN = 256
CHAINS = 2
TILE = CHAIN * CHAINS
LANES = 128
CHUNK = 32
K0 = math.sqrt(2.0 / math.pi)
BEND = (K0 * 0.044715) ** (1.0 / 3.0)
BASE = K0 / BEND
F32 = jnp.float32
BF16 = jnp.bfloat16


def gelu(m):
    square = m * m
    bent = jnp.tanh(m * (BASE + square))
    share = (0.5 / BEND) + (0.5 / BEND) * bent
    act = m * share
    return act, share + (act * (1.0 - bent)) * (BASE + 3.0 * square)


def scaled_by(gains, first, rows, hat):
    return hat * wide(gains[first, rows, :]) + wide(gains[first + 1, rows, :])


def wide(column):
    return jnp.concatenate([column, column], axis=1)


def fold(v):
    return v[:, :LANES] + v[:, LANES:]


def down_rows(v):
    return jnp.sum(v.reshape(-1, 8, v.shape[1]), axis=0)


def total_rows(v):
    return jnp.sum(v, axis=0, keepdims=True)


def chunks(count):
    return [slice(start, min(start + CHUNK, count)) for start in range(0, count, CHUNK)]


def half_chunks(count):
    half = count // 2
    return [slice(base + c.start, base + c.stop) for base in (0, half) for c in chunks(half)]


def up_to(value, step):
    return (value + step - 1) // step * step


def chain_lanes(chain):
    return slice(chain * CHAIN, (chain + 1) * CHAIN)


def together(*lists):
    marked = []
    for steps in lists:
        marked += [((k + 0.5) / len(steps), step) for k, step in enumerate(steps)]
    for _, step in sorted(marked, key=lambda pair: pair[0]):
        step()


def in_chains(*stages):
    built = [[stage(chain, chain_lanes(chain)) for stage in stages] for chain in range(CHAINS)]
    first, second = built
    together(first[0])
    for k in range(1, len(stages)):
        together(first[k], second[k - 1])
    together(second[-1])


def per_chunk(count, work):
    return [functools.partial(work, rows) for rows in chunks(count)]


class Places:
    def __init__(self, lengths, padding, own, step):
        self.own = own
        self.core = lax.axis_index("ch")
        self.step = step
        self.ends = []
        end = 0
        for k in range(lengths.shape[1]):
            end = end + lengths[0, k]
            self.ends.append(end)
        self.pad_start = 2 * own - padding[0]

    def of(self, chain):
        base = self.core * self.own + self.step * TILE + chain * CHAIN
        return base + lax.broadcasted_iota(jnp.int32, (1, CHAIN), 1)

    def segment(self, at):
        count = jnp.zeros((1, CHAIN), jnp.int32)
        for end in self.ends:
            count = count + jnp.where(at >= end, 1, 0)
        count = jnp.where(at >= self.pad_start, len(self.ends), count)
        return jnp.where(at < 0, -1, count)

    def valid(self, chain):
        return self.of(chain) < self.pad_start

    def tokens(self):
        return jnp.clip(self.pad_start - self.core * self.own, 0, self.own).astype(F32)


def tap_masks(places, chain, offsets):
    at = places.of(chain)
    mine = places.segment(at)
    result = []
    for offset in offsets:
        other = places.segment(at + offset * DILATION_RATE)
        keep = jnp.where((other == mine) & (mine < len(places.ends)), 1.0, 0.0)
        result.append(jnp.broadcast_to(keep, (16, CHAIN)).astype(BF16))
    return result


def shifted(parts, rows, chain, offset, mask):
    left, middle, right = parts
    lanes = chain_lanes(chain)
    if offset == 0:
        piece = middle[rows, lanes]
    elif offset < 0:
        before = left[rows, :] if chain == 0 else middle[rows, lanes.start - LANES : lanes.start]
        ext = jnp.concatenate([before, middle[rows, lanes]], axis=1)
        piece = pltpu.roll(ext, -offset * DILATION_RATE, 1)[:, LANES:]
    else:
        after = right[rows, :] if chain == CHAINS - 1 else middle[rows, lanes.stop : lanes.stop + LANES]
        ext = jnp.concatenate([middle[rows, lanes], after], axis=1)
        piece = pltpu.roll(ext, ext.shape[1] - offset * DILATION_RATE, 1)[:, :CHAIN]
    count = piece.shape[0]
    if count % 16:
        return piece * jnp.concatenate([mask] * (count // 16 + 1), axis=0)[:count]
    return (piece.reshape(count // 16, 16, CHAIN) * mask[None]).reshape(count, CHAIN)


def stack_forward(stack, parts, places, offsets):
    count = parts[1].shape[0]

    def stage(chain, lanes):
        masks = tap_masks(places, chain, offsets)

        def step(number, rows):
            piece = shifted(parts, rows, chain, offsets[number], masks[number])
            stack[number * count + rows.start : number * count + rows.stop, lanes] = piece

        return [functools.partial(step, number, rows) for number in range(len(offsets)) for rows in chunks(count)]

    return stage


def stack_backward(stack, parts, places, offsets):
    count = parts[1].shape[0]
    half = count // 2
    part = stack.shape[0] // 2

    def stage(chain, lanes):
        masks = tap_masks(places, chain, offsets)

        def step(number, rows):
            piece = shifted(parts, rows, chain, offsets[number], masks[number])
            for which in range(2):
                first = max(rows.start, which * half)
                last = min(rows.stop, (which + 1) * half)
                if first < last:
                    at = which * part + number * half + first - which * half
                    stack[at : at + last - first, lanes] = piece[first - rows.start : last - rows.start, :]

        return [functools.partial(step, number, rows) for number in range(len(offsets)) for rows in chunks(count)]

    return stage


class Totals:
    def __init__(self):
        self.sums = {}

    def add(self, name, value):
        value = down_rows(value)
        self.sums[name] = self.sums[name] + value if name in self.sums else value

    def get(self, name):
        return total_rows(self.sums[name])


def inner_norm(values, lanes, gains, first, act_out, hat_out, scale_out, slope_out=None):
    count = values.shape[0]
    totals, stats = Totals(), {}

    def measure(rows):
        value = values[rows, lanes]
        totals.add("one", value)
        totals.add("two", value * value)

    def settle():
        stats["centre"] = totals.get("one") / count
        stats["scale"] = lax.rsqrt(totals.get("two") / count - stats["centre"] * stats["centre"] + EPS)
        scale_out[:, lanes] = stats["scale"]

    def apply(rows):
        hat = (values[rows, lanes] - stats["centre"]) * stats["scale"]
        hat_out[rows, lanes] = hat.astype(hat_out.dtype)
        act, slope = gelu(scaled_by(gains, first, rows, hat))
        act_out[rows, lanes] = act.astype(BF16)
        if slope_out is not None:
            slope_out[rows, lanes] = slope.astype(BF16)

    return [*per_chunk(count, measure), settle, *per_chunk(count, apply)]


def outer_norm(begin, load, reload, count, lanes, gains, act_out, hat_out, scale_out, squares,
               slope_out=None):
    totals, stats = Totals(), {}

    def prepare():
        stats["about"] = begin()

    def measure(rows):
        shifted = load(rows) - stats["about"]
        totals.add("one", shifted)
        totals.add("two", shifted * shifted)

    def settle():
        off = totals.get("one") / count
        spread = totals.get("two") / count - off * off
        stats["centre"] = stats["about"] + off
        stats["scale"] = lax.rsqrt(spread + EPS)
        scale_out[:, lanes] = stats["scale"]
        squares(count * (spread + stats["centre"] * stats["centre"]))

    def apply(rows):
        hat = (reload(rows) - stats["centre"]) * stats["scale"]
        hat_out[rows, lanes] = hat.astype(BF16)
        act, slope = gelu(scaled_by(gains, 0, rows, hat))
        act_out[rows, lanes] = act.astype(BF16)
        if slope_out is not None:
            slope_out[rows, lanes] = slope.astype(BF16)

    return [prepare, *per_chunk(count, measure), settle, *per_chunk(count, apply)]


def norm_back(grad, lanes, hat_of, scale_of, gains, first, sums, store, slope_of=None, act_out=None):
    count = grad.shape[0]
    totals, stats = Totals(), {}

    def measure(rows):
        hat = hat_of(rows)
        if slope_of is None:
            act, slope = gelu(scaled_by(gains, first, rows, hat))
            if act_out is not None:
                act_out[rows, lanes] = act.astype(BF16)
        else:
            slope = slope_of(rows)
        gain = wide(gains[first, rows, :])
        before = grad[rows, lanes] * slope
        along = before * hat
        sums[0, rows, :] += fold(along)
        sums[1, rows, :] += fold(before)
        scaled = before * gain
        grad[rows, lanes] = scaled
        totals.add("one", scaled)
        totals.add("two", along * gain)

    def settle():
        scale = scale_of()
        stats["scale"] = scale
        stats["base"] = scale * (totals.get("one") / count)
        stats["tilt"] = scale * (totals.get("two") / count)

    def apply(rows):
        value = grad[rows, lanes] * stats["scale"] - stats["base"]
        store(rows, value - hat_of(rows) * stats["tilt"])

    return [*per_chunk(count, measure), settle, *per_chunk(count, apply)]


def kept_back(grad, lanes, hats, scales, gains, sums, store, slopes=None, **more):
    if slopes is not None:
        more["slope_of"] = lambda rows: slopes[rows, lanes].astype(F32)
    return norm_back(grad, lanes, lambda rows: hats[rows, lanes].astype(F32), lambda: scales[:, lanes], gains, 0,
                     sums, store, **more)


def dot(left, right):
    return jnp.dot(left, right, preferred_element_type=F32)


def dot_nt(left, right):
    return lax.dot_general(left, right, (((1,), (1,)), ((), ())), preferred_element_type=F32)


def multiply(target, left, right):
    rows, depth = left.shape

    def stage(chain, lanes):
        def deep(start):
            stop = min(start + 2 * CHAIN, depth)
            part = dot(left[:, start:stop], right[start:stop, lanes])
            target[:, lanes] = part if start == 0 else target[:, lanes] + part

        def high(start):
            stop = min(start + 400, rows)
            target[start:stop, lanes] = dot(left[start:stop, :], right[:, lanes])

        if depth > 2 * CHAIN:
            return [functools.partial(deep, start) for start in range(0, depth, 2 * CHAIN)]
        return [functools.partial(high, start) for start in range(0, rows, 400)]

    return stage


def add_product(target, left, right, lanes=slice(None)):
    count = 400 if left.shape[0] % 400 == 0 else 512

    def step(start):
        stop = min(start + count, left.shape[0])
        target[start:stop, :] += dot_nt(left[start:stop, lanes], right[:, lanes])

    return [functools.partial(step, start) for start in range(0, left.shape[0], count)]


def in_order(core, mine, other, axis):
    return jnp.where(
        core == 0, jnp.concatenate([mine, other], axis=axis), jnp.concatenate([other, mine], axis=axis)
    )


def spread_outer(gain, bias, gains):
    for place, vector in enumerate((gain, bias)):
        column = vector[...].astype(F32).reshape(1, -1).T
        gains[place, :, :] = jnp.broadcast_to(BEND * column, gains.shape[1:])


def spread_inner(core, small, small_other, numbers, gains):
    columns = in_order(core, small[...].astype(F32).T, small_other[...].astype(F32).T, 0)
    for place, number in enumerate(numbers):
        gains[place, :, :] = jnp.broadcast_to(BEND * columns[:, number : number + 1], gains.shape[1:])


def joined(core, mine, other, target):
    target[...] = in_order(core, mine[...], other[...], 0)


def joined_t(core, mine, other, target):
    target[...] = in_order(core, mine[...], other[...], 0).T


def conv_forward_weight(core, mine, other, target):
    taps, count, _ = mine.shape
    for tap in range(taps):
        target[:, tap * count : (tap + 1) * count] = in_order(core, mine[tap].T, other[tap].T, 0)


def conv_backward_weight(core, mine, other, target):
    taps, _, half = mine.shape
    part = target.shape[1] // 2
    target[...] = jnp.zeros(target.shape, target.dtype)
    for tap in range(taps):
        one, two = mine[tap], other[tap]
        target[:, tap * half : (tap + 1) * half] = jnp.where(core == 0, one, two)
        target[:, part + tap * half : part + (tap + 1) * half] = jnp.where(core == 0, two, one)


def pack_conv(acc, core, mine, other, base):
    both, count = acc.shape
    slabs = both // 2 // LANES
    for slab in range(slabs):
        one = acc[slab * LANES : (slab + 1) * LANES, :].astype(BF16).T
        two = acc[both // 2 + slab * LANES : both // 2 + (slab + 1) * LANES, :].astype(BF16).T
        at = base + slab * count
        mine[at : at + count, :] = jnp.where(core == 0, one, two)
        other[at : at + count, :] = jnp.where(core == 0, two, one)


def pack_wide(acc, core, mine, other, base):
    width, count = acc.shape
    half = count // 2
    for slab in range(up_to(width, LANES) // LANES):
        some = min(LANES, width - slab * LANES)
        value = acc[slab * LANES : slab * LANES + some, :]
        if some < LANES:
            value = jnp.concatenate([value, jnp.zeros((LANES - some, count), F32)], axis=0)
        value = value.astype(BF16).T
        one, two = value[:half, :], value[half:, :]
        at = base + slab * half
        mine[at : at + half, :] = jnp.where(core == 0, one, two)
        other[at : at + half, :] = jnp.where(core == 0, two, one)


def wide_rows(half, width):
    return up_to(width, LANES) // LANES * half


def row_form(sums, target):
    for k in range(sums.shape[0]):
        target[k, :, :] = lax.dot_general(
            jnp.full((8, LANES), BEND, F32), sums[k, :, :], (((1,), (1,)), ((), ())),
            precision=lax.Precision.HIGHEST, preferred_element_type=F32,
        )


def clear(step, *refs):
    @pl.when(step == 0)
    def _():
        for ref in refs:
            ref[...] = jnp.zeros(ref.shape, ref.dtype)


def row_list(line):
    width = line.shape[1]
    line = jnp.concatenate([line, jnp.zeros((1, up_to(width, LANES) - width), F32)], axis=1)
    return [line[:, at : at + LANES] for at in range(0, line.shape[1], LANES)]


def rows_together(rows, multiple):
    pad = up_to(len(rows), multiple) - len(rows)
    return jnp.concatenate(rows + [jnp.zeros((pad, LANES), F32)] * bool(pad), axis=0)


def small_rows(core, inner):
    mine, other = [], []
    for ref in inner:
        for k in range(2):
            line = ref[k, 0:1, :]
            half = line.shape[1] // 2
            for one, two in zip(row_list(line[:, :half]), row_list(line[:, half:])):
                mine.append(jnp.where(core == 0, one, two))
                other.append(jnp.where(core == 0, two, one))
    return rows_together(mine, 16), rows_together(other, 16)


def small_count(half):
    return up_to(8 * (up_to(half, LANES) // LANES), 16)


def moment_row(moments, count):
    lane = lax.broadcasted_iota(jnp.int32, (1, LANES), 1)
    line = jnp.where(lane == len(moments), count, jnp.zeros((1, LANES), F32))
    for k, row in enumerate(moments):
        line = line + jnp.where(lane == k, jnp.sum(row, axis=1, keepdims=True), 0.0)
    return line


def keep_edge(core, step, tiles, source, target):
    @pl.when(step == jnp.where(core == 0, tiles - 1, 0))
    def _():
        target[...] = jnp.where(core == 0, source[:, TILE - LANES :], source[:, :LANES])


def kernel_one(tiles, lengths, padding, x, norm_gain, norm_bias, small, small_other, down, down_other, a_out,
               xhat_out, xscale_out, b_out, hat_out, scale_out, slope_out, edge_out, moments, g_outer, g_inner, down_t, hidden):
    step = pl.program_id(0)
    places = Places(lengths, padding, tiles * TILE, step)
    core = places.core

    @pl.when(step == 0)
    def _():
        spread_outer(norm_gain, norm_bias, g_outer)
        spread_inner(core, small, small_other, (0, 2), g_inner)
        joined(core, down, down_other, down_t)

    clear(step, moments)

    def norm(chain, lanes):
        def load(rows):
            return x[rows, lanes].astype(F32)

        def squares(value):
            moments[0:1, :] += jnp.where(places.valid(chain), value, 0.0)

        return outer_norm(lambda: load(slice(0, 16))[0:1], load, load, x.shape[0], lanes, g_outer, a_out,
                          xhat_out, xscale_out, squares)

    def inner(chain, lanes):
        return inner_norm(hidden, lanes, g_inner, 0, b_out, hat_out, scale_out, slope_out)

    in_chains(norm, multiply(hidden, down_t, a_out), inner)
    keep_edge(core, step, tiles, b_out, edge_out)


def choose_edges(step, tiles, halo, left, right, edge_left, edge_right):
    if left is not None:
        edge_left[...] = jnp.where(step == 0, halo[...], left[...])
    if right is not None:
        edge_right[...] = jnp.where(step == tiles - 1, halo[...], right[...])


def kernel_two(tiles, lengths, padding, b_left, b_mid, b_right, x, b_halo, norm_gain, norm_bias, small,
               small_other, conv, conv_other, up, up_other, down, down_other, y_out, chat_out, cscale_out, a_out,
               yhat_out, yscale_out, yslope_out, b_out, hat_out, scale_out, slope_out, edge_out, moments, stack, g_outer, g_inner, conv_f, up_t, down_t, mixed, stream,
               edge_left, edge_right, act):
    step = pl.program_id(0)
    places = Places(lengths, padding, tiles * TILE, step)
    core = places.core

    @pl.when(step == 0)
    def _():
        spread_outer(norm_gain, norm_bias, g_outer)
        spread_inner(core, small, small_other, (1, 3, 4, 6), g_inner)
        conv_forward_weight(core, conv, conv_other, conv_f)
        joined_t(core, up, up_other, up_t)
        joined(core, down, down_other, down_t)

    clear(step, moments)
    choose_edges(step, tiles, b_halo, b_left, b_right, edge_left, edge_right)
    width = x.shape[0]
    gather = stack_forward(stack, (edge_left, b_mid, edge_right), places, (-2, -1, 0, 1, 2))

    def second(chain, lanes):
        return inner_norm(mixed, lanes, g_inner, 0, act, chat_out, cscale_out)

    def outer(chain, lanes):
        valid = places.valid(chain)
        totals = Totals()

        def branch_of(rows):
            return jnp.where(valid, stream[rows, lanes], 0.0)

        def begin():
            return branch_of(slice(0, 8))[0:1] + x[0:16, lanes].astype(F32)[0:1]

        def load(rows):
            branch = branch_of(rows)
            value = x[rows, lanes].astype(F32) + branch
            stream[rows, lanes] = value
            y_out[rows, lanes] = value.astype(BF16)
            totals.add("branch", branch * branch)
            return value

        def squares(value):
            moments[0:1, :] += totals.get("branch")
            moments[1:2, :] += jnp.where(valid, value, 0.0)

        return outer_norm(begin, load, lambda rows: stream[rows, lanes], width, lanes, g_outer, a_out,
                          yhat_out, yscale_out, squares, yslope_out)

    def first(chain, lanes):
        return inner_norm(mixed, lanes, g_inner, 2, b_out, hat_out, scale_out, slope_out)

    in_chains(gather, multiply(mixed, conv_f, stack), second, multiply(stream, up_t, act), outer,
              multiply(mixed, down_t, a_out), first)
    keep_edge(core, step, tiles, b_out, edge_out)


def kernel_three(tiles, lengths, padding, b_left, b_mid, t, b_halo, small, small_other, conv, conv_other, up,
                 up_other, act, dc_out, edge_out, mine, other, sums_out, stack, g_inner, conv_f, up_all, sums, mixed,
                 turned, hats, slopes, scales, du, edge_left, up_grad):
    step = pl.program_id(0)
    places = Places(lengths, padding, tiles * TILE, step)
    core = places.core

    @pl.when(step == 0)
    def _():
        spread_inner(core, small, small_other, (5, 7), g_inner)
        conv_forward_weight(core, conv, conv_other, conv_f)
        joined(core, up, up_other, up_all)

    clear(step, sums, up_grad)
    choose_edges(step, tiles, b_halo, b_left, None, edge_left, None)
    gather = stack_forward(stack, (edge_left, b_mid, None), places, (-2, -1, 0))

    def turn(chain, lanes):
        keep = jnp.where(places.valid(chain), 1.0, 0.0)
        keep = jnp.broadcast_to(keep, (16, CHAIN)).astype(BF16)

        def step(rows):
            piece = t[rows, lanes].reshape(-1, 16, CHAIN) * keep[None]
            du[rows, lanes] = piece.reshape(-1, CHAIN)

        return per_chunk(t.shape[0], step)

    def second(chain, lanes):
        return inner_norm(mixed, lanes, g_inner, 0, act, hats, scales, slopes)

    def back(chain, lanes):
        def store(rows, v):
            dc_out[rows, lanes] = v.astype(BF16)

        return kept_back(turned, lanes, hats, scales, g_inner, sums, store, slopes)

    one, two = ((chain, chain_lanes(chain)) for chain in range(CHAINS))
    convolve, lower = multiply(mixed, conv_f, stack), multiply(turned, up_all, du)
    together(gather(*one) + turn(*one))
    together(convolve(*one) + lower(*one), gather(*two) + turn(*two))
    together(convolve(*two) + lower(*two), second(*one) + back(*one))
    together(second(*two))
    together(add_product(up_grad, du, act), back(*two))
    keep_edge(core, step, tiles, dc_out, edge_out)

    @pl.when(step == tiles - 1)
    def _():
        row_form(sums, sums_out)
        pack_wide(up_grad, core, mine, other, 0)


def kernel_last(tiles, lengths, padding, e_mid, y, up, up_other, y_out, moments, up_t, stream):
    step = pl.program_id(0)
    places = Places(lengths, padding, tiles * TILE, step)

    @pl.when(step == 0)
    def _():
        joined_t(places.core, up, up_other, up_t)

    clear(step, moments)

    def finish(chain, lanes):
        valid = places.valid(chain)
        totals = Totals()

        def step(rows):
            branch = jnp.where(valid, stream[rows, lanes], 0.0)
            value = y[rows, lanes].astype(F32) + branch
            y_out[rows, lanes] = value.astype(BF16)
            totals.add("branch", branch * branch)
            totals.add("value", value * value)

        def settle():
            moments[0:1, :] += totals.get("branch")
            moments[1:2, :] += jnp.where(valid, totals.get("value"), 0.0)

        return [*per_chunk(y.shape[0], step), settle]

    in_chains(multiply(stream, up_t, e_mid), finish)


def back_conv(gather, conv_b, stack, hats, scales, slopes, g_inner, sums, mixed, dh, b_mid, a_mid, conv_grad, down_grad):
    def first(chain, lanes):
        def store(rows, v):
            dh[rows, lanes] = v.astype(BF16)

        return kept_back(mixed, lanes, hats, scales, g_inner, sums, store, slopes)

    one, two = ((chain, chain_lanes(chain)) for chain in range(CHAINS))
    convolve = multiply(mixed, conv_b, stack)
    together(gather(*one))
    together(convolve(*one), gather(*two))
    together(convolve(*two), first(*one))
    together(add_product(conv_grad, stack, b_mid), first(*two))
    together(add_product(down_grad, a_mid, dh))


def kernel_four(tiles, lengths, padding, dc_mid, dc_right, b_mid, hats, scales, slopes, a_mid, yhats, yscales, yslopes, t,
                chats, cscales, dc_halo, norm_gain, norm_bias, small, small_other, conv, conv_other, down, down_other, up,
                up_other, mine_up, other_up, g_out, dc_out, edge_out, mine, other, outer_out, inner_out, prev_out,
                stack, g_outer, g_inner, g_prev, conv_b, down_all, up_all, sums_outer, sums_inner, sums_prev,
                conv_grad, down_grad, up_grad, mixed, lower_mixed, wide_grad, dh, du, act, edge_right):
    step = pl.program_id(0)
    places = Places(lengths, padding, tiles * TILE, step)
    core = places.core

    @pl.when(step == 0)
    def _():
        spread_outer(norm_gain, norm_bias, g_outer)
        spread_inner(core, small, small_other, (4, 6), g_inner)
        spread_inner(core, small, small_other, (1, 3), g_prev)
        conv_backward_weight(core, conv, conv_other, conv_b)
        joined_t(core, down, down_other, down_all)
        joined(core, up, up_other, up_all)

    clear(step, stack, conv_grad, down_grad, up_grad, sums_outer, sums_inner, sums_prev)
    choose_edges(step, tiles, dc_halo, None, dc_right, None, edge_right)
    gather = stack_backward(stack, (None, dc_mid, edge_right), places, (2, 1, 0))

    def first(chain, lanes):
        def store(rows, v):
            dh[rows, lanes] = v.astype(BF16)

        return kept_back(mixed, lanes, hats, scales, g_inner, sums_inner, store, slopes)

    def outer(chain, lanes):
        keep = jnp.where(places.valid(chain), 1.0, 0.0)
        keep = jnp.broadcast_to(keep, (16, CHAIN)).astype(BF16)

        def store(rows, v):
            grad = (v + t[rows, lanes].astype(F32)).astype(BF16)
            g_out[rows, lanes] = grad
            du[rows, lanes] = (grad.reshape(-1, 16, CHAIN) * keep[None]).reshape(-1, CHAIN)

        return kept_back(wide_grad, lanes, yhats, yscales, g_outer, sums_outer, store, yslopes)

    def second(chain, lanes):
        def store(rows, v):
            dc_out[rows, lanes] = v.astype(BF16)

        return kept_back(lower_mixed, lanes, chats, cscales, g_prev, sums_prev, store, act_out=act)

    one, two = ((chain, chain_lanes(chain)) for chain in range(CHAINS))
    convolve, lift = multiply(mixed, conv_b, stack), multiply(wide_grad, down_all, dh)
    lower = multiply(lower_mixed, up_all, du)
    products = add_product(conv_grad, stack, b_mid)
    some = len(products) // 2
    together(gather(*one))
    together(convolve(*one), gather(*two))
    together(convolve(*two), first(*one))
    together(lift(*one), first(*two))
    together(lift(*two) + products[:some], outer(*one))
    together(lower(*one) + products[some:], outer(*two))
    together(lower(*two) + add_product(down_grad, a_mid, dh), second(*one))
    together(add_product(up_grad, du, act, one[1]), second(*two))
    together(add_product(up_grad, du, act, two[1]))
    keep_edge(core, step, tiles, dc_out, edge_out)

    @pl.when(step == tiles - 1)
    def _():
        row_form(sums_outer, outer_out)
        row_form(sums_inner, inner_out)
        row_form(sums_prev, prev_out)
        at = pack(core, mine, other, conv_grad, (down_grad, up_grad))
        rows = mine_up.shape[0]
        mine[at : at + rows, :] = mine_up[...]
        other[at : at + rows, :] = other_up[...]
        pad_payload(mine, other, at + rows)


def pack(core, mine, other, conv_grad, wides):
    both, count = conv_grad.shape
    pack_conv(conv_grad, core, mine, other, 0)
    at = count * (both // 2 // LANES)
    for ref in wides:
        pack_wide(ref, core, mine, other, at)
        at += wide_rows(count // 2, ref.shape[0])
    return at


def pad_payload(mine, other, at):
    if at < mine.shape[0]:
        for target in (mine, other):
            target[at:, :] = jnp.zeros((mine.shape[0] - at, LANES), BF16)


def kernel_six(tiles, lengths, padding, dc_left, dc_mid, dc_right, b_mid, hats, scales, slopes, a_mid, dc_halo, small, small_other, conv, conv_other, inner_two, prev_one, prev_two, dh_out,
               mine, other, stack, g_inner, conv_b, sums, conv_grad, down_grad, mixed, edge_left,
               edge_right, inner_one):
    step = pl.program_id(0)
    places = Places(lengths, padding, tiles * TILE, step)
    core = places.core

    @pl.when(step == 0)
    def _():
        spread_inner(core, small, small_other, (0, 2), g_inner)
        conv_backward_weight(core, conv, conv_other, conv_b)

    clear(step, stack, conv_grad, down_grad, sums)
    choose_edges(step, tiles, dc_halo, dc_left, dc_right, edge_left, edge_right)
    gather = stack_backward(stack, (edge_left, dc_mid, edge_right), places, (2, 1, 0, -1, -2))
    back_conv(gather, conv_b, stack, hats, scales, slopes, g_inner, sums, mixed, dh_out, b_mid, a_mid, conv_grad, down_grad)

    @pl.when(step == tiles - 1)
    def _():
        row_form(sums, inner_one)
        extra = small_rows(core, (inner_one, prev_one, inner_two, prev_two))
        at = pack(core, mine, other, conv_grad, (down_grad,))
        for target, value in zip((mine, other), extra):
            target[at : at + value.shape[0], :] = value.astype(BF16)
        pad_payload(mine, other, at + extra[0].shape[0])


def outer_first_tile(dh, xhats, xscales, g, down_all, g_outer, sums, dx_out, wide_grad):
    def outer(chain, lanes):
        def store(rows, v):
            dx_out[rows, lanes] = v + g[rows, lanes].astype(F32)

        return kept_back(wide_grad, lanes, xhats, xscales, g_outer, sums, store)

    in_chains(multiply(wide_grad, down_all, dh), outer)


def kernel_seven(tiles, lengths, padding, dh, xhats, xscales, g, norm_gain, norm_bias, down, down_other, dx_out,
                 sums, g_outer, down_all, wide_grad):
    step = pl.program_id(0)
    core = lax.axis_index("ch")

    @pl.when(step == 0)
    def _():
        spread_outer(norm_gain, norm_bias, g_outer)
        joined_t(core, down, down_other, down_all)

    clear(step, sums)
    outer_first_tile(dh, xhats, xscales, g, down_all, g_outer, sums, dx_out, wide_grad)


def kernel_eight(tiles, lengths, padding, dh, xhats, xscales, g, dx_begun, norm_gain, norm_bias, down, down_other,
                 sums_begun, moments_one, moments_two, moments_three, outer_two, dx_out, rows_out, g_outer,
                 down_all, sums, wide_grad, outer_one):
    step = pl.program_id(0)
    places = Places(lengths, padding, tiles * TILE, step)
    core = places.core

    @pl.when(step == 0)
    def _():
        spread_outer(norm_gain, norm_bias, g_outer)
        joined_t(core, down, down_other, down_all)
        sums[...] = sums_begun[...]

    outer_first_tile(dh, xhats, xscales, g, down_all, g_outer, sums, dx_out, wide_grad)

    @pl.when(step == pl.num_programs(0) - 1)
    def _():
        row_form(sums, outer_one)
        rows = [moments_one[0:1, :], moments_two[0:1, :], moments_two[1:2, :], moments_three[0:1, :],
                moments_three[1:2, :]]
        lines = [row for ref in (outer_one, outer_two) for k in range(2) for row in row_list(ref[k, 0:1, :])]
        rows_out[...] = rows_together(lines + [moment_row(rows, places.tokens())], 8)


def split_three(v):
    one = v.astype(BF16)
    rest = v - one.astype(F32)
    two = rest.astype(BF16)
    return one, two, (rest - two.astype(F32)).astype(BF16)


def sum_of_three(parts):
    one, two, three = (part.astype(F32) for part in parts)
    return one + (two + three)


def write_lines(out, at, lines):
    for part in split_three(lines):
        out[at : at + part.shape[0], :] = part
        at += part.shape[0]


def read_lines(ref, count):
    start = ref.shape[0] - 3 * count
    return sum_of_three([ref[start + k * count : start + (k + 1) * count, :] for k in range(3)])


def all_lines(refs, count):
    values = [read_lines(ref, count) for ref in refs]
    while len(values) > 1:
        values = [values[k] + values[k + 1] for k in range(0, len(values), 2)]
    return values[0]


def finish_kernel(own, *refs):
    *arrived, lines, lines_other, out = refs
    total = own[...]
    for ref in arrived:
        total = total + ref[...].astype(F32)
    rows = total.shape[0]
    out[:rows, :] = total.astype(BF16)
    write_lines(out, rows, lines[...] + lines_other[...])


def place_kernel(number, count, scal, *refs):
    *parts, out = refs
    rows = parts[0].shape[0] - 3 * count
    for turn, ref in enumerate(parts):
        out[pl.ds(pl.multiple_of((scal[number] ^ turn) * rows, 16), rows), :] = ref[:rows, :]
    if count:
        write_lines(out, len(parts) * rows, all_lines(parts, count))


def unpack(rows_of, conv_out, wide_outs, inner_outs):
    taps, count, half = conv_out.shape
    slabs = up_to(taps * half, LANES) // LANES
    for start in range(0, count, 80):
        rows = min(80, count - start)
        line = jnp.concatenate([rows_of(k * count + start, rows) for k in range(slabs)], axis=1)
        for tap in range(taps):
            conv_out[tap, start : start + rows, :] = line[:, tap * half : (tap + 1) * half]
    base = slabs * count
    for out in wide_outs:
        width = out.shape[1]
        for slab in range(up_to(width, LANES) // LANES):
            lanes = slice(slab * LANES, min(width, (slab + 1) * LANES))
            value = rows_of(base + slab * half, half)
            out[:, lanes] = value[:, : lanes.stop - lanes.start]
        base += wide_rows(half, width)
    if not inner_outs:
        return
    table = rows_of(base, small_count(half))
    at = 0
    count = up_to(half, LANES) // LANES
    for number in range(8):
        line = jnp.concatenate([table[at + k : at + k + 1, :] for k in range(count)], axis=1)
        norm, what = number // 2, number % 2
        inner_outs[2 * (norm // 2) + what][norm % 2 : norm % 2 + 1, :] = line[:, :half]
        at += count


def unpack_kernel(number, wides, count, scal, one, two, conv_out, *rest):
    flat = rest[-1]
    rows = one.shape[0] - 3 * count
    for turn, ref in enumerate((one, two)):
        flat[pl.ds(pl.multiple_of((scal[number] ^ turn) * rows, 16), rows), :] = ref[:rows, :]
    outs = rest[:-1]
    if count:
        *outs, moments_out = outs
        outs, vectors = outs[:-4], outs[-4:]
        lines = all_lines((one, two), count)
        width = vectors[0].shape[0]
        at = 0
        for vector in vectors:
            for start in range(0, width, LANES):
                some = min(LANES, width - start)
                vector[start : start + some] = lines[at : at + 1, :some].reshape(some)
                at += 1
        totals = lines[at : at + 1, :]
        amount = moments_out.shape[0]
        means = totals[:, :amount] / (totals[:, amount : amount + 1] * width)
        moments_out[...] = jnp.sqrt(means).reshape(amount)
    unpack(lambda at, some: flat[at : at + some, :].astype(F32), conv_out, outs[:wides], outs[wides:])


def swap(values):
    return lax.ppermute(values, "ch", [(0, 1), (1, 0)])


def local(inputs, cotangent, doc_lengths, trailing_pad_tokens, first_norm_gain, first_norm_bias, first_down,
          first_inner_gain, first_inner_bias, first_conv, first_up, second_norm_gain, second_norm_bias,
          second_down, second_inner_gain, second_inner_bias, second_conv, second_up):
    own, width = inputs.shape
    half = first_down.shape[1]
    inner = 2 * half
    tiles = own // TILE
    x = inputs.T
    t = cotangent.T

    small = jnp.concatenate([first_inner_gain, first_inner_bias, second_inner_gain, second_inner_bias], axis=0)
    smalls = (small, swap(small))
    vector_rows = up_to(width, LANES) // LANES
    first_vectors = (first_norm_gain, first_norm_bias)
    second_vectors = (second_norm_gain, second_norm_bias)

    def with_other(v):
        return v, swap(v)

    down_1 = with_other(first_down.T)
    conv_1 = with_other(first_conv)
    up_1 = with_other(first_up)
    down_2 = with_other(second_down.T)
    conv_2 = with_other(second_conv)
    up_2 = with_other(second_up)

    last_lane = own // LANES - 1
    ratio = TILE // LANES

    def tile_of(count, first=0):
        return pl.BlockSpec((count, TILE), lambda i, *s: (0, i + first))

    def left_of(count):
        return pl.BlockSpec((count, LANES), lambda i, *s: (0, jnp.maximum(ratio * i - 1, 0)))

    def right_of(count):
        return pl.BlockSpec((count, LANES), lambda i, *s: (0, jnp.minimum(ratio * i + ratio, last_lane)))

    def whole(*shape):
        zeros = (0,) * len(shape)
        return pl.BlockSpec(shape, lambda i, *s: zeros)

    def whole_of(v):
        return whole(*v.shape)

    anywhere = pl.BlockSpec(memory_space=pl.ANY)

    def shape(*dims, dtype=F32):
        return jax.ShapeDtypeStruct(dims, dtype)

    limits = {
        "norm_down": 16,
        "conv_up_norm_down": 36,
        "conv_turn": 22,
        "back_second": 47,
        "back_conv_first": 32,
        "up_second": 12,
        "back_outer_early": 16,
        "back_outer_late": 18,
        "places": 6,
        "finish": 6,
        "unpack_second": 14,
        "unpack_first": 14,
    }

    def params(name):
        return pltpu.CompilerParams(vmem_limit_bytes=limits[name] * 1024 * 1024)


    def call(kernel, name, in_specs, outs, scratch, *args, first=0, steps=tiles, aliases={}):
        specs = list(in_specs) + [whole_of(v) for v in args[len(in_specs):]]
        out_specs = [tile_of(o[0], first) if isinstance(o, tuple) else whole_of(o) for o in outs]
        out_shape = []
        for o in outs:
            if isinstance(o, tuple):
                o = pltpu.HBM((o[0], own), o[1]) if len(o) == 3 else shape(o[0], own, dtype=o[1])
            out_shape.append(o)
        return pl.pallas_call(
            functools.partial(kernel, tiles),
            grid_spec=pltpu.PrefetchScalarGridSpec(
                num_scalar_prefetch=2,
                grid=(steps,),
                in_specs=specs,
                out_specs=out_specs,
                scratch_shapes=scratch,
            ),
            out_shape=out_shape,
            input_output_aliases=aliases,
            compiler_params=params(name),
            cost_estimate=pl.CostEstimate(flops=15 * 1_150_000_000, bytes_accessed=0, transcendentals=0),
            name=name,
        )(doc_lengths, trailing_pad_tokens, *args)

    def stay(*arrays):
        return [pltpu.with_memory_space_constraint(v, pltpu.HBM) for v in arrays]

    def vm(*dims, dtype=F32):
        return pltpu.VMEM(dims, dtype)

    def tile(count, dtype=F32):
        return pltpu.VMEM((count, TILE), dtype)

    outer_gains = vm(2, width, LANES)
    inner_gains = vm(2, inner, LANES)
    edge = vm(inner, LANES, dtype=BF16)
    edge_shape = shape(inner, LANES, dtype=BF16)
    moment_shape = shape(8, CHAIN)
    taps_1, taps_2 = first_conv.shape[0], second_conv.shape[0]
    part_1, part_2 = up_to(taps_1 * half, LANES), up_to(taps_2 * half, LANES)
    away = True
    normed = [(inner, BF16, away), (1, F32)]
    kept = [(width, BF16, away), (width, BF16, away), (1, F32)]
    inner_slope, wide_slope = (inner, BF16, away), (width, BF16, away)

    a1, xhat, xscale, b1, hat1, scale1, slope1, b1_edge, moments_one = call(
        kernel_one, "norm_down", [tile_of(width)],
        [*kept, (inner, BF16), *normed, inner_slope, edge_shape, moment_shape],
        [outer_gains, inner_gains, vm(inner, width, dtype=BF16), tile(inner)],
        *stay(x), *first_vectors, *smalls, *down_1,
    )

    y1, chat1, cscale1, a2, yhat, yscale, yslope, b2, hat2, scale2, slope2, b2_edge, moments_two = call(
        kernel_two, "conv_up_norm_down",         [left_of(inner), tile_of(inner), right_of(inner), tile_of(width)],
        [(width, BF16, away), *normed, *kept, wide_slope, (inner, BF16), *normed, inner_slope, edge_shape,
         moment_shape],
        [tile(taps_1 * inner, BF16), outer_gains, vm(4, inner, LANES), vm(inner, taps_1 * inner, dtype=BF16),
         vm(width, inner, dtype=BF16), vm(inner, width, dtype=BF16), tile(inner), tile(width), edge, edge,
         tile(inner, BF16)],
        b1, b1, b1, x, swap(b1_edge), *second_vectors, *smalls, *conv_1, *up_1, *down_2,
    )

    pair = wide_rows(half, width)
    gradient_up = [shape(pair, LANES, dtype=BF16)] * 2
    e2, dc2, dc2_edge, mine_up, other_up, sums_c2 = call(
        kernel_three, "conv_turn", [left_of(inner), tile_of(inner), tile_of(width)],
        [(inner, BF16, away), (inner, BF16), edge_shape, *gradient_up, shape(2, 8, inner)],
        [tile(taps_2 * inner, BF16), inner_gains, vm(inner, taps_2 * inner, dtype=BF16),
         vm(inner, width, dtype=BF16), vm(2, inner, LANES), tile(inner), tile(inner), tile(inner),
         tile(inner, BF16), tile(1), tile(width, BF16), edge, vm(width, inner)],
        b2, b2, t, swap(b2_edge), *smalls, *conv_2, *up_2,
    )

    row_count = lax.axis_size("rows")
    inner_in = [tile_of(inner), tile_of(1)]
    wide_in = [tile_of(width), tile_of(1)]
    rows_two = up_to(inner * (part_2 // LANES) + 3 * pair, 16 * row_count)
    rows_one = up_to(inner * (part_1 // LANES) + pair + small_count(half), 16 * row_count)
    g1, dc1, dc1_edge, mine_two, other_two, sums_o2, sums_h2, sums_c1 = call(
        kernel_four, "back_second",
        [tile_of(inner), right_of(inner), tile_of(inner), *inner_in, tile_of(inner), tile_of(width), *wide_in,
         tile_of(width), tile_of(width), *inner_in],
        [(width, BF16, away), (inner, BF16), edge_shape, shape(rows_two, LANES, dtype=BF16),
         shape(rows_two, LANES, dtype=BF16), shape(2, 8, width), shape(2, 8, inner), shape(2, 8, inner)],
        [tile(2 * part_2, BF16), outer_gains, inner_gains, inner_gains, vm(inner, 2 * part_2, dtype=BF16),
         vm(width, inner, dtype=BF16), vm(inner, width, dtype=BF16), vm(2, width, LANES), vm(2, inner, LANES),
         vm(2, inner, LANES), vm(2 * part_2, inner), vm(width, inner), vm(width, inner), tile(inner),
         tile(inner), tile(width), tile(inner, BF16), tile(width, BF16), tile(inner, BF16), edge],
        dc2, dc2, b2, hat2, scale2, slope2, a2, yhat, yscale, yslope, t, chat1, cscale1, swap(dc2_edge), *second_vectors, *smalls,
        *conv_2, *down_2, *up_1, mine_up, other_up,
    )

    row_index = lax.axis_index("rows")
    core = lax.axis_index("ch")
    above = 0
    while 4 ** (above + 1) < row_count:
        above += 1
    assert 4 ** (above + 1) == row_count
    low, high = (row_index >> core) & 1, (row_index >> (1 - core)) & 1
    digits = jnp.stack(
        [2 * high + low, high, low] + [(row_index >> (2 * k + 2)) & 3 for k in range(above)]
    ).astype(jnp.int32)
    ALL, HIGH, LOW, ABOVE = 0, 1, 2, 3

    def radix(level):
        return 2 if level in (HIGH, LOW) else 4

    def flip(level, turn, c):
        if level >= ABOVE:
            return turn << (2 * (level - ABOVE) + 2)
        low_bit, high_bit = 1 << c, 1 << (1 - c)
        if level == LOW:
            return low_bit
        if level == HIGH:
            return high_bit
        return low_bit * (turn & 1) + high_bit * (turn >> 1)

    def send(v, level, turn):
        pairs = [(2 * r + c, 2 * (r ^ flip(level, turn, c)) + c) for r in range(row_count) for c in range(2)]
        return lax.ppermute(v, ("rows", "ch"), pairs)

    def small_call(kernel, name, out_shape, *args, scratch=()):
        return pl.pallas_call(
            kernel,
            grid_spec=pltpu.PrefetchScalarGridSpec(
                num_scalar_prefetch=1, grid=(1,), in_specs=[whole_of(v) for v in args],
                out_specs=jax.tree.map(whole_of, out_shape), scratch_shapes=list(scratch),
            ),
            out_shape=out_shape,
            compiler_params=params(name),
            name=name,
        )(digits, *args)

    z_levels = [ABOVE + k for k in range(above)]

    class Sum:
        def __init__(self, mine, other, levels):
            self.own, self.arrived = mine, [other]
            self.down, self.up = list(levels), [HIGH, LOW, *z_levels]

        def part(self):
            level = self.down[0]
            turns = radix(level)
            parts = [v.reshape(turns, -1, LANES) for v in (self.own, *self.arrived)]

            def share(turn):
                picked = [lax.dynamic_index_in_dim(v, digits[level] ^ turn, 0, False) for v in parts]
                return sum(v.astype(F32) for v in picked)

            self.own, *self.sends = [share(turn) for turn in range(turns)]
            self.sends = [v.astype(BF16) for v in self.sends]

        def go(self):
            level = self.down.pop(0)
            self.arrived = [send(v, level, turn + 1) for turn, v in enumerate(self.sends)]

        def finish(self, lines=None):
            self.lines = 0
            if lines is None:
                self.own = (self.own + sum(v.astype(F32) for v in self.arrived)).astype(BF16)
                return
            self.lines = lines.shape[0]
            self.own = pl.pallas_call(
                finish_kernel, out_shape=shape(self.own.shape[0] + 3 * self.lines, LANES, dtype=BF16),
                compiler_params=params("finish"), name="finish",
            )(self.own, *self.arrived, lines, swap(lines))

        def spread(self):
            self.level = self.up.pop()
            self.parts = [self.own] + [send(self.own, self.level, turn) for turn in range(1, radix(self.level))]

        def place(self):
            extra, turns = 3 * self.lines, len(self.parts)
            rows = turns * (self.own.shape[0] - extra) + extra
            self.own = small_call(
                functools.partial(place_kernel, self.level, self.lines), "places", shape(rows, LANES, dtype=BF16),
                *self.parts,
            )

    barrier = lax.optimization_barrier
    sum_two = Sum(mine_two, swap(other_two), [ALL, *z_levels])
    sum_two.part()
    dc1, *sum_two.sends = barrier((dc1, *sum_two.sends))
    sum_two.go()

    dh1, mine_one, other_one = call(
        kernel_six, "back_conv_first",
        [left_of(inner), tile_of(inner), right_of(inner), tile_of(inner), *inner_in, tile_of(inner), tile_of(width)],
        [(inner, BF16), shape(rows_one, LANES, dtype=BF16), shape(rows_one, LANES, dtype=BF16)],
        [tile(2 * part_1, BF16), inner_gains, vm(inner, 2 * part_1, dtype=BF16), vm(2, inner, LANES),
         vm(2 * part_1, inner), vm(width, inner), tile(inner), edge, edge, vm(2, 8, inner)],
        dc1, dc1, dc1, *stay(b1, hat1), scale1, *stay(slope1, a1), swap(dc1_edge), *smalls, *conv_1, sums_h2, sums_c1, sums_c2,
    )
    sum_two.part()
    dh1, mine_one, other_one, *sum_two.sends = barrier((dh1, mine_one, other_one, *sum_two.sends))
    sum_two.go()
    sum_one = Sum(mine_one, swap(other_one), [HIGH, LOW, *z_levels])
    sum_one.part()
    dh1, e2, *sum_one.sends = barrier((dh1, e2, *sum_one.sends))
    sum_one.go()

    y2, moments_three = call(
        kernel_last, "up_second", [tile_of(inner), tile_of(width)],
        [(width, BF16, away), moment_shape], [vm(width, inner, dtype=BF16), tile(width)],
        *stay(e2, y1), *up_2,
    )
    moments_three, *sum_two.arrived = barrier((moments_three, *sum_two.arrived))
    while sum_two.down:
        sum_two.part()
        sum_two.go()
    sum_two.finish()
    sum_one.part()
    dh1, moments_three, sum_two.own, *sum_one.sends = barrier((dh1, moments_three, sum_two.own, *sum_one.sends))
    sum_one.go()
    sum_two.spread()

    early = tiles // 2
    dx, sums_begun = call(
        kernel_seven, "back_outer_early", [tile_of(inner), *wide_in, tile_of(width)],
        [(width, F32, away), shape(2, width, LANES)],
        [outer_gains, vm(width, inner, dtype=BF16), tile(width)],
        dh1, *stay(xhat), xscale, *stay(g1), *first_vectors, *down_1, steps=early,
    )
    sum_two.place()
    sum_one.part()
    dh1, sums_begun, sum_two.own, *sum_one.sends = barrier((dh1, sums_begun, sum_two.own, *sum_one.sends))
    sum_one.go()
    sum_two.spread()

    line_count = up_to(4 * vector_rows + 1, 8)
    later = [tile_of(rows, early) for rows in (inner, width, 1, width)]
    dx, lines = call(
        kernel_eight, "back_outer_late", [*later, anywhere],
        [(width, F32, away), shape(line_count, LANES)],
        [outer_gains, vm(width, inner, dtype=BF16), vm(2, width, LANES), tile(width), vm(2, 8, width)],
        dh1, *stay(xhat), xscale, *stay(g1), dx, *first_vectors, *down_1, sums_begun, moments_one, moments_two,
        moments_three, sums_o2, first=early, steps=tiles - early, aliases={6: 0},
    )
    while sum_one.down:
        sum_one.part()
        if sum_two.up:
            sum_two.place()
        lines, sum_two.own, *sum_one.sends = barrier((lines, sum_two.own, *sum_one.sends))
        sum_one.go()
        if sum_two.up:
            sum_two.spread()
    sum_two.place()
    lines, sum_two.own = barrier((lines, sum_two.own))
    sum_one.finish(lines)
    sum_one.own, sum_two.own = barrier((sum_one.own, sum_two.own))
    sum_two.spread()
    assert not sum_two.up
    while sum_one.up:
        sum_one.spread()
        if sum_one.up:
            sum_one.place()
        if len(sum_one.up) == 2:
            sum_one.own, *sum_two.parts = barrier((sum_one.own, *sum_two.parts))

    wide_shape = shape(half, width)
    conv_grad2, down_grad2, up_grad1, up_grad2 = small_call(
        functools.partial(unpack_kernel, HIGH, 3, 0), "unpack_second",
        [shape(*second_conv.shape), wide_shape, wide_shape, wide_shape],
        *sum_two.parts, scratch=[vm(rows_two, LANES, dtype=BF16)],
    )
    conv_grad1, down_grad1, *rest = small_call(
        functools.partial(unpack_kernel, HIGH, 1, line_count), "unpack_first",
        [shape(*first_conv.shape), wide_shape] + [shape(2, half)] * 4 + [shape(width)] * 4 + [shape(5)],
        *sum_one.parts, scratch=[vm(rows_one, LANES, dtype=BF16)],
    )
    return (
        y1.T, y2.T, dx.T,
        rest[4], rest[5], down_grad1.T, rest[0], rest[1], conv_grad1, up_grad1,
        rest[6], rest[7], down_grad2.T, rest[2], rest[3], conv_grad2, up_grad2,
        rest[8],
    )


def solution(mesh):
    tokens = P(("rows", "ch"), None)
    block = (P(), P(), P(None, "ch"), P(None, "ch"), P(None, "ch"), P(None, None, "ch"), P("ch", None))
    return jax.shard_map(
        local,
        mesh=mesh,
        in_specs=(tokens, tokens, P("rows", None), P("rows"), *block, *block),
        out_specs=(tokens, tokens, tokens, *block, *block, P()),
        check_vma=False,
    )
```

```python
import functools
import math

import jax
import jax.numpy as jnp
from jax import lax
from jax.experimental import pallas as pl
from jax.experimental.pallas import tpu as pltpu
from jax.sharding import PartitionSpec as P

DILATION_RATE = 8
EPS = 1e-05
CHAIN = 256
CHAINS = 2
TILE = CHAIN * CHAINS
LANES = 128
CHUNK = 32
K0 = math.sqrt(2.0 / math.pi)
BEND = (K0 * 0.044715) ** (1.0 / 3.0)
BASE = K0 / BEND
F32 = jnp.float32
BF16 = jnp.bfloat16


def gelu(m):
    square = m * m
    bent = jnp.tanh(m * (BASE + square))
    share = (0.5 / BEND) + (0.5 / BEND) * bent
    act = m * share
    return act, share + (act * (1.0 - bent)) * (BASE + 3.0 * square)


def scaled_by(gains, first, rows, hat):
    return hat * wide(gains[first, rows, :]) + wide(gains[first + 1, rows, :])


def wide(column):
    return jnp.concatenate([column, column], axis=1)


def fold(v):
    return v[:, :LANES] + v[:, LANES:]


def down_rows(v):
    return jnp.sum(v.reshape(-1, 8, v.shape[1]), axis=0)


def total_rows(v):
    return jnp.sum(v, axis=0, keepdims=True)


def chunks(count):
    return [slice(start, min(start + CHUNK, count)) for start in range(0, count, CHUNK)]


def half_chunks(count):
    half = count // 2
    return [slice(base + c.start, base + c.stop) for base in (0, half) for c in chunks(half)]


def up_to(value, step):
    return (value + step - 1) // step * step


def chain_lanes(chain):
    return slice(chain * CHAIN, (chain + 1) * CHAIN)


def together(*lists):
    marked = []
    for steps in lists:
        marked += [((k + 0.5) / len(steps), step) for k, step in enumerate(steps)]
    for _, step in sorted(marked, key=lambda pair: pair[0]):
        step()


def in_chains(*stages):
    built = [[stage(chain, chain_lanes(chain)) for stage in stages] for chain in range(CHAINS)]
    first, second = built
    together(first[0])
    for k in range(1, len(stages)):
        together(first[k], second[k - 1])
    together(second[-1])


def per_chunk(count, work):
    return [functools.partial(work, rows) for rows in chunks(count)]


class Places:
    def __init__(self, lengths, padding, own, step):
        self.own = own
        self.core = lax.axis_index("ch")
        self.step = step
        self.ends = []
        end = 0
        for k in range(lengths.shape[1]):
            end = end + lengths[0, k]
            self.ends.append(end)
        self.pad_start = 2 * own - padding[0]

    def of(self, chain):
        base = self.core * self.own + self.step * TILE + chain * CHAIN
        return base + lax.broadcasted_iota(jnp.int32, (1, CHAIN), 1)

    def segment(self, at):
        count = jnp.zeros((1, CHAIN), jnp.int32)
        for end in self.ends:
            count = count + jnp.where(at >= end, 1, 0)
        count = jnp.where(at >= self.pad_start, len(self.ends), count)
        return jnp.where(at < 0, -1, count)

    def valid(self, chain):
        return self.of(chain) < self.pad_start

    def tokens(self):
        return jnp.clip(self.pad_start - self.core * self.own, 0, self.own).astype(F32)


def tap_masks(places, chain, offsets):
    at = places.of(chain)
    mine = places.segment(at)
    result = []
    for offset in offsets:
        other = places.segment(at + offset * DILATION_RATE)
        keep = jnp.where((other == mine) & (mine < len(places.ends)), 1.0, 0.0)
        result.append(jnp.broadcast_to(keep, (16, CHAIN)).astype(BF16))
    return result


def shifted(parts, rows, chain, offset, mask):
    left, middle, right = parts
    lanes = chain_lanes(chain)
    if offset == 0:
        piece = middle[rows, lanes]
    elif offset < 0:
        before = left[rows, :] if chain == 0 else middle[rows, lanes.start - LANES : lanes.start]
        ext = jnp.concatenate([before, middle[rows, lanes]], axis=1)
        piece = pltpu.roll(ext, -offset * DILATION_RATE, 1)[:, LANES:]
    else:
        after = right[rows, :] if chain == CHAINS - 1 else middle[rows, lanes.stop : lanes.stop + LANES]
        ext = jnp.concatenate([middle[rows, lanes], after], axis=1)
        piece = pltpu.roll(ext, ext.shape[1] - offset * DILATION_RATE, 1)[:, :CHAIN]
    count = piece.shape[0]
    if count % 16:
        return piece * jnp.concatenate([mask] * (count // 16 + 1), axis=0)[:count]
    return (piece.reshape(count // 16, 16, CHAIN) * mask[None]).reshape(count, CHAIN)


def stack_forward(stack, parts, places, offsets):
    count = parts[1].shape[0]

    def stage(chain, lanes):
        masks = tap_masks(places, chain, offsets)

        def step(number, rows):
            piece = shifted(parts, rows, chain, offsets[number], masks[number])
            stack[number * count + rows.start : number * count + rows.stop, lanes] = piece

        return [functools.partial(step, number, rows) for number in range(len(offsets)) for rows in chunks(count)]

    return stage


def stack_backward(stack, parts, places, offsets):
    count = parts[1].shape[0]
    half = count // 2
    part = stack.shape[0] // 2

    def stage(chain, lanes):
        masks = tap_masks(places, chain, offsets)

        def step(number, rows):
            piece = shifted(parts, rows, chain, offsets[number], masks[number])
            for which in range(2):
                first = max(rows.start, which * half)
                last = min(rows.stop, (which + 1) * half)
                if first < last:
                    at = which * part + number * half + first - which * half
                    stack[at : at + last - first, lanes] = piece[first - rows.start : last - rows.start, :]

        return [functools.partial(step, number, rows) for number in range(len(offsets)) for rows in chunks(count)]

    return stage


class Totals:
    def __init__(self):
        self.sums = {}

    def add(self, name, value):
        value = down_rows(value)
        self.sums[name] = self.sums[name] + value if name in self.sums else value

    def get(self, name):
        return total_rows(self.sums[name])


def inner_norm(values, lanes, gains, first, act_out, hat_out, scale_out, slope_out=None):
    count = values.shape[0]
    totals, stats = Totals(), {}

    def measure(rows):
        value = values[rows, lanes]
        totals.add("one", value)
        totals.add("two", value * value)

    def settle():
        stats["centre"] = totals.get("one") / count
        stats["scale"] = lax.rsqrt(totals.get("two") / count - stats["centre"] * stats["centre"] + EPS)
        scale_out[:, lanes] = stats["scale"]

    def apply(rows):
        hat = (values[rows, lanes] - stats["centre"]) * stats["scale"]
        hat_out[rows, lanes] = hat.astype(hat_out.dtype)
        act, slope = gelu(scaled_by(gains, first, rows, hat))
        act_out[rows, lanes] = act.astype(BF16)
        if slope_out is not None:
            slope_out[rows, lanes] = slope.astype(BF16)

    return [*per_chunk(count, measure), settle, *per_chunk(count, apply)]


def outer_norm(begin, load, reload, count, lanes, gains, act_out, hat_out, scale_out, squares,
               slope_out=None):
    totals, stats = Totals(), {}

    def prepare():
        stats["about"] = begin()

    def measure(rows):
        shifted = load(rows) - stats["about"]
        totals.add("one", shifted)
        totals.add("two", shifted * shifted)

    def settle():
        off = totals.get("one") / count
        spread = totals.get("two") / count - off * off
        stats["centre"] = stats["about"] + off
        stats["scale"] = lax.rsqrt(spread + EPS)
        scale_out[:, lanes] = stats["scale"]
        squares(count * (spread + stats["centre"] * stats["centre"]))

    def apply(rows):
        hat = (reload(rows) - stats["centre"]) * stats["scale"]
        hat_out[rows, lanes] = hat.astype(BF16)
        act, slope = gelu(scaled_by(gains, 0, rows, hat))
        act_out[rows, lanes] = act.astype(BF16)
        if slope_out is not None:
            slope_out[rows, lanes] = slope.astype(BF16)

    return [prepare, *per_chunk(count, measure), settle, *per_chunk(count, apply)]


def norm_back(grad, lanes, hat_of, scale_of, gains, first, sums, store, slope_of=None, act_out=None):
    count = grad.shape[0]
    totals, stats = Totals(), {}

    def measure(rows):
        hat = hat_of(rows)
        if slope_of is None:
            act, slope = gelu(scaled_by(gains, first, rows, hat))
            if act_out is not None:
                act_out[rows, lanes] = act.astype(BF16)
        else:
            slope = slope_of(rows)
        gain = wide(gains[first, rows, :])
        before = grad[rows, lanes] * slope
        along = before * hat
        sums[0, rows, :] += fold(along)
        sums[1, rows, :] += fold(before)
        scaled = before * gain
        grad[rows, lanes] = scaled
        totals.add("one", scaled)
        totals.add("two", along * gain)

    def settle():
        scale = scale_of()
        stats["scale"] = scale
        stats["base"] = scale * (totals.get("one") / count)
        stats["tilt"] = scale * (totals.get("two") / count)

    def apply(rows):
        value = grad[rows, lanes] * stats["scale"] - stats["base"]
        store(rows, value - hat_of(rows) * stats["tilt"])

    return [*per_chunk(count, measure), settle, *per_chunk(count, apply)]


def kept_back(grad, lanes, hats, scales, gains, sums, store, slopes=None, **more):
    if slopes is not None:
        more["slope_of"] = lambda rows: slopes[rows, lanes].astype(F32)
    return norm_back(grad, lanes, lambda rows: hats[rows, lanes].astype(F32), lambda: scales[:, lanes], gains, 0,
                     sums, store, **more)


def dot(left, right):
    return jnp.dot(left, right, preferred_element_type=F32)


def dot_nt(left, right):
    return lax.dot_general(left, right, (((1,), (1,)), ((), ())), preferred_element_type=F32)


def multiply(target, left, right):
    rows, depth = left.shape

    def stage(chain, lanes):
        def deep(start):
            stop = min(start + 2 * CHAIN, depth)
            part = dot(left[:, start:stop], right[start:stop, lanes])
            target[:, lanes] = part if start == 0 else target[:, lanes] + part

        def high(start):
            stop = min(start + 400, rows)
            target[start:stop, lanes] = dot(left[start:stop, :], right[:, lanes])

        if depth > 2 * CHAIN:
            return [functools.partial(deep, start) for start in range(0, depth, 2 * CHAIN)]
        return [functools.partial(high, start) for start in range(0, rows, 400)]

    return stage


def add_product(target, left, right, lanes=slice(None)):
    count = 400 if left.shape[0] % 400 == 0 else 512

    def step(start):
        stop = min(start + count, left.shape[0])
        target[start:stop, :] += dot_nt(left[start:stop, lanes], right[:, lanes])

    return [functools.partial(step, start) for start in range(0, left.shape[0], count)]


def in_order(core, mine, other, axis):
    return jnp.where(
        core == 0, jnp.concatenate([mine, other], axis=axis), jnp.concatenate([other, mine], axis=axis)
    )


def spread_outer(gain, bias, gains):
    for place, vector in enumerate((gain, bias)):
        column = vector[...].astype(F32).reshape(1, -1).T
        gains[place, :, :] = jnp.broadcast_to(BEND * column, gains.shape[1:])


def spread_inner(core, small, small_other, numbers, gains):
    columns = in_order(core, small[...].astype(F32).T, small_other[...].astype(F32).T, 0)
    for place, number in enumerate(numbers):
        gains[place, :, :] = jnp.broadcast_to(BEND * columns[:, number : number + 1], gains.shape[1:])


def joined(core, mine, other, target):
    target[...] = in_order(core, mine[...], other[...], 0)


def joined_t(core, mine, other, target):
    target[...] = in_order(core, mine[...], other[...], 0).T


def conv_forward_weight(core, mine, other, target):
    taps, count, _ = mine.shape
    for tap in range(taps):
        target[:, tap * count : (tap + 1) * count] = in_order(core, mine[tap].T, other[tap].T, 0)


def conv_backward_weight(core, mine, other, target):
    taps, _, half = mine.shape
    part = target.shape[1] // 2
    target[...] = jnp.zeros(target.shape, target.dtype)
    for tap in range(taps):
        one, two = mine[tap], other[tap]
        target[:, tap * half : (tap + 1) * half] = jnp.where(core == 0, one, two)
        target[:, part + tap * half : part + (tap + 1) * half] = jnp.where(core == 0, two, one)


def pack_conv(acc, core, mine, other, base):
    both, count = acc.shape
    slabs = both // 2 // LANES
    for slab in range(slabs):
        one = acc[slab * LANES : (slab + 1) * LANES, :].astype(BF16).T
        two = acc[both // 2 + slab * LANES : both // 2 + (slab + 1) * LANES, :].astype(BF16).T
        at = base + slab * count
        mine[at : at + count, :] = jnp.where(core == 0, one, two)
        other[at : at + count, :] = jnp.where(core == 0, two, one)


def pack_wide(acc, core, mine, other, base):
    width, count = acc.shape
    half = count // 2
    for slab in range(up_to(width, LANES) // LANES):
        some = min(LANES, width - slab * LANES)
        value = acc[slab * LANES : slab * LANES + some, :]
        if some < LANES:
            value = jnp.concatenate([value, jnp.zeros((LANES - some, count), F32)], axis=0)
        value = value.astype(BF16).T
        one, two = value[:half, :], value[half:, :]
        at = base + slab * half
        mine[at : at + half, :] = jnp.where(core == 0, one, two)
        other[at : at + half, :] = jnp.where(core == 0, two, one)


def wide_rows(half, width):
    return up_to(width, LANES) // LANES * half


def row_form(sums, target):
    for k in range(sums.shape[0]):
        target[k, :, :] = lax.dot_general(
            jnp.full((8, LANES), BEND, F32), sums[k, :, :], (((1,), (1,)), ((), ())),
            precision=lax.Precision.HIGHEST, preferred_element_type=F32,
        )


def clear(step, *refs):
    @pl.when(step == 0)
    def _():
        for ref in refs:
            ref[...] = jnp.zeros(ref.shape, ref.dtype)


def row_list(line):
    width = line.shape[1]
    line = jnp.concatenate([line, jnp.zeros((1, up_to(width, LANES) - width), F32)], axis=1)
    return [line[:, at : at + LANES] for at in range(0, line.shape[1], LANES)]


def rows_together(rows, multiple):
    pad = up_to(len(rows), multiple) - len(rows)
    return jnp.concatenate(rows + [jnp.zeros((pad, LANES), F32)] * bool(pad), axis=0)


def small_rows(core, inner):
    mine, other = [], []
    for ref in inner:
        for k in range(2):
            line = ref[k, 0:1, :]
            half = line.shape[1] // 2
            for one, two in zip(row_list(line[:, :half]), row_list(line[:, half:])):
                mine.append(jnp.where(core == 0, one, two))
                other.append(jnp.where(core == 0, two, one))
    return rows_together(mine, 16), rows_together(other, 16)


def small_count(half):
    return up_to(8 * (up_to(half, LANES) // LANES), 16)


def moment_row(moments, count):
    lane = lax.broadcasted_iota(jnp.int32, (1, LANES), 1)
    line = jnp.where(lane == len(moments), count, jnp.zeros((1, LANES), F32))
    for k, row in enumerate(moments):
        line = line + jnp.where(lane == k, jnp.sum(row, axis=1, keepdims=True), 0.0)
    return line


def keep_edge(core, step, tiles, source, target):
    @pl.when(step == jnp.where(core == 0, tiles - 1, 0))
    def _():
        target[...] = jnp.where(core == 0, source[:, TILE - LANES :], source[:, :LANES])


def kernel_one(tiles, lengths, padding, x, norm_gain, norm_bias, small, small_other, down, down_other, a_out,
               xhat_out, xscale_out, b_out, hat_out, scale_out, slope_out, edge_out, moments, g_outer, g_inner, down_t, hidden):
    step = pl.program_id(0)
    places = Places(lengths, padding, tiles * TILE, step)
    core = places.core

    @pl.when(step == 0)
    def _():
        spread_outer(norm_gain, norm_bias, g_outer)
        spread_inner(core, small, small_other, (0, 2), g_inner)
        joined(core, down, down_other, down_t)

    clear(step, moments)

    def norm(chain, lanes):
        def load(rows):
            return x[rows, lanes].astype(F32)

        def squares(value):
            moments[0:1, :] += jnp.where(places.valid(chain), value, 0.0)

        return outer_norm(lambda: load(slice(0, 16))[0:1], load, load, x.shape[0], lanes, g_outer, a_out,
                          xhat_out, xscale_out, squares)

    def inner(chain, lanes):
        return inner_norm(hidden, lanes, g_inner, 0, b_out, hat_out, scale_out, slope_out)

    in_chains(norm, multiply(hidden, down_t, a_out), inner)
    keep_edge(core, step, tiles, b_out, edge_out)


def choose_edges(step, tiles, halo, left, right, edge_left, edge_right):
    if left is not None:
        edge_left[...] = jnp.where(step == 0, halo[...], left[...])
    if right is not None:
        edge_right[...] = jnp.where(step == tiles - 1, halo[...], right[...])


def kernel_two(tiles, lengths, padding, b_left, b_mid, b_right, x, b_halo, norm_gain, norm_bias, small,
               small_other, conv, conv_other, up, up_other, down, down_other, y_out, chat_out, cscale_out, a_out,
               yhat_out, yscale_out, yslope_out, b_out, hat_out, scale_out, slope_out, edge_out, moments, stack, g_outer, g_inner, conv_f, up_t, down_t, mixed, stream,
               edge_left, edge_right, act):
    step = pl.program_id(0)
    places = Places(lengths, padding, tiles * TILE, step)
    core = places.core

    @pl.when(step == 0)
    def _():
        spread_outer(norm_gain, norm_bias, g_outer)
        spread_inner(core, small, small_other, (1, 3, 4, 6), g_inner)
        conv_forward_weight(core, conv, conv_other, conv_f)
        joined_t(core, up, up_other, up_t)
        joined(core, down, down_other, down_t)

    clear(step, moments)
    choose_edges(step, tiles, b_halo, b_left, b_right, edge_left, edge_right)
    width = x.shape[0]
    gather = stack_forward(stack, (edge_left, b_mid, edge_right), places, (-2, -1, 0, 1, 2))

    def second(chain, lanes):
        return inner_norm(mixed, lanes, g_inner, 0, act, chat_out, cscale_out)

    def outer(chain, lanes):
        valid = places.valid(chain)
        totals = Totals()

        def branch_of(rows):
            return jnp.where(valid, stream[rows, lanes], 0.0)

        def begin():
            return branch_of(slice(0, 8))[0:1] + x[0:16, lanes].astype(F32)[0:1]

        def load(rows):
            branch = branch_of(rows)
            value = x[rows, lanes].astype(F32) + branch
            stream[rows, lanes] = value
            y_out[rows, lanes] = value.astype(BF16)
            totals.add("branch", branch * branch)
            return value

        def squares(value):
            moments[0:1, :] += totals.get("branch")
            moments[1:2, :] += jnp.where(valid, value, 0.0)

        return outer_norm(begin, load, lambda rows: stream[rows, lanes], width, lanes, g_outer, a_out,
                          yhat_out, yscale_out, squares, yslope_out)

    def first(chain, lanes):
        return inner_norm(mixed, lanes, g_inner, 2, b_out, hat_out, scale_out, slope_out)

    in_chains(gather, multiply(mixed, conv_f, stack), second, multiply(stream, up_t, act), outer,
              multiply(mixed, down_t, a_out), first)
    keep_edge(core, step, tiles, b_out, edge_out)


def kernel_three(tiles, lengths, padding, b_left, b_mid, t, b_halo, small, small_other, conv, conv_other, up,
                 up_other, act, dc_out, edge_out, mine, other, sums_out, stack, g_inner, conv_f, up_all, sums, mixed,
                 turned, hats, slopes, scales, du, edge_left, up_grad):
    step = pl.program_id(0)
    places = Places(lengths, padding, tiles * TILE, step)
    core = places.core

    @pl.when(step == 0)
    def _():
        spread_inner(core, small, small_other, (5, 7), g_inner)
        conv_forward_weight(core, conv, conv_other, conv_f)
        joined(core, up, up_other, up_all)

    clear(step, sums, up_grad)
    choose_edges(step, tiles, b_halo, b_left, None, edge_left, None)
    gather = stack_forward(stack, (edge_left, b_mid, None), places, (-2, -1, 0))

    def turn(chain, lanes):
        keep = jnp.where(places.valid(chain), 1.0, 0.0)
        keep = jnp.broadcast_to(keep, (16, CHAIN)).astype(BF16)

        def step(rows):
            piece = t[rows, lanes].reshape(-1, 16, CHAIN) * keep[None]
            du[rows, lanes] = piece.reshape(-1, CHAIN)

        return per_chunk(t.shape[0], step)

    def second(chain, lanes):
        return inner_norm(mixed, lanes, g_inner, 0, act, hats, scales, slopes)

    def back(chain, lanes):
        def store(rows, v):
            dc_out[rows, lanes] = v.astype(BF16)

        return kept_back(turned, lanes, hats, scales, g_inner, sums, store, slopes)

    one, two = ((chain, chain_lanes(chain)) for chain in range(CHAINS))
    convolve, lower = multiply(mixed, conv_f, stack), multiply(turned, up_all, du)
    together(gather(*one) + turn(*one))
    together(convolve(*one) + lower(*one), gather(*two) + turn(*two))
    together(convolve(*two) + lower(*two), second(*one) + back(*one))
    together(second(*two))
    together(add_product(up_grad, du, act), back(*two))
    keep_edge(core, step, tiles, dc_out, edge_out)

    @pl.when(step == tiles - 1)
    def _():
        row_form(sums, sums_out)
        pack_wide(up_grad, core, mine, other, 0)


def kernel_last(tiles, lengths, padding, e_mid, y, up, up_other, y_out, moments, up_t, stream):
    step = pl.program_id(0)
    places = Places(lengths, padding, tiles * TILE, step)

    @pl.when(step == 0)
    def _():
        joined_t(places.core, up, up_other, up_t)

    clear(step, moments)

    def finish(chain, lanes):
        valid = places.valid(chain)
        totals = Totals()

        def step(rows):
            branch = jnp.where(valid, stream[rows, lanes], 0.0)
            value = y[rows, lanes].astype(F32) + branch
            y_out[rows, lanes] = value.astype(BF16)
            totals.add("branch", branch * branch)
            totals.add("value", value * value)

        def settle():
            moments[0:1, :] += totals.get("branch")
            moments[1:2, :] += jnp.where(valid, totals.get("value"), 0.0)

        return [*per_chunk(y.shape[0], step), settle]

    in_chains(multiply(stream, up_t, e_mid), finish)


def back_conv(gather, conv_b, stack, hats, scales, slopes, g_inner, sums, mixed, dh, b_mid, a_mid, conv_grad, down_grad):
    def first(chain, lanes):
        def store(rows, v):
            dh[rows, lanes] = v.astype(BF16)

        return kept_back(mixed, lanes, hats, scales, g_inner, sums, store, slopes)

    one, two = ((chain, chain_lanes(chain)) for chain in range(CHAINS))
    convolve = multiply(mixed, conv_b, stack)
    together(gather(*one))
    together(convolve(*one), gather(*two))
    together(convolve(*two), first(*one))
    together(add_product(conv_grad, stack, b_mid), first(*two))
    together(add_product(down_grad, a_mid, dh))


def kernel_four(tiles, lengths, padding, dc_mid, dc_right, b_mid, hats, scales, slopes, a_mid, yhats, yscales, yslopes, t,
                chats, cscales, dc_halo, norm_gain, norm_bias, small, small_other, conv, conv_other, down, down_other, up,
                up_other, mine_up, other_up, g_out, dc_out, edge_out, mine, other, outer_out, inner_out, prev_out,
                stack, g_outer, g_inner, g_prev, conv_b, down_all, up_all, sums_outer, sums_inner, sums_prev,
                conv_grad, down_grad, up_grad, mixed, lower_mixed, wide_grad, dh, du, act, edge_right):
    step = pl.program_id(0)
    places = Places(lengths, padding, tiles * TILE, step)
    core = places.core

    @pl.when(step == 0)
    def _():
        spread_outer(norm_gain, norm_bias, g_outer)
        spread_inner(core, small, small_other, (4, 6), g_inner)
        spread_inner(core, small, small_other, (1, 3), g_prev)
        conv_backward_weight(core, conv, conv_other, conv_b)
        joined_t(core, down, down_other, down_all)
        joined(core, up, up_other, up_all)

    clear(step, stack, conv_grad, down_grad, up_grad, sums_outer, sums_inner, sums_prev)
    choose_edges(step, tiles, dc_halo, None, dc_right, None, edge_right)
    gather = stack_backward(stack, (None, dc_mid, edge_right), places, (2, 1, 0))

    def first(chain, lanes):
        def store(rows, v):
            dh[rows, lanes] = v.astype(BF16)

        return kept_back(mixed, lanes, hats, scales, g_inner, sums_inner, store, slopes)

    def outer(chain, lanes):
        keep = jnp.where(places.valid(chain), 1.0, 0.0)
        keep = jnp.broadcast_to(keep, (16, CHAIN)).astype(BF16)

        def store(rows, v):
            grad = (v + t[rows, lanes].astype(F32)).astype(BF16)
            g_out[rows, lanes] = grad
            du[rows, lanes] = (grad.reshape(-1, 16, CHAIN) * keep[None]).reshape(-1, CHAIN)

        return kept_back(wide_grad, lanes, yhats, yscales, g_outer, sums_outer, store, yslopes)

    def second(chain, lanes):
        def store(rows, v):
            dc_out[rows, lanes] = v.astype(BF16)

        return kept_back(lower_mixed, lanes, chats, cscales, g_prev, sums_prev, store, act_out=act)

    one, two = ((chain, chain_lanes(chain)) for chain in range(CHAINS))
    convolve, lift = multiply(mixed, conv_b, stack), multiply(wide_grad, down_all, dh)
    lower = multiply(lower_mixed, up_all, du)
    products = add_product(conv_grad, stack, b_mid)
    some = len(products) // 2
    together(gather(*one))
    together(convolve(*one), gather(*two))
    together(convolve(*two), first(*one))
    together(lift(*one), first(*two))
    together(lift(*two) + products[:some], outer(*one))
    together(lower(*one) + products[some:], outer(*two))
    together(lower(*two) + add_product(down_grad, a_mid, dh), second(*one))
    together(add_product(up_grad, du, act, one[1]), second(*two))
    together(add_product(up_grad, du, act, two[1]))
    keep_edge(core, step, tiles, dc_out, edge_out)

    @pl.when(step == tiles - 1)
    def _():
        row_form(sums_outer, outer_out)
        row_form(sums_inner, inner_out)
        row_form(sums_prev, prev_out)
        at = pack(core, mine, other, conv_grad, (down_grad, up_grad))
        rows = mine_up.shape[0]
        mine[at : at + rows, :] = mine_up[...]
        other[at : at + rows, :] = other_up[...]
        pad_payload(mine, other, at + rows)


def pack(core, mine, other, conv_grad, wides):
    both, count = conv_grad.shape
    pack_conv(conv_grad, core, mine, other, 0)
    at = count * (both // 2 // LANES)
    for ref in wides:
        pack_wide(ref, core, mine, other, at)
        at += wide_rows(count // 2, ref.shape[0])
    return at


def pad_payload(mine, other, at):
    if at < mine.shape[0]:
        for target in (mine, other):
            target[at:, :] = jnp.zeros((mine.shape[0] - at, LANES), BF16)


def kernel_six(tiles, lengths, padding, dc_left, dc_mid, dc_right, b_mid, hats, scales, slopes, a_mid, dc_halo, small, small_other, conv, conv_other, inner_two, prev_one, prev_two, dh_out,
               mine, other, stack, g_inner, conv_b, sums, conv_grad, down_grad, mixed, edge_left,
               edge_right, inner_one):
    step = pl.program_id(0)
    places = Places(lengths, padding, tiles * TILE, step)
    core = places.core

    @pl.when(step == 0)
    def _():
        spread_inner(core, small, small_other, (0, 2), g_inner)
        conv_backward_weight(core, conv, conv_other, conv_b)

    clear(step, stack, conv_grad, down_grad, sums)
    choose_edges(step, tiles, dc_halo, dc_left, dc_right, edge_left, edge_right)
    gather = stack_backward(stack, (edge_left, dc_mid, edge_right), places, (2, 1, 0, -1, -2))
    back_conv(gather, conv_b, stack, hats, scales, slopes, g_inner, sums, mixed, dh_out, b_mid, a_mid, conv_grad, down_grad)

    @pl.when(step == tiles - 1)
    def _():
        row_form(sums, inner_one)
        extra = small_rows(core, (inner_one, prev_one, inner_two, prev_two))
        at = pack(core, mine, other, conv_grad, (down_grad,))
        for target, value in zip((mine, other), extra):
            target[at : at + value.shape[0], :] = value.astype(BF16)
        pad_payload(mine, other, at + extra[0].shape[0])


def outer_first_tile(dh, xhats, xscales, g, down_all, g_outer, sums, dx_out, wide_grad):
    def outer(chain, lanes):
        def store(rows, v):
            dx_out[rows, lanes] = v + g[rows, lanes].astype(F32)

        return kept_back(wide_grad, lanes, xhats, xscales, g_outer, sums, store)

    in_chains(multiply(wide_grad, down_all, dh), outer)


def kernel_seven(tiles, lengths, padding, dh, xhats, xscales, g, norm_gain, norm_bias, down, down_other, dx_out,
                 sums, g_outer, down_all, wide_grad):
    step = pl.program_id(0)
    core = lax.axis_index("ch")

    @pl.when(step == 0)
    def _():
        spread_outer(norm_gain, norm_bias, g_outer)
        joined_t(core, down, down_other, down_all)

    clear(step, sums)
    outer_first_tile(dh, xhats, xscales, g, down_all, g_outer, sums, dx_out, wide_grad)


def kernel_eight(tiles, lengths, padding, dh, xhats, xscales, g, dx_begun, norm_gain, norm_bias, down, down_other,
                 sums_begun, moments_one, moments_two, moments_three, outer_two, dx_out, rows_out, g_outer,
                 down_all, sums, wide_grad, outer_one):
    step = pl.program_id(0)
    places = Places(lengths, padding, tiles * TILE, step)
    core = places.core

    @pl.when(step == 0)
    def _():
        spread_outer(norm_gain, norm_bias, g_outer)
        joined_t(core, down, down_other, down_all)
        sums[...] = sums_begun[...]

    outer_first_tile(dh, xhats, xscales, g, down_all, g_outer, sums, dx_out, wide_grad)

    @pl.when(step == pl.num_programs(0) - 1)
    def _():
        row_form(sums, outer_one)
        rows = [moments_one[0:1, :], moments_two[0:1, :], moments_two[1:2, :], moments_three[0:1, :],
                moments_three[1:2, :]]
        lines = [row for ref in (outer_one, outer_two) for k in range(2) for row in row_list(ref[k, 0:1, :])]
        rows_out[...] = rows_together(lines + [moment_row(rows, places.tokens())], 8)


def split_three(v):
    one = v.astype(BF16)
    rest = v - one.astype(F32)
    two = rest.astype(BF16)
    return one, two, (rest - two.astype(F32)).astype(BF16)


def sum_of_three(parts):
    one, two, three = (part.astype(F32) for part in parts)
    return one + (two + three)


def write_lines(out, at, lines):
    for part in split_three(lines):
        out[at : at + part.shape[0], :] = part
        at += part.shape[0]


def read_lines(ref, count):
    start = ref.shape[0] - 3 * count
    return sum_of_three([ref[start + k * count : start + (k + 1) * count, :] for k in range(3)])


def all_lines(refs, count):
    values = [read_lines(ref, count) for ref in refs]
    while len(values) > 1:
        values = [values[k] + values[k + 1] for k in range(0, len(values), 2)]
    return values[0]


def finish_kernel(own, *refs):
    *arrived, lines, lines_other, out = refs
    total = own[...]
    for ref in arrived:
        total = total + ref[...].astype(F32)
    rows = total.shape[0]
    out[:rows, :] = total.astype(BF16)
    write_lines(out, rows, lines[...] + lines_other[...])


def place_kernel(number, count, scal, *refs):
    *parts, out = refs
    rows = parts[0].shape[0] - 3 * count
    for turn, ref in enumerate(parts):
        out[pl.ds(pl.multiple_of((scal[number] ^ turn) * rows, 16), rows), :] = ref[:rows, :]
    if count:
        write_lines(out, len(parts) * rows, all_lines(parts, count))


def unpack(rows_of, conv_out, wide_outs, inner_outs):
    taps, count, half = conv_out.shape
    slabs = up_to(taps * half, LANES) // LANES
    for start in range(0, count, 80):
        rows = min(80, count - start)
        line = jnp.concatenate([rows_of(k * count + start, rows) for k in range(slabs)], axis=1)
        for tap in range(taps):
            conv_out[tap, start : start + rows, :] = line[:, tap * half : (tap + 1) * half]
    base = slabs * count
    for out in wide_outs:
        width = out.shape[1]
        for slab in range(up_to(width, LANES) // LANES):
            lanes = slice(slab * LANES, min(width, (slab + 1) * LANES))
            value = rows_of(base + slab * half, half)
            out[:, lanes] = value[:, : lanes.stop - lanes.start]
        base += wide_rows(half, width)
    if not inner_outs:
        return
    table = rows_of(base, small_count(half))
    at = 0
    count = up_to(half, LANES) // LANES
    for number in range(8):
        line = jnp.concatenate([table[at + k : at + k + 1, :] for k in range(count)], axis=1)
        norm, what = number // 2, number % 2
        inner_outs[2 * (norm // 2) + what][norm % 2 : norm % 2 + 1, :] = line[:, :half]
        at += count


def unpack_kernel(number, wides, count, scal, one, two, conv_out, *rest):
    flat = rest[-1]
    rows = one.shape[0] - 3 * count
    for turn, ref in enumerate((one, two)):
        flat[pl.ds(pl.multiple_of((scal[number] ^ turn) * rows, 16), rows), :] = ref[:rows, :]
    outs = rest[:-1]
    if count:
        *outs, moments_out = outs
        outs, vectors = outs[:-4], outs[-4:]
        lines = all_lines((one, two), count)
        width = vectors[0].shape[0]
        at = 0
        for vector in vectors:
            for start in range(0, width, LANES):
                some = min(LANES, width - start)
                vector[start : start + some] = lines[at : at + 1, :some].reshape(some)
                at += 1
        totals = lines[at : at + 1, :]
        amount = moments_out.shape[0]
        means = totals[:, :amount] / (totals[:, amount : amount + 1] * width)
        moments_out[...] = jnp.sqrt(means).reshape(amount)
    unpack(lambda at, some: flat[at : at + some, :].astype(F32), conv_out, outs[:wides], outs[wides:])


def swap(values):
    return lax.ppermute(values, "ch", [(0, 1), (1, 0)])


def local(inputs, cotangent, doc_lengths, trailing_pad_tokens, first_norm_gain, first_norm_bias, first_down,
          first_inner_gain, first_inner_bias, first_conv, first_up, second_norm_gain, second_norm_bias,
          second_down, second_inner_gain, second_inner_bias, second_conv, second_up):
    own, width = inputs.shape
    half = first_down.shape[1]
    inner = 2 * half
    tiles = own // TILE
    x = inputs.T
    t = cotangent.T

    small = jnp.concatenate([first_inner_gain, first_inner_bias, second_inner_gain, second_inner_bias], axis=0)
    smalls = (small, swap(small))
    vector_rows = up_to(width, LANES) // LANES
    first_vectors = (first_norm_gain, first_norm_bias)
    second_vectors = (second_norm_gain, second_norm_bias)

    def with_other(v):
        return v, swap(v)

    down_1 = with_other(first_down.T)
    conv_1 = with_other(first_conv)
    up_1 = with_other(first_up)
    down_2 = with_other(second_down.T)
    conv_2 = with_other(second_conv)
    up_2 = with_other(second_up)

    last_lane = own // LANES - 1
    ratio = TILE // LANES

    def tile_of(count, first=0):
        return pl.BlockSpec((count, TILE), lambda i, *s: (0, i + first))

    def left_of(count):
        return pl.BlockSpec((count, LANES), lambda i, *s: (0, jnp.maximum(ratio * i - 1, 0)))

    def right_of(count):
        return pl.BlockSpec((count, LANES), lambda i, *s: (0, jnp.minimum(ratio * i + ratio, last_lane)))

    def whole(*shape):
        zeros = (0,) * len(shape)
        return pl.BlockSpec(shape, lambda i, *s: zeros)

    def whole_of(v):
        return whole(*v.shape)

    anywhere = pl.BlockSpec(memory_space=pl.ANY)

    def shape(*dims, dtype=F32):
        return jax.ShapeDtypeStruct(dims, dtype)

    limits = {
        "norm_down": 16,
        "conv_up_norm_down": 36,
        "conv_turn": 22,
        "back_second": 44,
        "back_conv_first": 32,
        "up_second": 12,
        "back_outer_early": 16,
        "back_outer_late": 18,
        "places": 6,
        "finish": 6,
        "unpack_second": 14,
        "unpack_first": 14,
    }

    def params(name):
        return pltpu.CompilerParams(vmem_limit_bytes=limits[name] * 1024 * 1024)


    def call(kernel, name, in_specs, outs, scratch, *args, first=0, steps=tiles, aliases={}):
        specs = list(in_specs) + [whole_of(v) for v in args[len(in_specs):]]
        out_specs = [tile_of(o[0], first) if isinstance(o, tuple) else whole_of(o) for o in outs]
        out_shape = []
        for o in outs:
            if isinstance(o, tuple):
                o = pltpu.HBM((o[0], own), o[1]) if len(o) == 3 else shape(o[0], own, dtype=o[1])
            out_shape.append(o)
        return pl.pallas_call(
            functools.partial(kernel, tiles),
            grid_spec=pltpu.PrefetchScalarGridSpec(
                num_scalar_prefetch=2,
                grid=(steps,),
                in_specs=specs,
                out_specs=out_specs,
                scratch_shapes=scratch,
            ),
            out_shape=out_shape,
            input_output_aliases=aliases,
            compiler_params=params(name),
            cost_estimate=pl.CostEstimate(flops=15 * 1_150_000_000, bytes_accessed=0, transcendentals=0),
            name=name,
        )(doc_lengths, trailing_pad_tokens, *args)

    def stay(*arrays):
        return [pltpu.with_memory_space_constraint(v, pltpu.HBM) for v in arrays]

    def vm(*dims, dtype=F32):
        return pltpu.VMEM(dims, dtype)

    def tile(count, dtype=F32):
        return pltpu.VMEM((count, TILE), dtype)

    outer_gains = vm(2, width, LANES)
    inner_gains = vm(2, inner, LANES)
    edge = vm(inner, LANES, dtype=BF16)
    edge_shape = shape(inner, LANES, dtype=BF16)
    moment_shape = shape(8, CHAIN)
    taps_1, taps_2 = first_conv.shape[0], second_conv.shape[0]
    part_1, part_2 = up_to(taps_1 * half, LANES), up_to(taps_2 * half, LANES)
    away = True
    normed = [(inner, BF16, away), (1, F32)]
    kept = [(width, BF16, away), (width, BF16, away), (1, F32)]
    inner_slope, wide_slope = (inner, BF16, away), (width, BF16, away)

    a1, xhat, xscale, b1, hat1, scale1, slope1, b1_edge, moments_one = call(
        kernel_one, "norm_down", [tile_of(width)],
        [*kept, (inner, BF16), *normed, inner_slope, edge_shape, moment_shape],
        [outer_gains, inner_gains, vm(inner, width, dtype=BF16), tile(inner)],
        *stay(x, *first_vectors), *smalls, *stay(down_1[0]), down_1[1],
    )

    y1, chat1, cscale1, a2, yhat, yscale, yslope, b2, hat2, scale2, slope2, b2_edge, moments_two = call(
        kernel_two, "conv_up_norm_down",         [left_of(inner), tile_of(inner), right_of(inner), tile_of(width)],
        [(width, BF16, away), *normed, *kept, wide_slope, (inner, BF16), *normed, inner_slope, edge_shape,
         moment_shape],
        [tile(taps_1 * inner, BF16), outer_gains, vm(4, inner, LANES), vm(inner, taps_1 * inner, dtype=BF16),
         vm(width, inner, dtype=BF16), vm(inner, width, dtype=BF16), tile(inner), tile(width), edge, edge,
         tile(inner, BF16)],
        b1, b1, b1, x, swap(b1_edge), *second_vectors, *smalls, *conv_1, *up_1, *down_2,
    )

    pair = wide_rows(half, width)
    gradient_up = [shape(pair, LANES, dtype=BF16)] * 2
    e2, dc2, dc2_edge, mine_up, other_up, sums_c2 = call(
        kernel_three, "conv_turn", [left_of(inner), tile_of(inner), tile_of(width)],
        [(inner, BF16, away), (inner, BF16), edge_shape, *gradient_up, shape(2, 8, inner)],
        [tile(taps_2 * inner, BF16), inner_gains, vm(inner, taps_2 * inner, dtype=BF16),
         vm(inner, width, dtype=BF16), vm(2, inner, LANES), tile(inner), tile(inner), tile(inner),
         tile(inner, BF16), tile(1), tile(width, BF16), edge, vm(width, inner)],
        b2, b2, t, swap(b2_edge), *smalls, *conv_2, *up_2,
    )

    row_count = lax.axis_size("rows")
    inner_in = [tile_of(inner), tile_of(1)]
    wide_in = [tile_of(width), tile_of(1)]
    rows_two = up_to(inner * (part_2 // LANES) + 3 * pair, 16 * row_count)
    rows_one = up_to(inner * (part_1 // LANES) + pair + small_count(half), 16 * row_count)
    g1, dc1, dc1_edge, mine_two, other_two, sums_o2, sums_h2, sums_c1 = call(
        kernel_four, "back_second",
        [tile_of(inner), right_of(inner), tile_of(inner), *inner_in, tile_of(inner), tile_of(width), *wide_in,
         tile_of(width), tile_of(width), *inner_in],
        [(width, BF16, away), (inner, BF16), edge_shape, shape(rows_two, LANES, dtype=BF16),
         shape(rows_two, LANES, dtype=BF16), shape(2, 8, width), shape(2, 8, inner), shape(2, 8, inner)],
        [tile(2 * part_2, BF16), outer_gains, inner_gains, inner_gains, vm(inner, 2 * part_2, dtype=BF16),
         vm(width, inner, dtype=BF16), vm(inner, width, dtype=BF16), vm(2, width, LANES), vm(2, inner, LANES),
         vm(2, inner, LANES), vm(2 * part_2, inner), vm(width, inner), vm(width, inner), tile(inner),
         tile(inner), tile(width), tile(inner, BF16), tile(width, BF16), tile(inner, BF16), edge],
        dc2, dc2, b2, hat2, scale2, slope2, a2, yhat, yscale, yslope, *stay(t), chat1, cscale1, swap(dc2_edge), *second_vectors, *smalls,
        *conv_2, *down_2, *up_1, mine_up, other_up,
    )

    row_index = lax.axis_index("rows")
    core = lax.axis_index("ch")
    above = 0
    while 4 ** (above + 1) < row_count:
        above += 1
    assert 4 ** (above + 1) == row_count
    low, high = (row_index >> core) & 1, (row_index >> (1 - core)) & 1
    digits = jnp.stack(
        [2 * high + low, high, low] + [(row_index >> (2 * k + 2)) & 3 for k in range(above)]
    ).astype(jnp.int32)
    ALL, HIGH, LOW, ABOVE = 0, 1, 2, 3

    def radix(level):
        return 2 if level in (HIGH, LOW) else 4

    def flip(level, turn, c):
        if level >= ABOVE:
            return turn << (2 * (level - ABOVE) + 2)
        low_bit, high_bit = 1 << c, 1 << (1 - c)
        if level == LOW:
            return low_bit
        if level == HIGH:
            return high_bit
        return low_bit * (turn & 1) + high_bit * (turn >> 1)

    def send(v, level, turn):
        pairs = [(2 * r + c, 2 * (r ^ flip(level, turn, c)) + c) for r in range(row_count) for c in range(2)]
        return lax.ppermute(v, ("rows", "ch"), pairs)

    def small_call(kernel, name, out_shape, *args, scratch=()):
        return pl.pallas_call(
            kernel,
            grid_spec=pltpu.PrefetchScalarGridSpec(
                num_scalar_prefetch=1, grid=(1,), in_specs=[whole_of(v) for v in args],
                out_specs=jax.tree.map(whole_of, out_shape), scratch_shapes=list(scratch),
            ),
            out_shape=out_shape,
            compiler_params=params(name),
            name=name,
        )(digits, *args)

    z_levels = [ABOVE + k for k in range(above)]

    class Sum:
        def __init__(self, mine, other, levels):
            self.own, self.arrived = mine, [other]
            self.down, self.up = list(levels), [HIGH, LOW, *z_levels]

        def part(self):
            level = self.down[0]
            turns = radix(level)
            parts = [v.reshape(turns, -1, LANES) for v in (self.own, *self.arrived)]

            def share(turn):
                picked = [lax.dynamic_index_in_dim(v, digits[level] ^ turn, 0, False) for v in parts]
                return sum(v.astype(F32) for v in picked)

            self.own, *self.sends = [share(turn) for turn in range(turns)]
            self.sends = [v.astype(BF16) for v in self.sends]

        def go(self):
            level = self.down.pop(0)
            self.arrived = [send(v, level, turn + 1) for turn, v in enumerate(self.sends)]

        def finish(self, lines=None):
            self.lines = 0
            if lines is None:
                self.own = (self.own + sum(v.astype(F32) for v in self.arrived)).astype(BF16)
                return
            self.lines = lines.shape[0]
            self.own = pl.pallas_call(
                finish_kernel, out_shape=shape(self.own.shape[0] + 3 * self.lines, LANES, dtype=BF16),
                compiler_params=params("finish"), name="finish",
            )(self.own, *self.arrived, lines, swap(lines))

        def spread(self):
            self.level = self.up.pop()
            self.parts = [self.own] + [send(self.own, self.level, turn) for turn in range(1, radix(self.level))]

        def place(self):
            extra, turns = 3 * self.lines, len(self.parts)
            rows = turns * (self.own.shape[0] - extra) + extra
            self.own = small_call(
                functools.partial(place_kernel, self.level, self.lines), "places", shape(rows, LANES, dtype=BF16),
                *self.parts,
            )

    barrier = lax.optimization_barrier
    sum_two = Sum(mine_two, swap(other_two), [ALL, *z_levels])
    sum_two.part()
    dc1, *sum_two.sends = barrier((dc1, *sum_two.sends))
    sum_two.go()

    dh1, mine_one, other_one = call(
        kernel_six, "back_conv_first",
        [left_of(inner), tile_of(inner), right_of(inner), tile_of(inner), *inner_in, tile_of(inner), tile_of(width)],
        [(inner, BF16), shape(rows_one, LANES, dtype=BF16), shape(rows_one, LANES, dtype=BF16)],
        [tile(2 * part_1, BF16), inner_gains, vm(inner, 2 * part_1, dtype=BF16), vm(2, inner, LANES),
         vm(2 * part_1, inner), vm(width, inner), tile(inner), edge, edge, vm(2, 8, inner)],
        dc1, dc1, dc1, *stay(b1, hat1), scale1, *stay(slope1, a1), swap(dc1_edge), *smalls, *conv_1, sums_h2, sums_c1, sums_c2,
    )
    sum_two.part()
    dh1, mine_one, other_one, *sum_two.sends = barrier((dh1, mine_one, other_one, *sum_two.sends))
    sum_two.go()
    sum_one = Sum(mine_one, swap(other_one), [HIGH, LOW, *z_levels])
    sum_one.part()
    dh1, e2, *sum_one.sends = barrier((dh1, e2, *sum_one.sends))
    sum_one.go()

    y2, moments_three = call(
        kernel_last, "up_second", [tile_of(inner), tile_of(width)],
        [(width, BF16, away), moment_shape], [vm(width, inner, dtype=BF16), tile(width)],
        *stay(e2, y1), *up_2,
    )
    moments_three, *sum_two.arrived = barrier((moments_three, *sum_two.arrived))
    while sum_two.down:
        sum_two.part()
        sum_two.go()
    sum_two.finish()
    sum_one.part()
    dh1, moments_three, sum_two.own, *sum_one.sends = barrier((dh1, moments_three, sum_two.own, *sum_one.sends))
    sum_one.go()
    sum_two.spread()

    early = tiles // 2
    dx, sums_begun = call(
        kernel_seven, "back_outer_early", [tile_of(inner), *wide_in, tile_of(width)],
        [(width, F32, away), shape(2, width, LANES)],
        [outer_gains, vm(width, inner, dtype=BF16), tile(width)],
        dh1, *stay(xhat), xscale, *stay(g1), *first_vectors, *down_1, steps=early,
    )
    sum_two.place()
    sum_one.part()
    dh1, sums_begun, sum_two.own, *sum_one.sends = barrier((dh1, sums_begun, sum_two.own, *sum_one.sends))
    sum_one.go()
    sum_two.spread()

    line_count = up_to(4 * vector_rows + 1, 8)
    later = [tile_of(rows, early) for rows in (inner, width, 1, width)]
    dx, lines = call(
        kernel_eight, "back_outer_late", [*later, anywhere],
        [(width, F32, away), shape(line_count, LANES)],
        [outer_gains, vm(width, inner, dtype=BF16), vm(2, width, LANES), tile(width), vm(2, 8, width)],
        dh1, *stay(xhat), xscale, *stay(g1), dx, *first_vectors, *down_1, sums_begun, moments_one, moments_two,
        moments_three, sums_o2, first=early, steps=tiles - early, aliases={6: 0},
    )
    while sum_one.down:
        sum_one.part()
        if sum_two.up:
            sum_two.place()
        lines, sum_two.own, *sum_one.sends = barrier((lines, sum_two.own, *sum_one.sends))
        sum_one.go()
        if sum_two.up:
            sum_two.spread()
    sum_two.place()
    lines, sum_two.own = barrier((lines, sum_two.own))
    sum_one.finish(lines)
    sum_one.own, sum_two.own = barrier((sum_one.own, sum_two.own))
    sum_two.spread()
    assert not sum_two.up
    while sum_one.up:
        sum_one.spread()
        if sum_one.up:
            sum_one.place()
        if len(sum_one.up) == 2:
            sum_one.own, *sum_two.parts = barrier((sum_one.own, *sum_two.parts))

    wide_shape = shape(half, width)
    conv_grad2, down_grad2, up_grad1, up_grad2 = small_call(
        functools.partial(unpack_kernel, HIGH, 3, 0), "unpack_second",
        [shape(*second_conv.shape), wide_shape, wide_shape, wide_shape],
        *sum_two.parts, scratch=[vm(rows_two, LANES, dtype=BF16)],
    )
    conv_grad1, down_grad1, *rest = small_call(
        functools.partial(unpack_kernel, HIGH, 1, line_count), "unpack_first",
        [shape(*first_conv.shape), wide_shape] + [shape(2, half)] * 4 + [shape(width)] * 4 + [shape(5)],
        *sum_one.parts, scratch=[vm(rows_one, LANES, dtype=BF16)],
    )
    return (
        y1.T, y2.T, dx.T,
        rest[4], rest[5], down_grad1.T, rest[0], rest[1], conv_grad1, up_grad1,
        rest[6], rest[7], down_grad2.T, rest[2], rest[3], conv_grad2, up_grad2,
        rest[8],
    )


def solution(mesh):
    tokens = P(("rows", "ch"), None)
    block = (P(), P(), P(None, "ch"), P(None, "ch"), P(None, "ch"), P(None, None, "ch"), P("ch", None))
    return jax.shard_map(
        local,
        mesh=mesh,
        in_specs=(tokens, tokens, P("rows", None), P("rows"), *block, *block),
        out_specs=(tokens, tokens, tokens, *block, *block, P()),
        check_vma=False,
    )
```

```python
import functools
import math

import jax
import jax.numpy as jnp
from jax import lax
from jax.experimental import pallas as pl
from jax.experimental.pallas import tpu as pltpu
from jax.sharding import PartitionSpec as P

DILATION_RATE = 8
EPS = 1e-05
CHAIN = 256
CHAINS = 2
TILE = CHAIN * CHAINS
LANES = 128
CHUNK = 32
K0 = math.sqrt(2.0 / math.pi)
BEND = (K0 * 0.044715) ** (1.0 / 3.0)
BASE = K0 / BEND
F32 = jnp.float32
BF16 = jnp.bfloat16


def gelu(m):
    square = m * m
    bent = jnp.tanh(m * (BASE + square))
    share = (0.5 / BEND) + (0.5 / BEND) * bent
    act = m * share
    return act, share + (act * (1.0 - bent)) * (BASE + 3.0 * square)


def scaled_by(gains, first, rows, hat):
    return hat * wide(gains[first, rows, :]) + wide(gains[first + 1, rows, :])


def wide(column):
    return jnp.concatenate([column, column], axis=1)


def fold(v):
    return v[:, :LANES] + v[:, LANES:]


def down_rows(v):
    return jnp.sum(v.reshape(-1, 8, v.shape[1]), axis=0)


def total_rows(v):
    return jnp.sum(v, axis=0, keepdims=True)


def chunks(count):
    return [slice(start, min(start + CHUNK, count)) for start in range(0, count, CHUNK)]


def half_chunks(count):
    half = count // 2
    return [slice(base + c.start, base + c.stop) for base in (0, half) for c in chunks(half)]


def up_to(value, step):
    return (value + step - 1) // step * step


def chain_lanes(chain):
    return slice(chain * CHAIN, (chain + 1) * CHAIN)


def together(*lists):
    marked = []
    for steps in lists:
        marked += [((k + 0.5) / len(steps), step) for k, step in enumerate(steps)]
    for _, step in sorted(marked, key=lambda pair: pair[0]):
        step()


def in_chains(*stages):
    built = [[stage(chain, chain_lanes(chain)) for stage in stages] for chain in range(CHAINS)]
    first, second = built
    together(first[0])
    for k in range(1, len(stages)):
        together(first[k], second[k - 1])
    together(second[-1])


def per_chunk(count, work):
    return [functools.partial(work, rows) for rows in chunks(count)]


class Places:
    def __init__(self, lengths, padding, own, step):
        self.own = own
        self.core = lax.axis_index("ch")
        self.step = step
        self.ends = []
        end = 0
        for k in range(lengths.shape[1]):
            end = end + lengths[0, k]
            self.ends.append(end)
        self.pad_start = 2 * own - padding[0]

    def of(self, chain):
        base = self.core * self.own + self.step * TILE + chain * CHAIN
        return base + lax.broadcasted_iota(jnp.int32, (1, CHAIN), 1)

    def segment(self, at):
        count = jnp.zeros((1, CHAIN), jnp.int32)
        for end in self.ends:
            count = count + jnp.where(at >= end, 1, 0)
        count = jnp.where(at >= self.pad_start, len(self.ends), count)
        return jnp.where(at < 0, -1, count)

    def valid(self, chain):
        return self.of(chain) < self.pad_start

    def tokens(self):
        return jnp.clip(self.pad_start - self.core * self.own, 0, self.own).astype(F32)


def tap_masks(places, chain, offsets):
    at = places.of(chain)
    mine = places.segment(at)
    result = []
    for offset in offsets:
        other = places.segment(at + offset * DILATION_RATE)
        keep = jnp.where((other == mine) & (mine < len(places.ends)), 1.0, 0.0)
        result.append(jnp.broadcast_to(keep, (16, CHAIN)).astype(BF16))
    return result


def shifted(parts, rows, chain, offset, mask):
    left, middle, right = parts
    lanes = chain_lanes(chain)
    if offset == 0:
        piece = middle[rows, lanes]
    elif offset < 0:
        before = left[rows, :] if chain == 0 else middle[rows, lanes.start - LANES : lanes.start]
        ext = jnp.concatenate([before, middle[rows, lanes]], axis=1)
        piece = pltpu.roll(ext, -offset * DILATION_RATE, 1)[:, LANES:]
    else:
        after = right[rows, :] if chain == CHAINS - 1 else middle[rows, lanes.stop : lanes.stop + LANES]
        ext = jnp.concatenate([middle[rows, lanes], after], axis=1)
        piece = pltpu.roll(ext, ext.shape[1] - offset * DILATION_RATE, 1)[:, :CHAIN]
    count = piece.shape[0]
    if count % 16:
        return piece * jnp.concatenate([mask] * (count // 16 + 1), axis=0)[:count]
    return (piece.reshape(count // 16, 16, CHAIN) * mask[None]).reshape(count, CHAIN)


def stack_forward(stack, parts, places, offsets):
    count = parts[1].shape[0]

    def stage(chain, lanes):
        masks = tap_masks(places, chain, offsets)

        def step(number, rows):
            piece = shifted(parts, rows, chain, offsets[number], masks[number])
            stack[number * count + rows.start : number * count + rows.stop, lanes] = piece

        return [functools.partial(step, number, rows) for number in range(len(offsets)) for rows in chunks(count)]

    return stage


def stack_backward(stack, parts, places, offsets):
    count = parts[1].shape[0]
    half = count // 2
    part = stack.shape[0] // 2

    def stage(chain, lanes):
        masks = tap_masks(places, chain, offsets)

        def step(number, rows):
            piece = shifted(parts, rows, chain, offsets[number], masks[number])
            for which in range(2):
                first = max(rows.start, which * half)
                last = min(rows.stop, (which + 1) * half)
                if first < last:
                    at = which * part + number * half + first - which * half
                    stack[at : at + last - first, lanes] = piece[first - rows.start : last - rows.start, :]

        return [functools.partial(step, number, rows) for number in range(len(offsets)) for rows in chunks(count)]

    return stage


class Totals:
    def __init__(self):
        self.sums = {}

    def add(self, name, value):
        value = down_rows(value)
        self.sums[name] = self.sums[name] + value if name in self.sums else value

    def get(self, name):
        return total_rows(self.sums[name])


def inner_norm(values, lanes, gains, first, act_out, hat_out, scale_out, slope_out=None):
    count = values.shape[0]
    totals, stats = Totals(), {}

    def measure(rows):
        value = values[rows, lanes]
        totals.add("one", value)
        totals.add("two", value * value)

    def settle():
        stats["centre"] = totals.get("one") / count
        stats["scale"] = lax.rsqrt(totals.get("two") / count - stats["centre"] * stats["centre"] + EPS)
        scale_out[:, lanes] = stats["scale"]

    def apply(rows):
        hat = (values[rows, lanes] - stats["centre"]) * stats["scale"]
        hat_out[rows, lanes] = hat.astype(hat_out.dtype)
        act, slope = gelu(scaled_by(gains, first, rows, hat))
        act_out[rows, lanes] = act.astype(BF16)
        if slope_out is not None:
            slope_out[rows, lanes] = slope.astype(BF16)

    return [*per_chunk(count, measure), settle, *per_chunk(count, apply)]


def outer_norm(begin, load, reload, count, lanes, gains, act_out, hat_out, scale_out, squares,
               slope_out=None):
    totals, stats = Totals(), {}

    def prepare():
        stats["about"] = begin()

    def measure(rows):
        shifted = load(rows) - stats["about"]
        totals.add("one", shifted)
        totals.add("two", shifted * shifted)

    def settle():
        off = totals.get("one") / count
        spread = totals.get("two") / count - off * off
        stats["centre"] = stats["about"] + off
        stats["scale"] = lax.rsqrt(spread + EPS)
        scale_out[:, lanes] = stats["scale"]
        squares(count * (spread + stats["centre"] * stats["centre"]))

    def apply(rows):
        hat = (reload(rows) - stats["centre"]) * stats["scale"]
        hat_out[rows, lanes] = hat.astype(BF16)
        act, slope = gelu(scaled_by(gains, 0, rows, hat))
        act_out[rows, lanes] = act.astype(BF16)
        if slope_out is not None:
            slope_out[rows, lanes] = slope.astype(BF16)

    return [prepare, *per_chunk(count, measure), settle, *per_chunk(count, apply)]


def norm_back(grad, lanes, hat_of, scale_of, gains, first, sums, store, slope_of=None, act_out=None):
    count = grad.shape[0]
    totals, stats = Totals(), {}

    def measure(rows):
        hat = hat_of(rows)
        if slope_of is None:
            act, slope = gelu(scaled_by(gains, first, rows, hat))
            if act_out is not None:
                act_out[rows, lanes] = act.astype(BF16)
        else:
            slope = slope_of(rows)
        gain = wide(gains[first, rows, :])
        before = grad[rows, lanes] * slope
        along = before * hat
        sums[0, rows, :] += fold(along)
        sums[1, rows, :] += fold(before)
        scaled = before * gain
        grad[rows, lanes] = scaled
        totals.add("one", scaled)
        totals.add("two", along * gain)

    def settle():
        scale = scale_of()
        stats["scale"] = scale
        stats["base"] = scale * (totals.get("one") / count)
        stats["tilt"] = scale * (totals.get("two") / count)

    def apply(rows):
        value = grad[rows, lanes] * stats["scale"] - stats["base"]
        store(rows, value - hat_of(rows) * stats["tilt"])

    return [*per_chunk(count, measure), settle, *per_chunk(count, apply)]


def kept_back(grad, lanes, hats, scales, gains, sums, store, slopes=None, **more):
    if slopes is not None:
        more["slope_of"] = lambda rows: slopes[rows, lanes].astype(F32)
    return norm_back(grad, lanes, lambda rows: hats[rows, lanes].astype(F32), lambda: scales[:, lanes], gains, 0,
                     sums, store, **more)


def dot(left, right):
    return jnp.dot(left, right, preferred_element_type=F32)


def dot_nt(left, right):
    return lax.dot_general(left, right, (((1,), (1,)), ((), ())), preferred_element_type=F32)


def multiply(target, left, right):
    rows, depth = left.shape

    def stage(chain, lanes):
        def deep(start):
            stop = min(start + 2 * CHAIN, depth)
            part = dot(left[:, start:stop], right[start:stop, lanes])
            target[:, lanes] = part if start == 0 else target[:, lanes] + part

        def high(start):
            stop = min(start + 800, rows)
            target[start:stop, lanes] = dot(left[start:stop, :], right[:, lanes])

        if depth > 2 * CHAIN:
            return [functools.partial(deep, start) for start in range(0, depth, 2 * CHAIN)]
        return [functools.partial(high, start) for start in range(0, rows, 800)]

    return stage


def add_product(target, left, right, lanes=slice(None)):
    count = 400 if left.shape[0] % 400 == 0 else 512

    def step(start):
        stop = min(start + count, left.shape[0])
        target[start:stop, :] += dot_nt(left[start:stop, lanes], right[:, lanes])

    return [functools.partial(step, start) for start in range(0, left.shape[0], count)]


def in_order(core, mine, other, axis):
    return jnp.where(
        core == 0, jnp.concatenate([mine, other], axis=axis), jnp.concatenate([other, mine], axis=axis)
    )


def spread_outer(gain, bias, gains):
    for place, vector in enumerate((gain, bias)):
        column = vector[...].astype(F32).reshape(1, -1).T
        gains[place, :, :] = jnp.broadcast_to(BEND * column, gains.shape[1:])


def spread_inner(core, small, small_other, numbers, gains):
    columns = in_order(core, small[...].astype(F32).T, small_other[...].astype(F32).T, 0)
    for place, number in enumerate(numbers):
        gains[place, :, :] = jnp.broadcast_to(BEND * columns[:, number : number + 1], gains.shape[1:])


def joined(core, mine, other, target):
    target[...] = in_order(core, mine[...], other[...], 0)


def joined_t(core, mine, other, target):
    target[...] = in_order(core, mine[...], other[...], 0).T


def conv_forward_weight(core, mine, other, target):
    taps, count, _ = mine.shape
    for tap in range(taps):
        target[:, tap * count : (tap + 1) * count] = in_order(core, mine[tap].T, other[tap].T, 0)


def conv_backward_weight(core, mine, other, target):
    taps, _, half = mine.shape
    part = target.shape[1] // 2
    target[...] = jnp.zeros(target.shape, target.dtype)
    for tap in range(taps):
        one, two = mine[tap], other[tap]
        target[:, tap * half : (tap + 1) * half] = jnp.where(core == 0, one, two)
        target[:, part + tap * half : part + (tap + 1) * half] = jnp.where(core == 0, two, one)


def pack_conv(acc, core, mine, other, base):
    both, count = acc.shape
    slabs = both // 2 // LANES
    for slab in range(slabs):
        one = acc[slab * LANES : (slab + 1) * LANES, :].astype(BF16).T
        two = acc[both // 2 + slab * LANES : both // 2 + (slab + 1) * LANES, :].astype(BF16).T
        at = base + slab * count
        mine[at : at + count, :] = jnp.where(core == 0, one, two)
        other[at : at + count, :] = jnp.where(core == 0, two, one)


def pack_wide(acc, core, mine, other, base):
    width, count = acc.shape
    half = count // 2
    for slab in range(up_to(width, LANES) // LANES):
        some = min(LANES, width - slab * LANES)
        value = acc[slab * LANES : slab * LANES + some, :]
        if some < LANES:
            value = jnp.concatenate([value, jnp.zeros((LANES - some, count), F32)], axis=0)
        value = value.astype(BF16).T
        one, two = value[:half, :], value[half:, :]
        at = base + slab * half
        mine[at : at + half, :] = jnp.where(core == 0, one, two)
        other[at : at + half, :] = jnp.where(core == 0, two, one)


def wide_rows(half, width):
    return up_to(width, LANES) // LANES * half


def row_form(sums, target):
    for k in range(sums.shape[0]):
        target[k, :, :] = lax.dot_general(
            jnp.full((8, LANES), BEND, F32), sums[k, :, :], (((1,), (1,)), ((), ())),
            precision=lax.Precision.HIGHEST, preferred_element_type=F32,
        )


def clear(step, *refs):
    @pl.when(step == 0)
    def _():
        for ref in refs:
            ref[...] = jnp.zeros(ref.shape, ref.dtype)


def row_list(line):
    width = line.shape[1]
    line = jnp.concatenate([line, jnp.zeros((1, up_to(width, LANES) - width), F32)], axis=1)
    return [line[:, at : at + LANES] for at in range(0, line.shape[1], LANES)]


def rows_together(rows, multiple):
    pad = up_to(len(rows), multiple) - len(rows)
    return jnp.concatenate(rows + [jnp.zeros((pad, LANES), F32)] * bool(pad), axis=0)


def small_rows(core, inner):
    mine, other = [], []
    for ref in inner:
        for k in range(2):
            line = ref[k, 0:1, :]
            half = line.shape[1] // 2
            for one, two in zip(row_list(line[:, :half]), row_list(line[:, half:])):
                mine.append(jnp.where(core == 0, one, two))
                other.append(jnp.where(core == 0, two, one))
    return rows_together(mine, 16), rows_together(other, 16)


def small_count(half):
    return up_to(8 * (up_to(half, LANES) // LANES), 16)


def moment_row(moments, count):
    lane = lax.broadcasted_iota(jnp.int32, (1, LANES), 1)
    line = jnp.where(lane == len(moments), count, jnp.zeros((1, LANES), F32))
    for k, row in enumerate(moments):
        line = line + jnp.where(lane == k, jnp.sum(row, axis=1, keepdims=True), 0.0)
    return line


def keep_edge(core, step, tiles, source, target):
    @pl.when(step == jnp.where(core == 0, tiles - 1, 0))
    def _():
        target[...] = jnp.where(core == 0, source[:, TILE - LANES :], source[:, :LANES])


def kernel_one(tiles, lengths, padding, x, norm_gain, norm_bias, small, small_other, down, down_other, a_out,
               xhat_out, xscale_out, b_out, hat_out, scale_out, slope_out, edge_out, moments, g_outer, g_inner, down_t, hidden):
    step = pl.program_id(0)
    places = Places(lengths, padding, tiles * TILE, step)
    core = places.core

    @pl.when(step == 0)
    def _():
        spread_outer(norm_gain, norm_bias, g_outer)
        spread_inner(core, small, small_other, (0, 2), g_inner)
        joined(core, down, down_other, down_t)

    clear(step, moments)

    def norm(chain, lanes):
        def load(rows):
            return x[rows, lanes].astype(F32)

        def squares(value):
            moments[0:1, :] += jnp.where(places.valid(chain), value, 0.0)

        return outer_norm(lambda: load(slice(0, 16))[0:1], load, load, x.shape[0], lanes, g_outer, a_out,
                          xhat_out, xscale_out, squares)

    def inner(chain, lanes):
        return inner_norm(hidden, lanes, g_inner, 0, b_out, hat_out, scale_out, slope_out)

    in_chains(norm, multiply(hidden, down_t, a_out), inner)
    keep_edge(core, step, tiles, b_out, edge_out)


def choose_edges(step, tiles, halo, left, right, edge_left, edge_right):
    if left is not None:
        edge_left[...] = jnp.where(step == 0, halo[...], left[...])
    if right is not None:
        edge_right[...] = jnp.where(step == tiles - 1, halo[...], right[...])


def kernel_two(tiles, lengths, padding, b_left, b_mid, b_right, x, b_halo, norm_gain, norm_bias, small,
               small_other, conv, conv_other, up, up_other, down, down_other, y_out, chat_out, cscale_out, a_out,
               yhat_out, yscale_out, yslope_out, b_out, hat_out, scale_out, slope_out, edge_out, moments, stack, g_outer, g_inner, conv_f, up_t, down_t, mixed, stream,
               edge_left, edge_right, act):
    step = pl.program_id(0)
    places = Places(lengths, padding, tiles * TILE, step)
    core = places.core

    @pl.when(step == 0)
    def _():
        spread_outer(norm_gain, norm_bias, g_outer)
        spread_inner(core, small, small_other, (1, 3, 4, 6), g_inner)
        conv_forward_weight(core, conv, conv_other, conv_f)
        joined_t(core, up, up_other, up_t)
        joined(core, down, down_other, down_t)

    clear(step, moments)
    choose_edges(step, tiles, b_halo, b_left, b_right, edge_left, edge_right)
    width = x.shape[0]
    gather = stack_forward(stack, (edge_left, b_mid, edge_right), places, (-2, -1, 0, 1, 2))

    def second(chain, lanes):
        return inner_norm(mixed, lanes, g_inner, 0, act, chat_out, cscale_out)

    def outer(chain, lanes):
        valid = places.valid(chain)
        totals = Totals()

        def branch_of(rows):
            return jnp.where(valid, stream[rows, lanes], 0.0)

        def begin():
            return branch_of(slice(0, 8))[0:1] + x[0:16, lanes].astype(F32)[0:1]

        def load(rows):
            branch = branch_of(rows)
            value = x[rows, lanes].astype(F32) + branch
            stream[rows, lanes] = value
            y_out[rows, lanes] = value.astype(BF16)
            totals.add("branch", branch * branch)
            return value

        def squares(value):
            moments[0:1, :] += totals.get("branch")
            moments[1:2, :] += jnp.where(valid, value, 0.0)

        return outer_norm(begin, load, lambda rows: stream[rows, lanes], width, lanes, g_outer, a_out,
                          yhat_out, yscale_out, squares, yslope_out)

    def first(chain, lanes):
        return inner_norm(mixed, lanes, g_inner, 2, b_out, hat_out, scale_out, slope_out)

    in_chains(gather, multiply(mixed, conv_f, stack), second, multiply(stream, up_t, act), outer,
              multiply(mixed, down_t, a_out), first)
    keep_edge(core, step, tiles, b_out, edge_out)


def kernel_three(tiles, lengths, padding, b_left, b_mid, t, b_halo, small, small_other, conv, conv_other, up,
                 up_other, act, dc_out, edge_out, mine, other, sums_out, stack, g_inner, conv_f, up_all, sums, mixed,
                 turned, hats, slopes, scales, du, edge_left, up_grad):
    step = pl.program_id(0)
    places = Places(lengths, padding, tiles * TILE, step)
    core = places.core

    @pl.when(step == 0)
    def _():
        spread_inner(core, small, small_other, (5, 7), g_inner)
        conv_forward_weight(core, conv, conv_other, conv_f)
        joined(core, up, up_other, up_all)

    clear(step, sums, up_grad)
    choose_edges(step, tiles, b_halo, b_left, None, edge_left, None)
    gather = stack_forward(stack, (edge_left, b_mid, None), places, (-2, -1, 0))

    def turn(chain, lanes):
        keep = jnp.where(places.valid(chain), 1.0, 0.0)
        keep = jnp.broadcast_to(keep, (16, CHAIN)).astype(BF16)

        def step(rows):
            piece = t[rows, lanes].reshape(-1, 16, CHAIN) * keep[None]
            du[rows, lanes] = piece.reshape(-1, CHAIN)

        return per_chunk(t.shape[0], step)

    def second(chain, lanes):
        return inner_norm(mixed, lanes, g_inner, 0, act, hats, scales, slopes)

    def back(chain, lanes):
        def store(rows, v):
            dc_out[rows, lanes] = v.astype(BF16)

        return kept_back(turned, lanes, hats, scales, g_inner, sums, store, slopes)

    one, two = ((chain, chain_lanes(chain)) for chain in range(CHAINS))
    convolve, lower = multiply(mixed, conv_f, stack), multiply(turned, up_all, du)
    together(gather(*one) + turn(*one))
    together(convolve(*one) + lower(*one), gather(*two) + turn(*two))
    together(convolve(*two) + lower(*two), second(*one) + back(*one))
    together(second(*two))
    together(add_product(up_grad, du, act), back(*two))
    keep_edge(core, step, tiles, dc_out, edge_out)

    @pl.when(step == tiles - 1)
    def _():
        row_form(sums, sums_out)
        pack_wide(up_grad, core, mine, other, 0)


def kernel_last(tiles, lengths, padding, e_mid, y, up, up_other, y_out, moments, up_t, stream):
    step = pl.program_id(0)
    places = Places(lengths, padding, tiles * TILE, step)

    @pl.when(step == 0)
    def _():
        joined_t(places.core, up, up_other, up_t)

    clear(step, moments)

    def finish(chain, lanes):
        valid = places.valid(chain)
        totals = Totals()

        def step(rows):
            branch = jnp.where(valid, stream[rows, lanes], 0.0)
            value = y[rows, lanes].astype(F32) + branch
            y_out[rows, lanes] = value.astype(BF16)
            totals.add("branch", branch * branch)
            totals.add("value", value * value)

        def settle():
            moments[0:1, :] += totals.get("branch")
            moments[1:2, :] += jnp.where(valid, totals.get("value"), 0.0)

        return [*per_chunk(y.shape[0], step), settle]

    in_chains(multiply(stream, up_t, e_mid), finish)


def back_conv(gather, conv_b, stack, hats, scales, slopes, g_inner, sums, mixed, dh, b_mid, a_mid, conv_grad, down_grad):
    def first(chain, lanes):
        def store(rows, v):
            dh[rows, lanes] = v.astype(BF16)

        return kept_back(mixed, lanes, hats, scales, g_inner, sums, store, slopes)

    one, two = ((chain, chain_lanes(chain)) for chain in range(CHAINS))
    convolve = multiply(mixed, conv_b, stack)
    together(gather(*one))
    together(convolve(*one), gather(*two))
    together(convolve(*two), first(*one))
    together(add_product(conv_grad, stack, b_mid), first(*two))
    together(add_product(down_grad, a_mid, dh))


def kernel_four(tiles, lengths, padding, dc_mid, dc_right, b_mid, hats, scales, slopes, a_mid, yhats, yscales, yslopes, t,
                chats, cscales, dc_halo, norm_gain, norm_bias, small, small_other, conv, conv_other, down, down_other, up,
                up_other, mine_up, other_up, g_out, dc_out, edge_out, mine, other, outer_out, inner_out, prev_out,
                stack, g_outer, g_inner, g_prev, conv_b, down_all, up_all, sums_outer, sums_inner, sums_prev,
                conv_grad, down_grad, up_grad, mixed, lower_mixed, wide_grad, dh, du, act, edge_right):
    step = pl.program_id(0)
    places = Places(lengths, padding, tiles * TILE, step)
    core = places.core

    @pl.when(step == 0)
    def _():
        spread_outer(norm_gain, norm_bias, g_outer)
        spread_inner(core, small, small_other, (4, 6), g_inner)
        spread_inner(core, small, small_other, (1, 3), g_prev)
        conv_backward_weight(core, conv, conv_other, conv_b)
        joined_t(core, down, down_other, down_all)
        joined(core, up, up_other, up_all)

    clear(step, stack, conv_grad, down_grad, up_grad, sums_outer, sums_inner, sums_prev)
    choose_edges(step, tiles, dc_halo, None, dc_right, None, edge_right)
    gather = stack_backward(stack, (None, dc_mid, edge_right), places, (2, 1, 0))

    def first(chain, lanes):
        def store(rows, v):
            dh[rows, lanes] = v.astype(BF16)

        return kept_back(mixed, lanes, hats, scales, g_inner, sums_inner, store, slopes)

    def outer(chain, lanes):
        keep = jnp.where(places.valid(chain), 1.0, 0.0)
        keep = jnp.broadcast_to(keep, (16, CHAIN)).astype(BF16)

        def store(rows, v):
            grad = (v + t[rows, lanes].astype(F32)).astype(BF16)
            g_out[rows, lanes] = grad
            du[rows, lanes] = (grad.reshape(-1, 16, CHAIN) * keep[None]).reshape(-1, CHAIN)

        return kept_back(wide_grad, lanes, yhats, yscales, g_outer, sums_outer, store, yslopes)

    def second(chain, lanes):
        def store(rows, v):
            dc_out[rows, lanes] = v.astype(BF16)

        return kept_back(lower_mixed, lanes, chats, cscales, g_prev, sums_prev, store, act_out=act)

    one, two = ((chain, chain_lanes(chain)) for chain in range(CHAINS))
    convolve, lift = multiply(mixed, conv_b, stack), multiply(wide_grad, down_all, dh)
    lower = multiply(lower_mixed, up_all, du)
    products = add_product(conv_grad, stack, b_mid)
    some = len(products) // 2
    together(gather(*one))
    together(convolve(*one), gather(*two))
    together(convolve(*two), first(*one))
    together(lift(*one), first(*two))
    together(lift(*two) + products[:some], outer(*one))
    together(lower(*one) + products[some:], outer(*two))
    together(lower(*two) + add_product(down_grad, a_mid, dh), second(*one))
    together(add_product(up_grad, du, act, one[1]), second(*two))
    together(add_product(up_grad, du, act, two[1]))
    keep_edge(core, step, tiles, dc_out, edge_out)

    @pl.when(step == tiles - 1)
    def _():
        row_form(sums_outer, outer_out)
        row_form(sums_inner, inner_out)
        row_form(sums_prev, prev_out)
        at = pack(core, mine, other, conv_grad, (down_grad, up_grad))
        rows = mine_up.shape[0]
        mine[at : at + rows, :] = mine_up[...]
        other[at : at + rows, :] = other_up[...]
        pad_payload(mine, other, at + rows)


def pack(core, mine, other, conv_grad, wides):
    both, count = conv_grad.shape
    pack_conv(conv_grad, core, mine, other, 0)
    at = count * (both // 2 // LANES)
    for ref in wides:
        pack_wide(ref, core, mine, other, at)
        at += wide_rows(count // 2, ref.shape[0])
    return at


def pad_payload(mine, other, at):
    if at < mine.shape[0]:
        for target in (mine, other):
            target[at:, :] = jnp.zeros((mine.shape[0] - at, LANES), BF16)


def kernel_six(tiles, lengths, padding, dc_left, dc_mid, dc_right, b_mid, hats, scales, slopes, a_mid, dc_halo, small, small_other, conv, conv_other, inner_two, prev_one, prev_two, dh_out,
               mine, other, stack, g_inner, conv_b, sums, conv_grad, down_grad, mixed, edge_left,
               edge_right, inner_one):
    step = pl.program_id(0)
    places = Places(lengths, padding, tiles * TILE, step)
    core = places.core

    @pl.when(step == 0)
    def _():
        spread_inner(core, small, small_other, (0, 2), g_inner)
        conv_backward_weight(core, conv, conv_other, conv_b)

    clear(step, stack, conv_grad, down_grad, sums)
    choose_edges(step, tiles, dc_halo, dc_left, dc_right, edge_left, edge_right)
    gather = stack_backward(stack, (edge_left, dc_mid, edge_right), places, (2, 1, 0, -1, -2))
    back_conv(gather, conv_b, stack, hats, scales, slopes, g_inner, sums, mixed, dh_out, b_mid, a_mid, conv_grad, down_grad)

    @pl.when(step == tiles - 1)
    def _():
        row_form(sums, inner_one)
        extra = small_rows(core, (inner_one, prev_one, inner_two, prev_two))
        at = pack(core, mine, other, conv_grad, (down_grad,))
        for target, value in zip((mine, other), extra):
            target[at : at + value.shape[0], :] = value.astype(BF16)
        pad_payload(mine, other, at + extra[0].shape[0])


def outer_first_tile(dh, xhats, xscales, g, down_all, g_outer, sums, dx_out, wide_grad):
    def outer(chain, lanes):
        def store(rows, v):
            dx_out[rows, lanes] = v + g[rows, lanes].astype(F32)

        return kept_back(wide_grad, lanes, xhats, xscales, g_outer, sums, store)

    in_chains(multiply(wide_grad, down_all, dh), outer)


def kernel_seven(tiles, lengths, padding, dh, xhats, xscales, g, norm_gain, norm_bias, down, down_other, dx_out,
                 sums, g_outer, down_all, wide_grad):
    step = pl.program_id(0)
    core = lax.axis_index("ch")

    @pl.when(step == 0)
    def _():
        spread_outer(norm_gain, norm_bias, g_outer)
        joined_t(core, down, down_other, down_all)

    clear(step, sums)
    outer_first_tile(dh, xhats, xscales, g, down_all, g_outer, sums, dx_out, wide_grad)


def kernel_eight(tiles, lengths, padding, dh, xhats, xscales, g, dx_begun, norm_gain, norm_bias, down, down_other,
                 sums_begun, moments_one, moments_two, moments_three, outer_two, dx_out, rows_out, g_outer,
                 down_all, sums, wide_grad, outer_one):
    step = pl.program_id(0)
    places = Places(lengths, padding, tiles * TILE, step)
    core = places.core

    @pl.when(step == 0)
    def _():
        spread_outer(norm_gain, norm_bias, g_outer)
        joined_t(core, down, down_other, down_all)
        sums[...] = sums_begun[...]

    outer_first_tile(dh, xhats, xscales, g, down_all, g_outer, sums, dx_out, wide_grad)

    @pl.when(step == pl.num_programs(0) - 1)
    def _():
        row_form(sums, outer_one)
        rows = [moments_one[0:1, :], moments_two[0:1, :], moments_two[1:2, :], moments_three[0:1, :],
                moments_three[1:2, :]]
        lines = [row for ref in (outer_one, outer_two) for k in range(2) for row in row_list(ref[k, 0:1, :])]
        rows_out[...] = rows_together(lines + [moment_row(rows, places.tokens())], 8)


def split_three(v):
    one = v.astype(BF16)
    rest = v - one.astype(F32)
    two = rest.astype(BF16)
    return one, two, (rest - two.astype(F32)).astype(BF16)


def sum_of_three(parts):
    one, two, three = (part.astype(F32) for part in parts)
    return one + (two + three)


def write_lines(out, at, lines):
    for part in split_three(lines):
        out[at : at + part.shape[0], :] = part
        at += part.shape[0]


def read_lines(ref, count):
    start = ref.shape[0] - 3 * count
    return sum_of_three([ref[start + k * count : start + (k + 1) * count, :] for k in range(3)])


def all_lines(refs, count):
    values = [read_lines(ref, count) for ref in refs]
    while len(values) > 1:
        values = [values[k] + values[k + 1] for k in range(0, len(values), 2)]
    return values[0]


def finish_kernel(own, *refs):
    *arrived, lines, lines_other, out = refs
    total = own[...]
    for ref in arrived:
        total = total + ref[...].astype(F32)
    rows = total.shape[0]
    out[:rows, :] = total.astype(BF16)
    write_lines(out, rows, lines[...] + lines_other[...])


def place_kernel(number, count, scal, *refs):
    *parts, out = refs
    rows = parts[0].shape[0] - 3 * count
    for turn, ref in enumerate(parts):
        out[pl.ds(pl.multiple_of((scal[number] ^ turn) * rows, 16), rows), :] = ref[:rows, :]
    if count:
        write_lines(out, len(parts) * rows, all_lines(parts, count))


def unpack(rows_of, conv_out, wide_outs, inner_outs):
    taps, count, half = conv_out.shape
    slabs = up_to(taps * half, LANES) // LANES
    for start in range(0, count, 80):
        rows = min(80, count - start)
        line = jnp.concatenate([rows_of(k * count + start, rows) for k in range(slabs)], axis=1)
        for tap in range(taps):
            conv_out[tap, start : start + rows, :] = line[:, tap * half : (tap + 1) * half]
    base = slabs * count
    for out in wide_outs:
        width = out.shape[1]
        for slab in range(up_to(width, LANES) // LANES):
            lanes = slice(slab * LANES, min(width, (slab + 1) * LANES))
            value = rows_of(base + slab * half, half)
            out[:, lanes] = value[:, : lanes.stop - lanes.start]
        base += wide_rows(half, width)
    if not inner_outs:
        return
    table = rows_of(base, small_count(half))
    at = 0
    count = up_to(half, LANES) // LANES
    for number in range(8):
        line = jnp.concatenate([table[at + k : at + k + 1, :] for k in range(count)], axis=1)
        norm, what = number // 2, number % 2
        inner_outs[2 * (norm // 2) + what][norm % 2 : norm % 2 + 1, :] = line[:, :half]
        at += count


def unpack_kernel(number, wides, count, scal, one, two, conv_out, *rest):
    flat = rest[-1]
    rows = one.shape[0] - 3 * count
    for turn, ref in enumerate((one, two)):
        flat[pl.ds(pl.multiple_of((scal[number] ^ turn) * rows, 16), rows), :] = ref[:rows, :]
    outs = rest[:-1]
    if count:
        *outs, moments_out = outs
        outs, vectors = outs[:-4], outs[-4:]
        lines = all_lines((one, two), count)
        width = vectors[0].shape[0]
        at = 0
        for vector in vectors:
            for start in range(0, width, LANES):
                some = min(LANES, width - start)
                vector[start : start + some] = lines[at : at + 1, :some].reshape(some)
                at += 1
        totals = lines[at : at + 1, :]
        amount = moments_out.shape[0]
        means = totals[:, :amount] / (totals[:, amount : amount + 1] * width)
        moments_out[...] = jnp.sqrt(means).reshape(amount)
    unpack(lambda at, some: flat[at : at + some, :].astype(F32), conv_out, outs[:wides], outs[wides:])


def swap(values):
    return lax.ppermute(values, "ch", [(0, 1), (1, 0)])


def local(inputs, cotangent, doc_lengths, trailing_pad_tokens, first_norm_gain, first_norm_bias, first_down,
          first_inner_gain, first_inner_bias, first_conv, first_up, second_norm_gain, second_norm_bias,
          second_down, second_inner_gain, second_inner_bias, second_conv, second_up):
    own, width = inputs.shape
    half = first_down.shape[1]
    inner = 2 * half
    tiles = own // TILE
    x = inputs.T
    t = cotangent.T

    small = jnp.concatenate([first_inner_gain, first_inner_bias, second_inner_gain, second_inner_bias], axis=0)
    smalls = (small, swap(small))
    vector_rows = up_to(width, LANES) // LANES
    first_vectors = (first_norm_gain, first_norm_bias)
    second_vectors = (second_norm_gain, second_norm_bias)

    def with_other(v):
        return v, swap(v)

    down_1 = with_other(first_down.T)
    conv_1 = with_other(first_conv)
    up_1 = with_other(first_up)
    down_2 = with_other(second_down.T)
    conv_2 = with_other(second_conv)
    up_2 = with_other(second_up)

    last_lane = own // LANES - 1
    ratio = TILE // LANES

    def tile_of(count, first=0):
        return pl.BlockSpec((count, TILE), lambda i, *s: (0, i + first))

    def left_of(count):
        return pl.BlockSpec((count, LANES), lambda i, *s: (0, jnp.maximum(ratio * i - 1, 0)))

    def right_of(count):
        return pl.BlockSpec((count, LANES), lambda i, *s: (0, jnp.minimum(ratio * i + ratio, last_lane)))

    def whole(*shape):
        zeros = (0,) * len(shape)
        return pl.BlockSpec(shape, lambda i, *s: zeros)

    def whole_of(v):
        return whole(*v.shape)

    anywhere = pl.BlockSpec(memory_space=pl.ANY)

    def shape(*dims, dtype=F32):
        return jax.ShapeDtypeStruct(dims, dtype)

    limits = {
        "norm_down": 16,
        "conv_up_norm_down": 36,
        "conv_turn": 22,
        "back_second": 44,
        "back_conv_first": 32,
        "up_second": 12,
        "back_outer_early": 16,
        "back_outer_late": 18,
        "places": 6,
        "finish": 6,
        "unpack_second": 14,
        "unpack_first": 14,
    }

    def params(name):
        return pltpu.CompilerParams(vmem_limit_bytes=limits[name] * 1024 * 1024)


    def call(kernel, name, in_specs, outs, scratch, *args, first=0, steps=tiles, aliases={}):
        specs = list(in_specs) + [whole_of(v) for v in args[len(in_specs):]]
        out_specs = [tile_of(o[0], first) if isinstance(o, tuple) else whole_of(o) for o in outs]
        out_shape = []
        for o in outs:
            if isinstance(o, tuple):
                o = pltpu.HBM((o[0], own), o[1]) if len(o) == 3 else shape(o[0], own, dtype=o[1])
            out_shape.append(o)
        return pl.pallas_call(
            functools.partial(kernel, tiles),
            grid_spec=pltpu.PrefetchScalarGridSpec(
                num_scalar_prefetch=2,
                grid=(steps,),
                in_specs=specs,
                out_specs=out_specs,
                scratch_shapes=scratch,
            ),
            out_shape=out_shape,
            input_output_aliases=aliases,
            compiler_params=params(name),
            cost_estimate=pl.CostEstimate(flops=15 * 1_150_000_000, bytes_accessed=0, transcendentals=0),
            name=name,
        )(doc_lengths, trailing_pad_tokens, *args)

    def stay(*arrays):
        return [pltpu.with_memory_space_constraint(v, pltpu.HBM) for v in arrays]

    def vm(*dims, dtype=F32):
        return pltpu.VMEM(dims, dtype)

    def tile(count, dtype=F32):
        return pltpu.VMEM((count, TILE), dtype)

    outer_gains = vm(2, width, LANES)
    inner_gains = vm(2, inner, LANES)
    edge = vm(inner, LANES, dtype=BF16)
    edge_shape = shape(inner, LANES, dtype=BF16)
    moment_shape = shape(8, CHAIN)
    taps_1, taps_2 = first_conv.shape[0], second_conv.shape[0]
    part_1, part_2 = up_to(taps_1 * half, LANES), up_to(taps_2 * half, LANES)
    away = True
    normed = [(inner, BF16, away), (1, F32)]
    kept = [(width, BF16, away), (width, BF16, away), (1, F32)]
    inner_slope, wide_slope = (inner, BF16, away), (width, BF16, away)

    a1, xhat, xscale, b1, hat1, scale1, slope1, b1_edge, moments_one = call(
        kernel_one, "norm_down", [tile_of(width)],
        [*kept, (inner, BF16), *normed, inner_slope, edge_shape, moment_shape],
        [outer_gains, inner_gains, vm(inner, width, dtype=BF16), tile(inner)],
        *stay(x, *first_vectors), *smalls, *stay(down_1[0]), down_1[1],
    )

    y1, chat1, cscale1, a2, yhat, yscale, yslope, b2, hat2, scale2, slope2, b2_edge, moments_two = call(
        kernel_two, "conv_up_norm_down",         [left_of(inner), tile_of(inner), right_of(inner), tile_of(width)],
        [(width, BF16, away), *normed, *kept, wide_slope, (inner, BF16), *normed, inner_slope, edge_shape,
         moment_shape],
        [tile(taps_1 * inner, BF16), outer_gains, vm(4, inner, LANES), vm(inner, taps_1 * inner, dtype=BF16),
         vm(width, inner, dtype=BF16), vm(inner, width, dtype=BF16), tile(inner), tile(width), edge, edge,
         tile(inner, BF16)],
        b1, b1, b1, x, swap(b1_edge), *second_vectors, *smalls, *conv_1, *up_1, *down_2,
    )

    pair = wide_rows(half, width)
    gradient_up = [shape(pair, LANES, dtype=BF16)] * 2
    e2, dc2, dc2_edge, mine_up, other_up, sums_c2 = call(
        kernel_three, "conv_turn", [left_of(inner), tile_of(inner), tile_of(width)],
        [(inner, BF16, away), (inner, BF16), edge_shape, *gradient_up, shape(2, 8, inner)],
        [tile(taps_2 * inner, BF16), inner_gains, vm(inner, taps_2 * inner, dtype=BF16),
         vm(inner, width, dtype=BF16), vm(2, inner, LANES), tile(inner), tile(inner), tile(inner),
         tile(inner, BF16), tile(1), tile(width, BF16), edge, vm(width, inner)],
        b2, b2, t, swap(b2_edge), *smalls, *conv_2, *up_2,
    )

    row_count = lax.axis_size("rows")
    inner_in = [tile_of(inner), tile_of(1)]
    wide_in = [tile_of(width), tile_of(1)]
    rows_two = up_to(inner * (part_2 // LANES) + 3 * pair, 16 * row_count)
    rows_one = up_to(inner * (part_1 // LANES) + pair + small_count(half), 16 * row_count)
    g1, dc1, dc1_edge, mine_two, other_two, sums_o2, sums_h2, sums_c1 = call(
        kernel_four, "back_second",
        [tile_of(inner), right_of(inner), tile_of(inner), *inner_in, tile_of(inner), tile_of(width), *wide_in,
         tile_of(width), tile_of(width), *inner_in],
        [(width, BF16, away), (inner, BF16), edge_shape, shape(rows_two, LANES, dtype=BF16),
         shape(rows_two, LANES, dtype=BF16), shape(2, 8, width), shape(2, 8, inner), shape(2, 8, inner)],
        [tile(2 * part_2, BF16), outer_gains, inner_gains, inner_gains, vm(inner, 2 * part_2, dtype=BF16),
         vm(width, inner, dtype=BF16), vm(inner, width, dtype=BF16), vm(2, width, LANES), vm(2, inner, LANES),
         vm(2, inner, LANES), vm(2 * part_2, inner), vm(width, inner), vm(width, inner), tile(inner),
         tile(inner), tile(width), tile(inner, BF16), tile(width, BF16), tile(inner, BF16), edge],
        dc2, dc2, b2, hat2, scale2, slope2, a2, yhat, yscale, yslope, *stay(t), chat1, cscale1, swap(dc2_edge), *second_vectors, *smalls,
        *conv_2, *down_2, *up_1, mine_up, other_up,
    )

    row_index = lax.axis_index("rows")
    core = lax.axis_index("ch")
    above = 0
    while 4 ** (above + 1) < row_count:
        above += 1
    assert 4 ** (above + 1) == row_count
    low, high = (row_index >> core) & 1, (row_index >> (1 - core)) & 1
    digits = jnp.stack(
        [2 * high + low, high, low] + [(row_index >> (2 * k + 2)) & 3 for k in range(above)]
    ).astype(jnp.int32)
    ALL, HIGH, LOW, ABOVE = 0, 1, 2, 3

    def radix(level):
        return 2 if level in (HIGH, LOW) else 4

    def flip(level, turn, c):
        if level >= ABOVE:
            return turn << (2 * (level - ABOVE) + 2)
        low_bit, high_bit = 1 << c, 1 << (1 - c)
        if level == LOW:
            return low_bit
        if level == HIGH:
            return high_bit
        return low_bit * (turn & 1) + high_bit * (turn >> 1)

    def send(v, level, turn):
        pairs = [(2 * r + c, 2 * (r ^ flip(level, turn, c)) + c) for r in range(row_count) for c in range(2)]
        return lax.ppermute(v, ("rows", "ch"), pairs)

    def small_call(kernel, name, out_shape, *args, scratch=()):
        return pl.pallas_call(
            kernel,
            grid_spec=pltpu.PrefetchScalarGridSpec(
                num_scalar_prefetch=1, grid=(1,), in_specs=[whole_of(v) for v in args],
                out_specs=jax.tree.map(whole_of, out_shape), scratch_shapes=list(scratch),
            ),
            out_shape=out_shape,
            compiler_params=params(name),
            name=name,
        )(digits, *args)

    z_levels = [ABOVE + k for k in range(above)]

    class Sum:
        def __init__(self, mine, other, levels):
            self.own, self.arrived = mine, [other]
            self.down, self.up = list(levels), [HIGH, LOW, *z_levels]

        def part(self):
            level = self.down[0]
            turns = radix(level)
            parts = [v.reshape(turns, -1, LANES) for v in (self.own, *self.arrived)]

            def share(turn):
                picked = [lax.dynamic_index_in_dim(v, digits[level] ^ turn, 0, False) for v in parts]
                return sum(v.astype(F32) for v in picked)

            self.own, *self.sends = [share(turn) for turn in range(turns)]
            self.sends = [v.astype(BF16) for v in self.sends]

        def go(self):
            level = self.down.pop(0)
            self.arrived = [send(v, level, turn + 1) for turn, v in enumerate(self.sends)]

        def finish(self, lines=None):
            self.lines = 0
            if lines is None:
                self.own = (self.own + sum(v.astype(F32) for v in self.arrived)).astype(BF16)
                return
            self.lines = lines.shape[0]
            self.own = pl.pallas_call(
                finish_kernel, out_shape=shape(self.own.shape[0] + 3 * self.lines, LANES, dtype=BF16),
                compiler_params=params("finish"), name="finish",
            )(self.own, *self.arrived, lines, swap(lines))

        def spread(self):
            self.level = self.up.pop()
            self.parts = [self.own] + [send(self.own, self.level, turn) for turn in range(1, radix(self.level))]

        def place(self):
            extra, turns = 3 * self.lines, len(self.parts)
            rows = turns * (self.own.shape[0] - extra) + extra
            self.own = small_call(
                functools.partial(place_kernel, self.level, self.lines), "places", shape(rows, LANES, dtype=BF16),
                *self.parts,
            )

    barrier = lax.optimization_barrier
    sum_two = Sum(mine_two, swap(other_two), [ALL, *z_levels])
    sum_two.part()
    dc1, *sum_two.sends = barrier((dc1, *sum_two.sends))
    sum_two.go()

    dh1, mine_one, other_one = call(
        kernel_six, "back_conv_first",
        [left_of(inner), tile_of(inner), right_of(inner), tile_of(inner), *inner_in, tile_of(inner), tile_of(width)],
        [(inner, BF16), shape(rows_one, LANES, dtype=BF16), shape(rows_one, LANES, dtype=BF16)],
        [tile(2 * part_1, BF16), inner_gains, vm(inner, 2 * part_1, dtype=BF16), vm(2, inner, LANES),
         vm(2 * part_1, inner), vm(width, inner), tile(inner), edge, edge, vm(2, 8, inner)],
        dc1, dc1, dc1, *stay(b1, hat1), scale1, *stay(slope1, a1), swap(dc1_edge), *smalls, *conv_1, sums_h2, sums_c1, sums_c2,
    )
    sum_two.part()
    dh1, mine_one, other_one, *sum_two.sends = barrier((dh1, mine_one, other_one, *sum_two.sends))
    sum_two.go()
    sum_one = Sum(mine_one, swap(other_one), [HIGH, LOW, *z_levels])
    sum_one.part()
    dh1, e2, *sum_one.sends = barrier((dh1, e2, *sum_one.sends))
    sum_one.go()

    y2, moments_three = call(
        kernel_last, "up_second", [tile_of(inner), tile_of(width)],
        [(width, BF16, away), moment_shape], [vm(width, inner, dtype=BF16), tile(width)],
        *stay(e2, y1), *up_2,
    )
    moments_three, *sum_two.arrived = barrier((moments_three, *sum_two.arrived))
    while sum_two.down:
        sum_two.part()
        sum_two.go()
    sum_two.finish()
    sum_one.part()
    dh1, moments_three, sum_two.own, *sum_one.sends = barrier((dh1, moments_three, sum_two.own, *sum_one.sends))
    sum_one.go()
    sum_two.spread()

    early = tiles // 2
    dx, sums_begun = call(
        kernel_seven, "back_outer_early", [tile_of(inner), *wide_in, tile_of(width)],
        [(width, F32, away), shape(2, width, LANES)],
        [outer_gains, vm(width, inner, dtype=BF16), tile(width)],
        dh1, *stay(xhat), xscale, *stay(g1), *first_vectors, *down_1, steps=early,
    )
    sum_two.place()
    sum_one.part()
    dh1, sums_begun, sum_two.own, *sum_one.sends = barrier((dh1, sums_begun, sum_two.own, *sum_one.sends))
    sum_one.go()
    sum_two.spread()

    line_count = up_to(4 * vector_rows + 1, 8)
    later = [tile_of(rows, early) for rows in (inner, width, 1, width)]
    dx, lines = call(
        kernel_eight, "back_outer_late", [*later, anywhere],
        [(width, F32, away), shape(line_count, LANES)],
        [outer_gains, vm(width, inner, dtype=BF16), vm(2, width, LANES), tile(width), vm(2, 8, width)],
        dh1, *stay(xhat), xscale, *stay(g1), dx, *first_vectors, *down_1, sums_begun, moments_one, moments_two,
        moments_three, sums_o2, first=early, steps=tiles - early, aliases={6: 0},
    )
    while sum_one.down:
        sum_one.part()
        if sum_two.up:
            sum_two.place()
        lines, sum_two.own, *sum_one.sends = barrier((lines, sum_two.own, *sum_one.sends))
        sum_one.go()
        if sum_two.up:
            sum_two.spread()
    sum_two.place()
    lines, sum_two.own = barrier((lines, sum_two.own))
    sum_one.finish(lines)
    sum_one.own, sum_two.own = barrier((sum_one.own, sum_two.own))
    sum_two.spread()
    assert not sum_two.up
    while sum_one.up:
        sum_one.spread()
        if sum_one.up:
            sum_one.place()
        if len(sum_one.up) == 2:
            sum_one.own, *sum_two.parts = barrier((sum_one.own, *sum_two.parts))

    wide_shape = shape(half, width)
    conv_grad2, down_grad2, up_grad1, up_grad2 = small_call(
        functools.partial(unpack_kernel, HIGH, 3, 0), "unpack_second",
        [shape(*second_conv.shape), wide_shape, wide_shape, wide_shape],
        *sum_two.parts, scratch=[vm(rows_two, LANES, dtype=BF16)],
    )
    conv_grad1, down_grad1, *rest = small_call(
        functools.partial(unpack_kernel, HIGH, 1, line_count), "unpack_first",
        [shape(*first_conv.shape), wide_shape] + [shape(2, half)] * 4 + [shape(width)] * 4 + [shape(5)],
        *sum_one.parts, scratch=[vm(rows_one, LANES, dtype=BF16)],
    )
    return (
        y1.T, y2.T, dx.T,
        rest[4], rest[5], down_grad1.T, rest[0], rest[1], conv_grad1, up_grad1,
        rest[6], rest[7], down_grad2.T, rest[2], rest[3], conv_grad2, up_grad2,
        rest[8],
    )


def solution(mesh):
    tokens = P(("rows", "ch"), None)
    block = (P(), P(), P(None, "ch"), P(None, "ch"), P(None, "ch"), P(None, None, "ch"), P("ch", None))
    return jax.shard_map(
        local,
        mesh=mesh,
        in_specs=(tokens, tokens, P("rows", None), P("rows"), *block, *block),
        out_specs=(tokens, tokens, tokens, *block, *block, P()),
        check_vma=False,
    )
```
